32 devices in a mesh: ctx: 8 (over z, x), blk: 4 (over y, core).
Axes of the slice: x: 2, y: 2, z: 4, core: 2. Of those that a mesh axis runs over, the one named last changes fastest.
Arguments:
- layer_in: bfloat16 [16, 4096, 256], P('ctx', 'blk'), may hold values from -6 to 6
- matrices: bfloat16 [3072, 256], P(('ctx', 'blk')), may hold values from -2 to 2
- vectors: bfloat16 [2304], P(('ctx', 'blk')), may hold values from -2 to 2
- out_grad: bfloat16 [16, 4096, 256], P('ctx', 'blk'), may hold values from -6 to 6
Outputs:
- layer_out: bfloat16 [16, 4096, 256], P('ctx', 'blk')
- layer_grad: bfloat16 [16, 4096, 256], P('ctx', 'blk')
- matrices_grad: float32 [3072, 256], P(('ctx', 'blk'))
- vectors_grad: float32 [2304], P(('ctx', 'blk'))
The draws below stay inside these ranges and needn't reach their ends.
All inputs are finite; a program needn't handle non-finite values.
Results may differ from the reference program's by a relative error of at most 0.015.
Values may be sent and summed in bfloat16 or wider, within the bound.
A program may use at most 128 MiB of HBM per device.

```python
import math
import jax
import jax.numpy as jnp
from jax import lax

D = 256
HEADS = 4
HEAD_DIM = 64
FF = 1024
CTX_LEN = 4096
CONTEXTS = 16
MAT_ROWS = 3072
VEC_LEN = 2304


def draw_matrices(key, part):
    key = jax.random.fold_in(key, 7)
    places = lax.broadcasted_iota(jnp.int32, (MAT_ROWS, 1), 0)
    factor = jnp.where(places < 2 * D, 1.4, 1.0)
    factor = jnp.where((places >= 3 * D) & (places < 4 * D), 4.0, factor)
    factor = jnp.where(places >= 4 * D + FF, math.sqrt(D / FF), factor)
    factor = factor / math.sqrt(D)
    noise = jnp.clip(jax.random.normal(key, (MAT_ROWS, D), jnp.float32), -4.0, 4.0)
    return (noise * factor).astype(jnp.bfloat16)


def draw_vectors(key, part):
    key = jax.random.fold_in(key, 13)
    places = lax.iota(jnp.int32, VEC_LEN)
    is_gain = (places < D) | (places >= 2 * D) & (places < 3 * D)
    gain_key, offset_key = jax.random.split(key)
    gains = 1.0 + 0.4 * jax.random.uniform(gain_key, (VEC_LEN,), jnp.float32, -1.0, 1.0)
    offsets = 0.5 * jnp.clip(jax.random.normal(offset_key, (VEC_LEN,), jnp.float32), -4.0, 4.0)
    return jnp.where(is_gain, gains, offsets).astype(jnp.bfloat16)


def shard_levels(own_key, dims, cuts, low, high):
    factor_of, own = 1.0, jax.random.fold_in(own_key, 6)
    for position, parts in cuts:
        heights = jnp.exp(jax.random.uniform(jax.random.fold_in(own, position), (parts,), jnp.float32, low / len(cuts), high / len(cuts)))
        factor_of = factor_of * jnp.repeat(heights, dims[position] // parts).reshape([-1 if axis == position else 1 for axis in range(len(dims))])
    return factor_of


def gaussian(key, extent, spread, reach, cuts=(), held_as=jnp.bfloat16):
    array = spread * jax.random.normal(key, extent, jnp.float32)
    if cuts:
        array = array * shard_levels(key, extent, cuts, -0.22, 0.18)
    return jnp.clip(array, -reach, reach).astype(held_as)


def setup_inputs(seed: int = 0) -> dict:
    splits = jax.random.split(jax.random.key(seed), 5)
    layer_in = gaussian(splits[0], (CONTEXTS, CTX_LEN, D), 1.0, 6.0, ((0, 8), (1, 4)))
    matrices = draw_matrices(jax.random.fold_in(splits[4], 71), 0)
    vectors = draw_vectors(jax.random.fold_in(splits[4], 71), 0)
    out_grad = gaussian(splits[3], (CONTEXTS, CTX_LEN, D), 1.0, 6.0, ((0, 8), (1, 4)))
    return {"layer_in": layer_in, "matrices": matrices, "vectors": vectors, "out_grad": out_grad}


@jax.custom_vjp
def low(v):
    return lax.optimization_barrier(v.astype(jnp.bfloat16)).astype(jnp.float32)

@jax.custom_vjp
def low_back(v):
    return v

def low_keep(v):
    return (low(v), None)

def low_pass(kept, grad):
    return (grad,)

def back_keep(v):
    return (v, None)

def back_low(kept, grad):
    return (low(grad),)
low.defvjp(low_keep, low_pass)
low_back.defvjp(back_keep, back_low)
EPSILON = 1e-05

def layer_norm(inputs, gain, offset):
    centre = lax.optimization_barrier(jnp.mean(inputs, -1, keepdims=True))
    shifted = inputs - centre
    variance = lax.optimization_barrier(jnp.mean(shifted * shifted, -1, keepdims=True))
    return shifted * lax.rsqrt(variance + EPSILON) * gain + offset

def attend(triple):
    queries, key_rows, value_rows = triple
    length = queries.shape[0]
    block_width = math.gcd(length, 512)
    inv_root = 1.0 / math.sqrt(HEAD_DIM)
    head_keys = key_rows.reshape(length, HEADS, -1)
    head_values = value_rows.reshape(length, HEADS, -1)

    def one_block(block):
        head_queries = block.reshape(block_width, HEADS, -1)
        scores = low_back(jnp.einsum('qhd,khd->hqk', head_queries, head_keys, precision=lax.Precision.HIGHEST) * inv_root)
        highest = lax.optimization_barrier(jnp.max(scores, -1, keepdims=True))
        expo = jnp.exp(scores - highest)
        totals = lax.optimization_barrier(jnp.sum(expo, -1))
        mixed = jnp.einsum('hqk,khd->qhd', low(expo), head_values, precision=lax.Precision.HIGHEST) / totals.T[..., None]
        return mixed.reshape(block_width, -1)
    blocks = queries.reshape(length // block_width, block_width, -1)
    return lax.map(jax.checkpoint(one_block), blocks).reshape(length, -1)

def layer(inputs, matrices, vectors):
    contexts, length, width = inputs.shape
    hidden_width = vectors.shape[0] - 5 * width
    highest = lax.Precision.HIGHEST
    gain_in = vectors[:width]
    bias_in = vectors[width:2 * width]
    gain_mid = vectors[2 * width:3 * width]
    bias_mid = vectors[3 * width:4 * width]
    up_bias = vectors[4 * width:4 * width + hidden_width]
    down_bias = vectors[4 * width + hidden_width:]
    out_proj = matrices[3 * width:4 * width]
    up_rows = matrices[4 * width:4 * width + hidden_width]
    down_rows = matrices[4 * width + hidden_width:]
    rows_all = inputs.reshape(contexts * length, width)
    ln_in = low(layer_norm(rows_all, gain_in, bias_in))
    projected = []
    for index in range(3):
        weight = matrices[index * width:(index + 1) * width]
        made = low_back(low(jnp.dot(ln_in, weight, precision=highest)))
        projected.append(made.reshape(contexts, length, width))
    attended = lax.map(jax.checkpoint(attend), tuple(projected)).reshape(contexts * length, width)
    attended = low_back(low(attended))
    branch = low_back(jnp.dot(attended, out_proj, precision=highest))
    middle = rows_all + branch
    ln_mid = low(layer_norm(middle, gain_mid, bias_mid))
    upper = low_back(jnp.dot(ln_mid, up_rows.T, precision=highest) + up_bias)
    hidden = low(jax.nn.gelu(upper, approximate=False))
    result = middle + jnp.dot(hidden, down_rows, precision=highest) + down_bias
    return result.reshape(contexts, length, width)

def reference(layer_in, matrices, vectors, out_grad):
    result, pullback = jax.vjp(layer, layer_in.astype(jnp.float32), matrices.astype(jnp.float32), vectors.astype(jnp.float32))
    grad_in, grad_mats, grad_vecs = pullback(out_grad.astype(jnp.float32))
    return (result.astype(jnp.bfloat16), grad_in.astype(jnp.bfloat16), grad_mats, grad_vecs)
```

```python
import functools
import math

import jax
import jax.numpy as jnp
from jax import lax
from jax.experimental import pallas as pl
from jax.experimental.pallas import tpu as pltpu
from jax.sharding import PartitionSpec as P

HEADS = 4
EPSILON = 1e-05
LOG2E = math.log2(math.e)
LN2 = math.log(2.0)
AUG = 80
SAFE_BOUND = 90.0
BF = jnp.bfloat16
F32 = jnp.float32
NT = (((1,), (1,)), ((), ()))
TN = (((0,), (0,)), ((), ()))


def dot(a, b):
    return jnp.dot(a, b, preferred_element_type=F32)


def dot_nt(a, b):
    return lax.dot_general(a, b, NT, preferred_element_type=F32)


def dot_tn(a, b):
    return lax.dot_general(a, b, TN, preferred_element_type=F32)


def params(**kw):
    return pltpu.CompilerParams(vmem_limit_bytes=60 << 20, **kw)


def whole(*shape):
    return pl.BlockSpec(shape, lambda *_: (0,) * len(shape))


def normalize(inputs):
    centre = jnp.mean(inputs, -1, keepdims=True)
    shifted = inputs - centre
    inverse = lax.rsqrt(jnp.mean(shifted * shifted, -1, keepdims=True) + EPSILON)
    return shifted * inverse, inverse


def normalize_back(grad_hat, normed, inverse):
    return inverse * (
        grad_hat
        - jnp.mean(grad_hat, -1, keepdims=True)
        - normed * jnp.mean(grad_hat * normed, -1, keepdims=True)
    )


def prep_kernel(own_steps, x_ref, w_ref, vec_ref, ln_ref, qt_ref, kn_ref, kta_ref, vta_ref, wt, wkp):
    width = x_ref.shape[1]
    head = width // HEADS
    step = pl.program_id(0)

    @pl.when(step == 0)
    def _():
        for index in range(3):
            piece = w_ref[index * width : (index + 1) * width, :].astype(F32)
            wt[index * width : (index + 1) * width, :] = piece.T.astype(BF)
        wk = w_ref[width : 2 * width, :].astype(F32)
        for h in range(HEADS):
            wide = jnp.concatenate([wk[:, h * head : (h + 1) * head], jnp.zeros((width, 128 - head), F32)], 1)
            wkp[:, h * 128 : (h + 1) * 128] = wide.astype(BF)

    normed, _ = normalize(x_ref[...].astype(F32))
    ln = (normed * vec_ref[0:1, :] + vec_ref[1:2, :]).astype(BF)
    ln_ref[...] = ln
    rows = ln.shape[0]
    extra = (lax.broadcasted_iota(jnp.int32, (AUG - head, rows), 0) < 3).astype(F32).astype(BF)

    kt = dot_nt(wt[width : 2 * width, :], ln).astype(BF)
    vt = dot_nt(wt[2 * width : 3 * width, :], ln).astype(BF)
    kn = dot(ln, wkp[...]).astype(BF)
    for h in range(HEADS):
        kta_ref[h, :head, :] = kt[h * head : (h + 1) * head, :]
        kta_ref[h, head:, :] = extra
        vta_ref[h, :head, :] = vt[h * head : (h + 1) * head, :]
        vta_ref[h, head:, :] = extra
        kn_ref[h] = kn[:, h * 128 : (h + 1) * 128]

    @pl.when(step < own_steps)
    def _():
        qt = dot_nt(wt[0:width, :], ln) * (LOG2E / math.sqrt(head))
        for h in range(HEADS):
            qt_ref[h] = qt[h * head : (h + 1) * head, :].astype(BF)


def prep(rows_all, own, w_input, vec):
    total, width = rows_all.shape
    head = width // HEADS
    block = min(512, own)
    steps, own_steps = total // block, own // block
    last = own_steps - 1
    return pl.pallas_call(
        functools.partial(prep_kernel, own_steps),
        grid=(steps,),
        in_specs=[
            pl.BlockSpec((block, width), lambda i: (i, 0)),
            whole(3 * width, width),
            whole(*vec.shape),
        ],
        out_specs=[
            pl.BlockSpec((block, width), lambda i: (i, 0)),
            pl.BlockSpec((HEADS, head, block), lambda i: (0, 0, jnp.minimum(i, last))),
            pl.BlockSpec((HEADS, block, 128), lambda i: (0, i, 0)),
            pl.BlockSpec((HEADS, AUG, block), lambda i: (0, 0, i)),
            pl.BlockSpec((HEADS, AUG, block), lambda i: (0, 0, i)),
        ],
        out_shape=[
            jax.ShapeDtypeStruct((total, width), BF),
            jax.ShapeDtypeStruct((HEADS, head, own), BF),
            jax.ShapeDtypeStruct((HEADS, total, 128), BF),
            jax.ShapeDtypeStruct((HEADS, AUG, total), BF),
            jax.ShapeDtypeStruct((HEADS, AUG, total), BF),
        ],
        scratch_shapes=[pltpu.VMEM((3 * width, width), BF), pltpu.VMEM((width, HEADS * 128), BF)],
        compiler_params=params(),
        name="project",
    )(rows_all, w_input, vec)


def attend_kernel(qt_ref, kn_ref, kta_ref, vta_ref, att_ref, lse_ref):
    head, own = qt_ref.shape[1:]
    total = kn_ref.shape[1]
    tq = min(1024, own)
    tk = min(256, total)
    count = total // tk

    def longest(rows):
        rows = rows.astype(F32)
        return jnp.max(jnp.sum(rows * rows, 0, keepdims=True))

    bound = longest(qt_ref[0]) * longest(kta_ref[0, :head, :])

    def finish(where, summed, top):
        totals = summed[head : head + 1, :]
        att_ref[0, :, where] = summed[:head, :] / totals
        level = jnp.log2(totals)
        lse_ref[0, :, where] = jnp.broadcast_to(level if top is None else level + top, (8, tq))

    def scores(queries, j):
        return dot(kn_ref[0, j * tk : (j + 1) * tk, :head], queries)

    @pl.when(bound <= SAFE_BOUND * SAFE_BOUND)
    def _():
        @pl.loop(0, own // tq)
        def _(i):
            where = pl.ds(pl.multiple_of(i * tq, tq), tq)
            queries = qt_ref[0, :, where]
            summed = jnp.zeros((AUG, tq), F32)
            now = scores(queries, 0)
            for j in range(count):
                expo = jnp.exp2(now).astype(BF)
                if j + 1 < count:
                    now = scores(queries, j + 1)
                summed = summed + dot(vta_ref[0, :, j * tk : (j + 1) * tk], expo)
            finish(where, summed, None)

    @pl.when(jnp.logical_not(bound <= SAFE_BOUND * SAFE_BOUND))
    def _():
        @pl.loop(0, own // tq)
        def _(i):
            where = pl.ds(pl.multiple_of(i * tq, tq), tq)
            queries = qt_ref[0, :, where]

            def absorb(j, carry):
                summed, top = carry
                part = pl.ds(pl.multiple_of(j * tk, tk), tk)
                now = dot(kn_ref[0, part, :head], queries)
                higher = jnp.maximum(top, jnp.max(now, 0, keepdims=True))
                expo = jnp.exp2(now - higher).astype(BF)
                summed = summed * jnp.exp2(top - higher) + dot(vta_ref[0, :, part], expo)
                return summed, higher

            start = (jnp.zeros((AUG, tq), F32), jnp.full((1, tq), -1e30, F32))
            summed, top = lax.fori_loop(0, count, absorb, start)
            finish(where, summed, top)


def attend(qt, kn, kta, vta):
    _, head, own = qt.shape
    total = kn.shape[1]
    per_head = lambda *shape: pl.BlockSpec((1, *shape), lambda h: (h, 0, 0))
    return pl.pallas_call(
        attend_kernel,
        grid=(HEADS,),
        in_specs=[per_head(head, own), per_head(total, 128), per_head(AUG, total), per_head(AUG, total)],
        out_specs=[per_head(head, own), per_head(8, own)],
        out_shape=[
            jax.ShapeDtypeStruct((HEADS, head, own), F32),
            jax.ShapeDtypeStruct((HEADS, 8, own), F32),
        ],
        compiler_params=params(),
        name="attend",
    )(qt, kn, kta, vta)


def gelu_both(value):
    square = value * value
    density = jnp.exp(-0.5 * square)
    place = pl.reciprocal(1.0 + (0.3275911 / math.sqrt(2.0)) * jnp.abs(value), approx=True)
    series = 1.061405429 * place - 1.453152027
    series = series * place + 1.421413741
    series = series * place - 0.284496736
    series = series * place + 0.254829592
    tail = 0.5 * series * place * density
    below = jnp.where(value >= 0.0, 1.0 - tail, tail)
    return value * below, below + value * density * (1.0 / math.sqrt(2.0 * math.pi))


def split_rows(level, count):
    high = level.astype(BF).astype(F32)
    middle = (level - high).astype(BF).astype(F32)
    low = level - high - middle
    place = lax.broadcasted_iota(jnp.int32, (count, level.shape[1]), 0)
    rows = jnp.where(place == 0, high, jnp.where(place == 1, middle, jnp.where(place == 2, low, 0.0)))
    return rows


def middle_kernel(
    x_ref, g_ref, att_ref, lse_ref, qt_ref, w_ref, vec_ref,
    out_ref, gmid_ref, qa_ref, doa_ref, dot_ref, gwo_ref, gup_ref, gdown_ref, gvec_ref,
):
    width = x_ref.shape[1]
    head = width // HEADS
    rows = x_ref.shape[0]
    hidden_width = (w_ref.shape[0] - width) // 2
    wo = w_ref[:width, :]
    up = w_ref[width : width + hidden_width, :]
    down = w_ref[width + hidden_width :, :]
    pieces = hidden_width // width
    up_bias = jnp.concatenate([vec_ref[4 + p : 5 + p, :] for p in range(pieces)], 1)
    down_bias = vec_ref[4 + pieces : 5 + pieces, :]
    gain, bias = vec_ref[2:3, :], vec_ref[3:4, :]

    @pl.when(pl.program_id(0) == 0)
    def _():
        gwo_ref[...] = jnp.zeros_like(gwo_ref)
        gup_ref[...] = jnp.zeros_like(gup_ref)
        gdown_ref[...] = jnp.zeros_like(gdown_ref)
        gvec_ref[...] = jnp.zeros_like(gvec_ref)

    att = att_ref[...].reshape(width, rows)
    att_low = att.astype(BF)
    grad = g_ref[...]
    gradf = grad.astype(F32)
    middle = x_ref[...].astype(F32) + dot_tn(att_low, wo)
    normed, inverse = normalize(middle)
    ln_mid = (normed * gain + bias).astype(BF)
    upper = dot_nt(ln_mid, up) + up_bias
    grad_hidden = dot_nt(grad, down)
    activated, slope = gelu_both(upper)
    hidden = activated.astype(BF)
    grad_upper = (grad_hidden * slope).astype(BF)
    out_ref[...] = (middle + dot(hidden, down) + down_bias).astype(BF)
    gdown_ref[...] += dot_tn(grad, hidden)
    gup_ref[...] += dot_tn(ln_mid, grad_upper)
    grad_ln = dot(grad_upper, up)
    total_up = jnp.sum(grad_upper.astype(F32), 0, keepdims=True)
    gvec_ref[2:3, :] += jnp.sum(grad_ln * normed, 0, keepdims=True)
    gvec_ref[3:4, :] += jnp.sum(grad_ln, 0, keepdims=True)
    for p in range(pieces):
        gvec_ref[4 + p : 5 + p, :] += total_up[:, p * width : (p + 1) * width]
    gvec_ref[4 + pieces : 5 + pieces, :] += jnp.sum(gradf, 0, keepdims=True)
    grad_mid = gradf + normalize_back(grad_ln * gain, normed, inverse)
    gmid_ref[...] = grad_mid
    branch = grad_mid.astype(BF)
    gwo_ref[...] += dot(att_low, branch)
    grad_att = dot_nt(wo, branch).astype(BF)
    spare = jnp.zeros((128 - AUG, rows), F32)
    for h in range(HEADS):
        mine = slice(h * head, (h + 1) * head)
        grad_head = grad_att[mine, :]
        dot_ref[h] = grad_head
        delta = jnp.sum(grad_head.astype(F32) * att[mine, :], 0, keepdims=True)
        wide = jnp.concatenate([grad_head.astype(F32), split_rows(-delta, AUG - head), spare], 0)
        doa_ref[h] = wide.T.astype(BF)
        level = lse_ref[h, 0:1, :]
        wide = jnp.concatenate([qt_ref[h].astype(F32), split_rows(-level, AUG - head), spare], 0)
        qa_ref[h] = wide.T.astype(BF)


def between(x, grad, att, lse, qt, weights, vec):
    own, width = x.shape
    head = width // HEADS
    hidden_width = (weights.shape[0] - width) // 2
    block = min(512, own)
    rows = lambda i: (i, 0)
    lanes = lambda i: (0, 0, i)
    tall = lambda i: (0, i, 0)
    return pl.pallas_call(
        middle_kernel,
        grid=(own // block,),
        in_specs=[
            pl.BlockSpec((block, width), rows),
            pl.BlockSpec((block, width), rows),
            pl.BlockSpec((HEADS, head, block), lanes),
            pl.BlockSpec((HEADS, 8, block), lanes),
            pl.BlockSpec((HEADS, head, block), lanes),
            whole(*weights.shape),
            whole(*vec.shape),
        ],
        out_specs=[
            pl.BlockSpec((block, width), rows),
            pl.BlockSpec((block, width), rows),
            pl.BlockSpec((HEADS, block, 128), tall),
            pl.BlockSpec((HEADS, block, 128), tall),
            pl.BlockSpec((HEADS, head, block), lanes),
            whole(width, width),
            whole(width, hidden_width),
            whole(width, hidden_width),
            whole(16, width),
        ],
        out_shape=[
            jax.ShapeDtypeStruct((own, width), BF),
            jax.ShapeDtypeStruct((own, width), F32),
            jax.ShapeDtypeStruct((HEADS, own, 128), BF),
            jax.ShapeDtypeStruct((HEADS, own, 128), BF),
            jax.ShapeDtypeStruct((HEADS, head, own), BF),
            jax.ShapeDtypeStruct((width, width), F32),
            jax.ShapeDtypeStruct((width, hidden_width), F32),
            jax.ShapeDtypeStruct((width, hidden_width), F32),
            jax.ShapeDtypeStruct((16, width), F32),
        ],
        compiler_params=params(),
        name="between",
    )(x, grad, att, lse, qt, weights, vec)


def attend_back_kernel(qa_ref, doa_ref, qt_ref, dot_ref, kta_ref, vta_ref, kn_ref, dq_ref, dk_ref, dv_ref, dk_sum, dv_sum):
    head, own = qt_ref.shape[1:]
    total = kn_ref.shape[1]
    tq = min(1024, own)
    tk = min(512, total)
    count = total // tk
    dk_sum[...] = jnp.zeros_like(dk_sum)
    dv_sum[...] = jnp.zeros_like(dv_sum)

    @pl.loop(0, own // tq)
    def _(i):
        where = pl.ds(pl.multiple_of(i * tq, tq), tq)
        queries, grads = qa_ref[0, where, :AUG], doa_ref[0, where, :AUG]
        queries_t, grads_t = qt_ref[0, :, where], dot_ref[0, :, where]

        def pair(j):
            part = slice(j * tk, (j + 1) * tk)
            return dot(queries, kta_ref[0, :, part]), dot(grads, vta_ref[0, :, part])

        grad_query = jnp.zeros((tq, 128), F32)
        level, change = pair(0)
        for j in range(count):
            part = slice(j * tk, (j + 1) * tk)
            probs = jnp.exp2(level)
            probs_low = probs.astype(BF)
            grad_scores = (probs * change).astype(BF)
            if j + 1 < count:
                level, change = pair(j + 1)
            dv_sum[:, part] += dot(grads_t, probs_low)
            dk_sum[:, part] += dot(queries_t, grad_scores)
            grad_query = grad_query + dot(grad_scores, kn_ref[0, part, :])
        dq_ref[0, where, :] = (grad_query * (1.0 / math.sqrt(head))).astype(BF)

    dk_ref[0] = (dk_sum[...] * LN2).astype(BF)
    dv_ref[0] = dv_sum[...].astype(BF)


def attend_back(qa, doa, qt, dot_t, kta, vta, kn):
    _, head, own = qt.shape
    total = kn.shape[1]
    per_head = lambda *shape: pl.BlockSpec((1, *shape), lambda h: (h, 0, 0))
    return pl.pallas_call(
        attend_back_kernel,
        grid=(HEADS,),
        in_specs=[
            per_head(own, 128), per_head(own, 128), per_head(head, own), per_head(head, own),
            per_head(AUG, total), per_head(AUG, total), per_head(total, 128),
        ],
        out_specs=[per_head(own, 128), per_head(head, total), per_head(head, total)],
        out_shape=[
            jax.ShapeDtypeStruct((HEADS, own, 128), BF),
            jax.ShapeDtypeStruct((HEADS, head, total), BF),
            jax.ShapeDtypeStruct((HEADS, head, total), BF),
        ],
        scratch_shapes=[pltpu.VMEM((head, total), F32), pltpu.VMEM((head, total), F32)],
        compiler_params=params(),
        name="attend_back",
    )(qa, doa, qt, dot_t, kta, vta, kn)


def unproject_kernel(own_steps, dq_ref, dk_ref, dv_ref, ln_ref, w_ref, gw_ref, part_ref, gq, gk, gv):
    width = ln_ref.shape[1]
    head = width // HEADS
    rows = ln_ref.shape[0]
    step = pl.program_id(0)

    @pl.when(step == 0)
    def _():
        gq[...] = jnp.zeros_like(gq)
        gk[...] = jnp.zeros_like(gk)
        gv[...] = jnp.zeros_like(gv)

    ln = ln_ref[...]
    dk = dk_ref[...].reshape(width, rows)
    dv = dv_ref[...].reshape(width, rows)
    gk[...] += dot(dk, ln)
    gv[...] += dot(dv, ln)
    part_ref[...] = (dot(w_ref[width : 2 * width, :], dk) + dot(w_ref[2 * width : 3 * width, :], dv)).astype(BF)

    @pl.when(step < own_steps)
    def _():
        dq = jnp.concatenate([dq_ref[h] for h in range(HEADS)], 1)
        gq[...] += dot_tn(ln, dq)

    @pl.when(step == pl.num_programs(0) - 1)
    def _():
        for h in range(HEADS):
            gw_ref[:width, h * head : (h + 1) * head] = gq[:, h * 128 : h * 128 + head]
        gw_ref[width : 2 * width, :] = gk[...].T
        gw_ref[2 * width :, :] = gv[...].T


def unproject(dq, dk, dv, ln, w_input):
    total, width = ln.shape
    _, own, _ = dq.shape
    head = width // HEADS
    block = min(512, own)
    own_steps = own // block
    last = own_steps - 1
    return pl.pallas_call(
        functools.partial(unproject_kernel, own_steps),
        grid=(total // block,),
        in_specs=[
            pl.BlockSpec((HEADS, block, 128), lambda i: (0, jnp.minimum(i, last), 0)),
            pl.BlockSpec((HEADS, head, block), lambda i: (0, 0, i)),
            pl.BlockSpec((HEADS, head, block), lambda i: (0, 0, i)),
            pl.BlockSpec((block, width), lambda i: (i, 0)),
            whole(3 * width, width),
        ],
        out_specs=[whole(3 * width, width), pl.BlockSpec((width, block), lambda i: (0, i))],
        out_shape=[
            jax.ShapeDtypeStruct((3 * width, width), F32),
            jax.ShapeDtypeStruct((width, total), BF),
        ],
        scratch_shapes=[
            pltpu.VMEM((width, HEADS * 128), F32), pltpu.VMEM((width, width), F32), pltpu.VMEM((width, width), F32),
        ],
        compiler_params=params(),
        name="unproject",
    )(dq, dk, dv, ln, w_input)


def finish_kernel(x_ref, gmid_ref, dq_ref, part_ref, other_ref, w_ref, vec_ref, out_ref, gvec_ref, wqt):
    width = x_ref.shape[1]
    head = width // HEADS

    @pl.when(pl.program_id(0) == 0)
    def _():
        gvec_ref[...] = jnp.zeros_like(gvec_ref)
        turned = w_ref[...].astype(F32).T
        for h in range(HEADS):
            wqt[h * 128 : h * 128 + head, :] = turned[h * head : (h + 1) * head, :].astype(BF)
            wqt[h * 128 + head : (h + 1) * 128, :] = jnp.zeros((128 - head, width), BF)

    dq = jnp.concatenate([dq_ref[h] for h in range(HEADS)], 1)
    from_rows = part_ref[...].astype(F32) + other_ref[...].astype(F32)
    grad_ln = dot(dq, wqt[...]) + from_rows.T
    normed, inverse = normalize(x_ref[...].astype(F32))
    gvec_ref[0:1, :] += jnp.sum(grad_ln * normed, 0, keepdims=True)
    gvec_ref[1:2, :] += jnp.sum(grad_ln, 0, keepdims=True)
    out_ref[...] = (gmid_ref[...] + normalize_back(grad_ln * vec_ref[0:1, :], normed, inverse)).astype(BF)


def finish(x, gmid, dq, part, other, w_query, vec):
    own, width = x.shape
    block = min(512, own)
    rows = lambda i: (i, 0)
    lanes = lambda i: (0, i)
    return pl.pallas_call(
        finish_kernel,
        grid=(own // block,),
        in_specs=[
            pl.BlockSpec((block, width), rows),
            pl.BlockSpec((block, width), rows),
            pl.BlockSpec((HEADS, block, 128), lambda i: (0, i, 0)),
            pl.BlockSpec((width, block), lanes),
            pl.BlockSpec((width, block), lanes),
            whole(width, width),
            whole(*vec.shape),
        ],
        out_specs=[pl.BlockSpec((block, width), rows), whole(8, width)],
        out_shape=[jax.ShapeDtypeStruct((own, width), BF), jax.ShapeDtypeStruct((8, width), F32)],
        scratch_shapes=[pltpu.VMEM((HEADS * 128, width), BF)],
        compiler_params=params(),
        name="finish",
    )(x, gmid, dq, part, other, w_query, vec)


def per_device(blk_size, layer_in, matrices, vectors, out_grad):
    seq_count, local_rows, width = layer_in.shape
    group = blk_size // seq_count
    blk = lax.axis_index("blk")
    mine = blk // group
    far = [(b, (b + group) % blk_size) for b in range(blk_size)]
    near = [(b, b ^ 1) for b in range(blk_size)]

    def swap(pair):
        kept = lax.dynamic_index_in_dim(pair, mine, 0, keepdims=False)
        sent = lax.dynamic_index_in_dim(pair, 1 - mine, 0, keepdims=False)
        return jnp.concatenate([kept, lax.ppermute(sent, "blk", far)], 0)

    def unswap(rows):
        kept, sent = rows[:local_rows], rows[local_rows:]
        got = lax.ppermute(sent, "blk", far)
        return jnp.where(mine == 0, jnp.stack([kept, got]), jnp.stack([got, kept]))

    x = swap(layer_in)
    grad = swap(out_grad)
    rows_all = jnp.concatenate([x, lax.ppermute(x, "blk", near)], 0)
    mats = lax.all_gather(matrices, ("ctx", "blk"), axis=0, tiled=True)
    vec = lax.all_gather(vectors, ("ctx", "blk"), axis=0, tiled=True).astype(F32).reshape(-1, width)
    vec = jnp.pad(vec, ((0, 16 - vec.shape[0]), (0, 0)))
    own = x.shape[0]
    ln, qt, kn, kta, vta = prep(rows_all, own, mats[: 3 * width], vec)
    att, lse = attend(qt, kn, kta, vta)
    out, gmid, qa, doa, dot_t, gwo, gup, gdown, gvec = between(x, grad, att, lse, qt, mats[3 * width :], vec)
    layer_out = unswap(out)
    dq, dk, dv = attend_back(qa, doa, qt, dot_t, kta, vta, kn)
    gw, part = unproject(dq, dk, dv, ln, mats[: 3 * width])
    other = lax.ppermute(part[:, own:], "blk", near)
    grad_rows, gvec_in = finish(x, gmid, dq, part[:, :own], other, mats[:width], vec)
    layer_grad = unswap(grad_rows)
    grad_mats = jnp.concatenate([gw, gwo, gup.T, gdown.T], 0)
    grad_vecs = jnp.concatenate([gvec_in[:2], gvec[2:9]], 0).reshape(-1)
    matrices_grad = lax.psum_scatter(grad_mats, ("ctx", "blk"), scatter_dimension=0, tiled=True)
    vectors_grad = lax.psum_scatter(grad_vecs, ("ctx", "blk"), scatter_dimension=0, tiled=True)
    return layer_out, layer_grad, matrices_grad, vectors_grad


def solution(mesh):
    rows = P("ctx", "blk", None)
    flat = P(("ctx", "blk"))
    return jax.shard_map(
        functools.partial(per_device, mesh.shape["blk"]),
        mesh=mesh,
        in_specs=(rows, flat, flat, rows),
        out_specs=(rows, rows, flat, flat),
        check_vma=False,
    )
```

```python
import functools
import math

import jax
import jax.numpy as jnp
from jax import lax
from jax.experimental import pallas as pl
from jax.experimental.pallas import tpu as pltpu
from jax.sharding import PartitionSpec as P

HEADS = 4
EPSILON = 1e-05
LOG2E = math.log2(math.e)
LN2 = math.log(2.0)
AUG = 80
SAFE_BOUND = 90.0
BF = jnp.bfloat16
F32 = jnp.float32
NT = (((1,), (1,)), ((), ()))
TN = (((0,), (0,)), ((), ()))


def dot(a, b):
    return jnp.dot(a, b, preferred_element_type=F32)


def dot_nt(a, b):
    return lax.dot_general(a, b, NT, preferred_element_type=F32)


def dot_tn(a, b):
    return lax.dot_general(a, b, TN, preferred_element_type=F32)


def params(**kw):
    return pltpu.CompilerParams(vmem_limit_bytes=60 << 20, **kw)


def whole(*shape):
    return pl.BlockSpec(shape, lambda *_: (0,) * len(shape))


def normalize(inputs):
    centre = jnp.mean(inputs, -1, keepdims=True)
    shifted = inputs - centre
    inverse = lax.rsqrt(jnp.mean(shifted * shifted, -1, keepdims=True) + EPSILON)
    return shifted * inverse, inverse


def normalize_back(grad_hat, normed, inverse):
    return inverse * (
        grad_hat
        - jnp.mean(grad_hat, -1, keepdims=True)
        - normed * jnp.mean(grad_hat * normed, -1, keepdims=True)
    )


MESH = pl.DeviceIdType.MESH


def send(source, target, sent, received, device):
    copy = pltpu.make_async_remote_copy(
        src_ref=source, dst_ref=target, send_sem=sent, recv_sem=received, device_id=device, device_id_type=MESH
    )
    copy.start()
    return copy


def greet(devices):
    barrier = pltpu.get_barrier_semaphore()
    for device in devices:
        pl.semaphore_signal(barrier, inc=1, device_id=device, device_id_type=MESH)
    pl.semaphore_wait(barrier, len(devices))


def partners(blk_size):
    ctx, blk = lax.axis_index("ctx"), lax.axis_index("blk")
    half = blk_size // 2
    return ctx, blk, blk + 1 - 2 * lax.rem(blk, 2), lax.rem(blk + half, blk_size), lax.div(blk, half)


def exchange_kernel(
    ctx_size, blk_size, x_ref, w_ref, rows_ref, all_ref,
    far_sent, far_got, near_sent, near_got, relay_sent, relay_got, own_sem,
    first_sent, first_got, second_sent, second_got, third_sent, third_got, keep_sem,
):
    ctx, blk, near, far, mine = partners(blk_size)
    length = x_ref.shape[1]
    owners = all_ref.shape[0] // blk_size
    chunks = far_sent.shape[0]
    size = length // chunks
    others = [lax.rem(ctx + step, ctx_size) for step in range(1, ctx_size)]
    greet([(ctx, near), (ctx, far)] + [(other, blk) for other in others])

    @pl.when(ctx < owners)
    def _():
        keep = pltpu.make_async_copy(w_ref, all_ref.at[ctx * blk_size + blk], keep_sem)
        keep.start()
        for step, other in enumerate(others):
            send(w_ref, all_ref.at[ctx * blk_size + blk], first_sent.at[step], first_got.at[ctx], (other, blk))

    far_copies = []
    for c in range(chunks):
        part = pl.ds(c * size, size)
        far_copies.append(
            send(x_ref.at[1 - mine, part], rows_ref.at[pl.ds(length + c * size, size)], far_sent.at[c], far_got.at[c], (ctx, far))
        )
    near_copy = send(x_ref.at[mine], rows_ref.at[pl.ds(2 * length, length)], near_sent, near_got, (ctx, near))
    own_copy = pltpu.make_async_copy(x_ref.at[mine], rows_ref.at[pl.ds(0, length)], own_sem)
    own_copy.start()

    @pl.when(ctx < owners)
    def _():
        pltpu.make_async_copy(w_ref, all_ref.at[ctx * blk_size + blk], keep_sem).wait()

    def copy_of(slot, sent, got, device):
        return pltpu.make_async_remote_copy(
            src_ref=all_ref.at[slot], dst_ref=all_ref.at[slot], send_sem=sent, recv_sem=got,
            device_id=device, device_id_type=MESH,
        )

    for o in range(owners):
        @pl.when(ctx != o)
        def _():
            copy_of(o * blk_size + blk, first_sent.at[0], first_got.at[o], (ctx, near)).wait_recv()

        copy_of(o * blk_size + blk, second_sent.at[o], second_got.at[o], (ctx, far)).start()
        copy_of(o * blk_size + blk, third_sent.at[o], third_got.at[o], (ctx, near)).start()
    relays = []
    for c in range(chunks):
        far_copies[c].wait_recv()
        here = rows_ref.at[pl.ds(length + c * size, size)]
        there = rows_ref.at[pl.ds(3 * length + c * size, size)]
        relays.append(send(here, there, relay_sent.at[c], relay_got.at[c], (ctx, near)))
    for o in range(owners):
        copy_of(o * blk_size + far, second_sent.at[o], second_got.at[o], (ctx, far)).wait_recv()
        copy_of(o * blk_size + far, third_sent.at[owners + o], third_got.at[owners + o], (ctx, near)).start()

    for o in range(owners):
        copy_of(o * blk_size + blk, second_sent.at[o], second_got.at[o], (ctx, far)).wait_send()
        for turn in range(2):
            copy_of(o * blk_size + blk, third_sent.at[turn * owners + o], third_got.at[turn * owners + o], (ctx, near)).wait()
    for c in range(chunks):
        far_copies[c].wait_send()
        relays[c].wait()
    near_copy.wait()
    own_copy.wait()

    @pl.when(ctx < owners)
    def _():
        for step, other in enumerate(others):
            pltpu.make_async_remote_copy(
                src_ref=w_ref, dst_ref=all_ref.at[ctx * blk_size + blk], send_sem=first_sent.at[step],
                recv_sem=first_got.at[ctx], device_id=(other, blk), device_id_type=MESH,
            ).wait_send()


def exchange(ctx_size, blk_size, layer_in, block, owners):
    seq_count, length, width = layer_in.shape
    chunks = 4 if length % 64 == 0 else 1
    dma = pltpu.SemaphoreType.DMA
    place = pl.BlockSpec(memory_space=pl.ANY)
    return pl.pallas_call(
        functools.partial(exchange_kernel, ctx_size, blk_size),
        in_specs=[place] * 2,
        out_specs=[place] * 2,
        out_shape=[
            jax.ShapeDtypeStruct((4 * length, width), BF),
            jax.ShapeDtypeStruct((owners * blk_size, *block.shape), BF),
        ],
        scratch_shapes=[
            dma((chunks,)), dma((chunks,)), dma, dma, dma((chunks,)), dma((chunks,)), dma,
            dma((ctx_size - 1,)) if ctx_size > 1 else dma((1,)), dma((owners,)), dma((owners,)), dma((owners,)),
            dma((2 * owners,)), dma((2 * owners,)), dma,
        ],
        compiler_params=params(collective_id=1, has_side_effects=True),
        name="exchange",
    )(layer_in, block)


def prep_kernel(own_steps, x_ref, w_ref, vec_ref, ln_ref, qt_ref, kn_ref, kta_ref, vta_ref, wt, wkp):
    width = x_ref.shape[1]
    head = width // HEADS
    step = pl.program_id(0)

    @pl.when(step == 0)
    def _():
        for index in range(3):
            piece = w_ref[index * width : (index + 1) * width, :].astype(F32)
            wt[index * width : (index + 1) * width, :] = piece.T.astype(BF)
        wk = w_ref[width : 2 * width, :].astype(F32)
        for h in range(HEADS):
            wide = jnp.concatenate([wk[:, h * head : (h + 1) * head], jnp.zeros((width, 128 - head), F32)], 1)
            wkp[:, h * 128 : (h + 1) * 128] = wide.astype(BF)

    normed, _ = normalize(x_ref[...].astype(F32))
    ln = (normed * vec_ref[0:1, :] + vec_ref[1:2, :]).astype(BF)
    ln_ref[...] = ln
    rows = ln.shape[0]
    extra = (lax.broadcasted_iota(jnp.int32, (AUG - head, rows), 0) < 3).astype(F32).astype(BF)

    kt = dot_nt(wt[width : 2 * width, :], ln).astype(BF)
    vt = dot_nt(wt[2 * width : 3 * width, :], ln).astype(BF)
    kn = dot(ln, wkp[...]).astype(BF)
    for h in range(HEADS):
        kta_ref[h, :head, :] = kt[h * head : (h + 1) * head, :]
        kta_ref[h, head:, :] = extra
        vta_ref[h, :head, :] = vt[h * head : (h + 1) * head, :]
        vta_ref[h, head:, :] = extra
        kn_ref[h] = kn[:, h * 128 : (h + 1) * 128]

    @pl.when(step < own_steps)
    def _():
        qt = dot_nt(wt[0:width, :], ln) * (LOG2E / math.sqrt(head))
        for h in range(HEADS):
            qt_ref[h] = qt[h * head : (h + 1) * head, :].astype(BF)


def prep(rows_all, own, w_input, vec):
    total, width = rows_all.shape
    head = width // HEADS
    block = min(512, own)
    steps, own_steps = total // block, own // block
    last = own_steps - 1
    return pl.pallas_call(
        functools.partial(prep_kernel, own_steps),
        grid=(steps,),
        in_specs=[
            pl.BlockSpec((block, width), lambda i: (i, 0)),
            whole(3 * width, width),
            whole(*vec.shape),
        ],
        out_specs=[
            pl.BlockSpec((block, width), lambda i: (i, 0)),
            pl.BlockSpec((HEADS, head, block), lambda i: (0, 0, jnp.minimum(i, last))),
            pl.BlockSpec((HEADS, block, 128), lambda i: (0, i, 0)),
            pl.BlockSpec((HEADS, AUG, block), lambda i: (0, 0, i)),
            pl.BlockSpec((HEADS, AUG, block), lambda i: (0, 0, i)),
        ],
        out_shape=[
            jax.ShapeDtypeStruct((total, width), BF),
            jax.ShapeDtypeStruct((HEADS, head, own), BF),
            jax.ShapeDtypeStruct((HEADS, total, 128), BF),
            jax.ShapeDtypeStruct((HEADS, AUG, total), BF),
            jax.ShapeDtypeStruct((HEADS, AUG, total), BF),
        ],
        scratch_shapes=[pltpu.VMEM((3 * width, width), BF), pltpu.VMEM((width, HEADS * 128), BF)],
        compiler_params=params(),
        name="project",
    )(rows_all, w_input, vec)


def attend_kernel(qt_ref, kn_ref, kta_ref, vta_ref, att_ref, lse_ref):
    head, own = qt_ref.shape[1:]
    total = kn_ref.shape[1]
    tq = min(1024, own)
    tk = min(256, total)
    count = total // tk

    def longest(rows):
        rows = rows.astype(F32)
        return jnp.max(jnp.sum(rows * rows, 0, keepdims=True))

    bound = longest(qt_ref[0]) * longest(kta_ref[0, :head, :])

    def finish(where, summed, top):
        totals = summed[head : head + 1, :]
        att_ref[0, :, where] = summed[:head, :] / totals
        level = jnp.log2(totals)
        lse_ref[0, :, where] = jnp.broadcast_to(level if top is None else level + top, (8, tq))

    def scores(queries, j):
        return dot(kn_ref[0, j * tk : (j + 1) * tk, :head], queries)

    @pl.when(bound <= SAFE_BOUND * SAFE_BOUND)
    def _():
        @pl.loop(0, own // tq)
        def _(i):
            where = pl.ds(pl.multiple_of(i * tq, tq), tq)
            queries = qt_ref[0, :, where]
            summed = jnp.zeros((AUG, tq), F32)
            now = scores(queries, 0)
            for j in range(count):
                expo = jnp.exp2(now).astype(BF)
                if j + 1 < count:
                    now = scores(queries, j + 1)
                summed = summed + dot(vta_ref[0, :, j * tk : (j + 1) * tk], expo)
            finish(where, summed, None)

    @pl.when(jnp.logical_not(bound <= SAFE_BOUND * SAFE_BOUND))
    def _():
        @pl.loop(0, own // tq)
        def _(i):
            where = pl.ds(pl.multiple_of(i * tq, tq), tq)
            queries = qt_ref[0, :, where]

            def absorb(j, carry):
                summed, top = carry
                part = pl.ds(pl.multiple_of(j * tk, tk), tk)
                now = dot(kn_ref[0, part, :head], queries)
                higher = jnp.maximum(top, jnp.max(now, 0, keepdims=True))
                expo = jnp.exp2(now - higher).astype(BF)
                summed = summed * jnp.exp2(top - higher) + dot(vta_ref[0, :, part], expo)
                return summed, higher

            start = (jnp.zeros((AUG, tq), F32), jnp.full((1, tq), -1e30, F32))
            summed, top = lax.fori_loop(0, count, absorb, start)
            finish(where, summed, top)


def attend(qt, kn, kta, vta):
    _, head, own = qt.shape
    total = kn.shape[1]
    per_head = lambda *shape: pl.BlockSpec((1, *shape), lambda h: (h, 0, 0))
    return pl.pallas_call(
        attend_kernel,
        grid=(HEADS,),
        in_specs=[per_head(head, own), per_head(total, 128), per_head(AUG, total), per_head(AUG, total)],
        out_specs=[per_head(head, own), per_head(8, own)],
        out_shape=[
            jax.ShapeDtypeStruct((HEADS, head, own), F32),
            jax.ShapeDtypeStruct((HEADS, 8, own), F32),
        ],
        compiler_params=params(),
        name="attend",
    )(qt, kn, kta, vta)


def gelu_both(value):
    square = value * value
    density = jnp.exp(-0.5 * square)
    place = pl.reciprocal(1.0 + (0.3275911 / math.sqrt(2.0)) * jnp.abs(value), approx=True)
    series = 1.061405429 * place - 1.453152027
    series = series * place + 1.421413741
    series = series * place - 0.284496736
    series = series * place + 0.254829592
    tail = 0.5 * series * place * density
    below = jnp.where(value >= 0.0, 1.0 - tail, tail)
    return value * below, below + value * density * (1.0 / math.sqrt(2.0 * math.pi))


def split_rows(level, count):
    high = level.astype(BF).astype(F32)
    middle = (level - high).astype(BF).astype(F32)
    low = level - high - middle
    place = lax.broadcasted_iota(jnp.int32, (count, level.shape[1]), 0)
    rows = jnp.where(place == 0, high, jnp.where(place == 1, middle, jnp.where(place == 2, low, 0.0)))
    return rows


def middle_kernel(
    x_ref, g_ref, att_ref, lse_ref, qt_ref, w_ref, vec_ref,
    out_ref, gmid_ref, qa_ref, doa_ref, dot_ref, gwo_ref, gup_ref, gdown_ref, gvec_ref,
):
    width = x_ref.shape[1]
    head = width // HEADS
    rows = x_ref.shape[0]
    hidden_width = (w_ref.shape[0] - width) // 2
    wo = w_ref[:width, :]
    up = w_ref[width : width + hidden_width, :]
    down = w_ref[width + hidden_width :, :]
    pieces = hidden_width // width
    up_bias = jnp.concatenate([vec_ref[4 + p : 5 + p, :] for p in range(pieces)], 1)
    down_bias = vec_ref[4 + pieces : 5 + pieces, :]
    gain, bias = vec_ref[2:3, :], vec_ref[3:4, :]

    @pl.when(pl.program_id(0) == 0)
    def _():
        gwo_ref[...] = jnp.zeros_like(gwo_ref)
        gup_ref[...] = jnp.zeros_like(gup_ref)
        gdown_ref[...] = jnp.zeros_like(gdown_ref)
        gvec_ref[...] = jnp.zeros_like(gvec_ref)

    att = att_ref[...].reshape(width, rows)
    att_low = att.astype(BF)
    grad = g_ref[...]
    gradf = grad.astype(F32)
    middle = x_ref[...].astype(F32) + dot_tn(att_low, wo)
    normed, inverse = normalize(middle)
    ln_mid = (normed * gain + bias).astype(BF)
    upper = dot_nt(ln_mid, up) + up_bias
    grad_hidden = dot_nt(grad, down)
    activated, slope = gelu_both(upper)
    hidden = activated.astype(BF)
    grad_upper = (grad_hidden * slope).astype(BF)
    out_ref[...] = (middle + dot(hidden, down) + down_bias).astype(BF)
    gdown_ref[...] += dot_tn(grad, hidden)
    gup_ref[...] += dot_tn(ln_mid, grad_upper)
    grad_ln = dot(grad_upper, up)
    total_up = jnp.sum(grad_upper.astype(F32), 0, keepdims=True)
    gvec_ref[2:3, :] += jnp.sum(grad_ln * normed, 0, keepdims=True)
    gvec_ref[3:4, :] += jnp.sum(grad_ln, 0, keepdims=True)
    for p in range(pieces):
        gvec_ref[4 + p : 5 + p, :] += total_up[:, p * width : (p + 1) * width]
    gvec_ref[4 + pieces : 5 + pieces, :] += jnp.sum(gradf, 0, keepdims=True)
    grad_mid = gradf + normalize_back(grad_ln * gain, normed, inverse)
    gmid_ref[...] = grad_mid
    branch = grad_mid.astype(BF)
    gwo_ref[...] += dot(att_low, branch)
    grad_att = dot_nt(wo, branch).astype(BF)
    spare = jnp.zeros((128 - AUG, rows), F32)
    for h in range(HEADS):
        mine = slice(h * head, (h + 1) * head)
        grad_head = grad_att[mine, :]
        dot_ref[h] = grad_head
        delta = jnp.sum(grad_head.astype(F32) * att[mine, :], 0, keepdims=True)
        wide = jnp.concatenate([grad_head.astype(F32), split_rows(-delta, AUG - head), spare], 0)
        doa_ref[h] = wide.T.astype(BF)
        level = lse_ref[h, 0:1, :]
        wide = jnp.concatenate([qt_ref[h].astype(F32), split_rows(-level, AUG - head), spare], 0)
        qa_ref[h] = wide.T.astype(BF)


def between(x, grad, att, lse, qt, weights, vec):
    own, width = grad.shape
    head = width // HEADS
    hidden_width = (weights.shape[0] - width) // 2
    block = min(512, own)
    rows = lambda i: (i, 0)
    lanes = lambda i: (0, 0, i)
    tall = lambda i: (0, i, 0)
    return pl.pallas_call(
        middle_kernel,
        grid=(own // block,),
        in_specs=[
            pl.BlockSpec((block, width), rows),
            pl.BlockSpec((block, width), rows),
            pl.BlockSpec((HEADS, head, block), lanes),
            pl.BlockSpec((HEADS, 8, block), lanes),
            pl.BlockSpec((HEADS, head, block), lanes),
            whole(*weights.shape),
            whole(*vec.shape),
        ],
        out_specs=[
            pl.BlockSpec((block, width), rows),
            pl.BlockSpec((block, width), rows),
            pl.BlockSpec((HEADS, block, 128), tall),
            pl.BlockSpec((HEADS, block, 128), tall),
            pl.BlockSpec((HEADS, head, block), lanes),
            whole(width, width),
            whole(width, hidden_width),
            whole(width, hidden_width),
            whole(16, width),
        ],
        out_shape=[
            jax.ShapeDtypeStruct((own, width), BF),
            jax.ShapeDtypeStruct((own, width), F32),
            jax.ShapeDtypeStruct((HEADS, own, 128), BF),
            jax.ShapeDtypeStruct((HEADS, own, 128), BF),
            jax.ShapeDtypeStruct((HEADS, head, own), BF),
            jax.ShapeDtypeStruct((width, width), F32),
            jax.ShapeDtypeStruct((width, hidden_width), F32),
            jax.ShapeDtypeStruct((width, hidden_width), F32),
            jax.ShapeDtypeStruct((16, width), F32),
        ],
        compiler_params=params(),
        name="between",
    )(x, grad, att, lse, qt, weights, vec)


def attend_back_kernel(qa_ref, doa_ref, qt_ref, dot_ref, kta_ref, vta_ref, kn_ref, dq_ref, dk_ref, dv_ref, dk_sum, dv_sum):
    head, own = qt_ref.shape[1:]
    total = kn_ref.shape[1]
    tq = min(1024, own)
    tk = min(512, total)
    count = total // tk
    dk_sum[...] = jnp.zeros_like(dk_sum)
    dv_sum[...] = jnp.zeros_like(dv_sum)

    @pl.loop(0, own // tq)
    def _(i):
        where = pl.ds(pl.multiple_of(i * tq, tq), tq)
        queries, grads = qa_ref[0, where, :AUG], doa_ref[0, where, :AUG]
        queries_t, grads_t = qt_ref[0, :, where], dot_ref[0, :, where]

        def pair(j):
            part = slice(j * tk, (j + 1) * tk)
            return dot(queries, kta_ref[0, :, part]), dot(grads, vta_ref[0, :, part])

        grad_query = jnp.zeros((tq, 128), F32)
        level, change = pair(0)
        for j in range(count):
            part = slice(j * tk, (j + 1) * tk)
            probs = jnp.exp2(level)
            probs_low = probs.astype(BF)
            grad_scores = (probs * change).astype(BF)
            if j + 1 < count:
                level, change = pair(j + 1)
            dv_sum[:, part] += dot(grads_t, probs_low)
            dk_sum[:, part] += dot(queries_t, grad_scores)
            grad_query = grad_query + dot(grad_scores, kn_ref[0, part, :])
        dq_ref[0, where, :] = (grad_query * (1.0 / math.sqrt(head))).astype(BF)

    dk_ref[0] = (dk_sum[...] * LN2).astype(BF)
    dv_ref[0] = dv_sum[...].astype(BF)


def attend_back(qa, doa, qt, dot_t, kta, vta, kn):
    _, head, own = qt.shape
    total = kn.shape[1]
    per_head = lambda *shape: pl.BlockSpec((1, *shape), lambda h: (h, 0, 0))
    return pl.pallas_call(
        attend_back_kernel,
        grid=(HEADS,),
        in_specs=[
            per_head(own, 128), per_head(own, 128), per_head(head, own), per_head(head, own),
            per_head(AUG, total), per_head(AUG, total), per_head(total, 128),
        ],
        out_specs=[per_head(own, 128), per_head(head, total), per_head(head, total)],
        out_shape=[
            jax.ShapeDtypeStruct((HEADS, own, 128), BF),
            jax.ShapeDtypeStruct((HEADS, head, total), BF),
            jax.ShapeDtypeStruct((HEADS, head, total), BF),
        ],
        scratch_shapes=[pltpu.VMEM((head, total), F32), pltpu.VMEM((head, total), F32)],
        compiler_params=params(),
        name="attend_back",
    )(qa, doa, qt, dot_t, kta, vta, kn)


def unproject_kernel(own_steps, places, dq_ref, dk_ref, dv_ref, ln_ref, w_ref, gw_ref, part_ref, gq, gk, gv):
    width = ln_ref.shape[1]
    head = width // HEADS
    rows = ln_ref.shape[0]
    step = pl.program_id(0)

    @pl.when(step == 0)
    def _():
        gq[...] = jnp.zeros_like(gq)
        gk[...] = jnp.zeros_like(gk)
        gv[...] = jnp.zeros_like(gv)

    ln = ln_ref[...]
    dk = dk_ref[...].reshape(width, rows)
    dv = dv_ref[...].reshape(width, rows)
    gk[...] += dot(dk, ln)
    gv[...] += dot(dv, ln)
    part_ref[...] = (dot(w_ref[width : 2 * width, :], dk) + dot(w_ref[2 * width : 3 * width, :], dv)).astype(BF)

    @pl.when(step < own_steps)
    def _():
        dq = jnp.concatenate([dq_ref[h] for h in range(HEADS)], 1)
        gq[...] += dot_tn(ln, dq)

    @pl.when(step == pl.num_programs(0) - 1)
    def _():
        narrow = jnp.concatenate([gq[:, h * 128 : h * 128 + head] for h in range(HEADS)], 1)
        grads = jnp.concatenate([narrow, gk[...].T, gv[...].T], 0)
        blk_size, owners, per = places
        filler = jnp.zeros((gw_ref.shape[2] - per, width), F32)
        for slot in range(blk_size * owners):
            o, k = slot // blk_size, slot % blk_size
            piece = grads[slot * per : (slot + 1) * per, :]
            if filler.shape[0]:
                piece = jnp.concatenate([piece, filler], 0)
            gw_ref[k, o] = piece.astype(BF)


def unproject(dq, dk, dv, ln, w_input, places):
    total, width = ln.shape
    _, own, _ = dq.shape
    head = width // HEADS
    block = min(1024, own)
    own_steps = own // block
    last = own_steps - 1
    blk_size, owners, per = places
    slots = (blk_size, owners, -(-per // 16) * 16, width)
    return pl.pallas_call(
        functools.partial(unproject_kernel, own_steps, places),
        grid=(total // block,),
        in_specs=[
            pl.BlockSpec((HEADS, block, 128), lambda i: (0, jnp.minimum(i, last), 0)),
            pl.BlockSpec((HEADS, head, block), lambda i: (0, 0, i)),
            pl.BlockSpec((HEADS, head, block), lambda i: (0, 0, i)),
            pl.BlockSpec((block, width), lambda i: (i, 0)),
            whole(3 * width, width),
        ],
        out_specs=[whole(*slots), pl.BlockSpec((width, block), lambda i: (0, i))],
        out_shape=[
            jax.ShapeDtypeStruct(slots, BF),
            jax.ShapeDtypeStruct((width, total), BF),
        ],
        scratch_shapes=[
            pltpu.VMEM((width, HEADS * 128), F32), pltpu.VMEM((width, width), F32), pltpu.VMEM((width, width), F32),
        ],
        compiler_params=params(),
        name="unproject",
    )(dq, dk, dv, ln, w_input)


def finish_kernel(
    ctx_size, blk_size, x_hbm, gmid_hbm, dq_hbm, part_hbm, gw_hbm, w_ref, vec_ref,
    grad_ref, gw_ref, gvec_ref,
    x, gmid, dq, part, other, gw_own, gw_first, gw_pass, gw_second, gw_sum, gw_third, gw_fourth,
    made, vec_own, vec_near, vec_pair, vec_far, vec_four, vec_group, vec_all, vec_every, wqt,
    load_sem, part_sent, part_got, first_sent, first_got, second_sent, second_got, third_sent, third_got,
    fourth_sent, fourth_got, out_sent, out_got, keep_sem, vn_sent, vn_got, vf_sent, vf_got, vg_sent, vg_got,
    va_sent, va_got,
):
    ctx, blk, near, far, mine = partners(blk_size)
    width = x.shape[1]
    head = width // HEADS
    own = x.shape[0]
    length = own // 2
    owners = gw_hbm.shape[1]
    groups = ctx_size // owners
    core = lax.rem(blk, 2)
    group, place = lax.div(ctx, owners), lax.rem(ctx, owners)
    peers = [lax.rem(place + step, owners) for step in range(1, owners)]
    peer_devices = [(group * owners + peer, blk) for peer in peers]
    others = [lax.rem(group + step, groups) for step in range(1, groups)]
    other_devices = [(other_group * owners + place, blk) for other_group in others]
    greet([(ctx, near), (ctx, far)] + peer_devices + other_devices)

    first = [send(gw_hbm.at[2 * y + 1 - core], gw_first.at[y], first_sent.at[y], first_got.at[y], (ctx, near)) for y in range(2)]
    halves = []
    for half in (1, 0):
        there = pl.ds(half * length, length)
        halves.append(
            send(part_hbm.at[:, pl.ds(own + half * length, length)], other.at[:, there], part_sent.at[half], part_got.at[half], (ctx, near))
        )
    loads = [
        pltpu.make_async_copy(gw_hbm.at[2 * y + core], gw_own.at[y], load_sem.at[y]) for y in range(2)
    ]
    for half in (1, 0):
        rows = pl.ds(half * length, length)
        base = 2 + 4 * half
        loads += [
            pltpu.make_async_copy(x_hbm.at[rows], x.at[rows], load_sem.at[base]),
            pltpu.make_async_copy(gmid_hbm.at[rows], gmid.at[rows], load_sem.at[base + 1]),
            pltpu.make_async_copy(dq_hbm.at[:, rows], dq.at[:, rows], load_sem.at[base + 2]),
            pltpu.make_async_copy(part_hbm.at[:, rows], part.at[:, rows], load_sem.at[base + 3]),
        ]
    for load in loads:
        load.start()

    turned = w_ref[...].astype(F32).T
    for h in range(HEADS):
        wqt[h * 128 : h * 128 + head, :] = turned[h * head : (h + 1) * head, :].astype(BF)
        wqt[h * 128 + head : (h + 1) * 128, :] = jnp.zeros((128 - head, width), BF)

    gain = vec_ref[0:1, :]
    size = min(512, length)
    state = [jnp.zeros((1, width), F32), jnp.zeros((1, width), F32)]

    def rows_back(low):
        rows = slice(low, low + size)
        from_q = dot(jnp.concatenate([dq[h, rows, :] for h in range(HEADS)], 1), wqt[...])
        grad_ln = from_q + (part[:, rows].astype(F32) + other[:, rows].astype(F32)).T
        normed, inverse = normalize(x[rows, :].astype(F32))
        state[0] = state[0] + jnp.sum(grad_ln * normed, 0, keepdims=True)
        state[1] = state[1] + jnp.sum(grad_ln, 0, keepdims=True)
        made[rows, :] = (gmid[rows, :] + normalize_back(grad_ln * gain, normed, inverse)).astype(BF)

    sums = (2, owners) + gw_hbm.shape[2:]

    for y in range(2):
        loads[y].wait()
        first[y].wait_recv()
    for y in range(2):
        gw_pass[y] = (gw_own[y].astype(F32) + gw_first[y].astype(F32)).astype(BF)
    second = send(gw_pass.at[1 - mine], gw_second, second_sent, second_got, (ctx, far))

    for load in loads[2:6]:
        load.wait()
    halves[0].wait_recv()
    outs = []
    chunk = 0
    for low in range(length, own, size):
        rows_back(low)
        outs.append(
            send(
                made.at[pl.ds(low, size)], grad_ref.at[mine, pl.ds(low - length, size)],
                out_sent.at[chunk], out_got.at[chunk], (ctx, far),
            )
        )
        chunk += 1

    second.wait_recv()
    gw_sum[...] = (gw_pass[mine].astype(F32) + gw_second[...].astype(F32)).astype(BF)
    third = [
        send(gw_sum.at[peer], gw_third.at[place], third_sent.at[step], third_got.at[place], peer_devices[step])
        for step, peer in enumerate(peers)
    ]

    for load in loads[6:]:
        load.wait()
    halves[1].wait_recv()
    keeps = []
    for low in range(0, length, size):
        rows_back(low)
        keeps.append(
            pltpu.make_async_copy(made.at[pl.ds(low, size)], grad_ref.at[mine, pl.ds(low, size)], keep_sem.at[low // size])
        )
        keeps[-1].start()

    row = lax.broadcasted_iota(jnp.int32, (8, width), 0)
    vec_own[...] = jnp.where(row == 0, state[0], jnp.where(row == 1, state[1], 0.0))
    to_near = send(vec_own, vec_near, vn_sent, vn_got, (ctx, near))

    def from_peer(slot, holder, got, which):
        return pltpu.make_async_remote_copy(
            src_ref=holder.at[slot], dst_ref=holder.at[slot], send_sem=got.at[slot], recv_sem=got.at[slot],
            device_id=(ctx, near), device_id_type=MESH,
        )

    total = gw_sum[place].astype(F32)
    for slot in range(owners):
        @pl.when(place != slot)
        def _():
            from_peer(slot, gw_third, third_got, None).wait_recv()

        total = total + jnp.where(place != slot, gw_third[slot].astype(F32), 0.0)
    gw_ref[...] = total
    gw_own[0, 0] = total.astype(BF)
    if groups > 1:
        @pl.when(group > 0)
        def _():
            send(gw_own.at[0, 0], gw_fourth.at[group - 1], fourth_sent, fourth_got.at[group - 1], (place, blk))

    to_near.wait_recv()
    vec_pair[...] = vec_own[...] + vec_near[...]
    to_far = send(vec_pair, vec_far, vf_sent, vf_got, (ctx, far))
    to_far.wait_recv()
    vec_four[...] = vec_pair[...] + vec_far[...]
    to_peers = [
        send(vec_four, vec_group.at[place], vg_sent.at[step], vg_got.at[place], device)
        for step, device in enumerate(peer_devices)
    ]
    vec_total = vec_four[...]
    for slot in range(owners):
        @pl.when(place != slot)
        def _():
            from_peer(slot, vec_group, vg_got, None).wait_recv()

        vec_total = vec_total + jnp.where(place != slot, vec_group[slot], 0.0)
    vec_all[...] = vec_total
    to_others = [
        send(vec_all, vec_every.at[group], va_sent.at[step], va_got.at[group], device)
        for step, device in enumerate(other_devices)
    ]
    for slot in range(groups):
        @pl.when(group != slot)
        def _():
            from_peer(slot, vec_every, va_got, None).wait_recv()

        vec_total = vec_total + jnp.where(group != slot, vec_every[slot], 0.0)
    gvec_ref[...] = vec_total

    if groups > 1:
        @pl.when(group == 0)
        def _():
            total = gw_ref[...]
            for slot in range(groups - 1):
                from_peer(slot, gw_fourth, fourth_got, None).wait_recv()
                total = total + gw_fourth[slot].astype(F32)
            gw_ref[...] = total

        @pl.when(group > 0)
        def _():
            pltpu.make_async_remote_copy(
                src_ref=gw_own.at[0, 0], dst_ref=gw_fourth.at[group - 1], send_sem=fourth_sent,
                recv_sem=fourth_got.at[group - 1], device_id=(place, blk), device_id_type=MESH,
            ).wait_send()

    for copy in first + halves + [second] + third + [to_near, to_far] + to_peers + to_others:
        copy.wait_send()
    for copy in outs:
        copy.wait()
    for copy in keeps:
        copy.wait()


def finish(ctx_size, blk_size, rows_all, gmid, dq, part, gw, w_query, vec):
    own, width = gmid.shape
    length = own // 2
    _, owners, per, _ = gw.shape
    groups = ctx_size // owners
    dma = pltpu.SemaphoreType.DMA
    place = pl.BlockSpec(memory_space=pl.ANY)
    vmem = pl.BlockSpec(memory_space=pltpu.VMEM)
    chunks = length // min(512, length)
    low = lambda *shape: pltpu.VMEM(shape, BF)
    single = lambda *shape: pltpu.VMEM(shape, F32)
    return pl.pallas_call(
        functools.partial(finish_kernel, ctx_size, blk_size),
        in_specs=[place] * 5 + [vmem] * 2,
        out_specs=[place, vmem, vmem],
        out_shape=[
            jax.ShapeDtypeStruct((2, length, width), BF),
            jax.ShapeDtypeStruct((per, width), F32),
            jax.ShapeDtypeStruct((8, width), F32),
        ],
        scratch_shapes=[
            low(own, width), single(own, width), low(HEADS, own, 128), low(width, own), low(width, own),
            low(2, owners, per, width), low(2, owners, per, width), low(2, owners, per, width),
            low(owners, per, width), low(owners, per, width), low(owners, per, width), low(max(groups - 1, 1), per, width),
            low(own, width), single(8, width), single(8, width), single(8, width), single(8, width), single(8, width),
            single(owners, 8, width), single(8, width), single(groups, 8, width), low(HEADS * 128, width),
            dma((10,)), dma((2,)), dma((2,)), dma((2,)), dma((2,)), dma, dma, dma((max(owners - 1, 1),)), dma((owners,)),
            dma, dma((max(groups - 1, 1),)), dma((chunks,)), dma((chunks,)), dma((chunks,)), dma, dma, dma, dma,
            dma((max(owners - 1, 1),)), dma((owners,)), dma((max(groups - 1, 1),)), dma((groups,)),
        ],
        compiler_params=params(collective_id=2, has_side_effects=True),
        name="finish",
    )(rows_all, gmid, dq, part, gw, w_query, vec)


def per_device(ctx_size, blk_size, layer_in, matrices, vectors, out_grad):
    seq_count, local_rows, width = layer_in.shape
    per, entries = matrices.shape[0], vectors.shape[0]
    slots = -(-per // 16) * 16
    devices = ctx_size * blk_size
    flat = lax.axis_index("ctx") * blk_size + lax.axis_index("blk")
    mine = lax.axis_index("blk") // (blk_size // seq_count)
    far = [(b, (b + blk_size // 2) % blk_size) for b in range(blk_size)]
    in_rows = 3 * width
    owners = max(-(-in_rows // (per * blk_size)), -(-2 * width // (entries * blk_size)))

    block = jnp.concatenate(
        [
            jnp.pad(matrices, ((0, slots - per), (0, 0))),
            jnp.pad(vectors.reshape(1, entries), ((0, 15), (0, width - entries))),
        ],
        0,
    )
    rows_all, first = exchange(ctx_size, blk_size, layer_in, block, owners)
    w_input = first[:, :per].reshape(-1, width)[:in_rows]
    vec_in = first[:, slots, :entries].reshape(-1)[: 2 * width].reshape(2, width).astype(F32)
    vec_in = jnp.pad(vec_in, ((0, 6), (0, 0)))

    every = lax.all_gather(block, ("ctx", "blk"), axis=0)
    weights = every[:, :per].reshape(-1, width)[in_rows:]
    vec = every[:, slots, :entries].reshape(-1, width).astype(F32)
    vec = jnp.pad(vec, ((0, 16 - vec.shape[0]), (0, 0)))

    kept = lax.dynamic_index_in_dim(out_grad, mine, 0, keepdims=False)
    sent = lax.dynamic_index_in_dim(out_grad, 1 - mine, 0, keepdims=False)
    grad = jnp.concatenate([kept, lax.ppermute(sent, "blk", far)], 0)

    own = 2 * local_rows
    ln, qt, kn, kta, vta = prep(rows_all, own, w_input, vec_in)
    att, lse = attend(qt, kn, kta, vta)
    out, gmid, qa, doa, dot_t, gwo, gup, gdown, gvec = between(rows_all, grad, att, lse, qt, weights, vec)

    got = lax.ppermute(out[local_rows:], "blk", far)
    layer_out = jnp.where(mine == 0, jnp.stack([out[:local_rows], got]), jnp.stack([got, out[:local_rows]]))

    late = jnp.concatenate([jnp.zeros((in_rows, width), F32), gwo, gup.T, gdown.T], 0).reshape(devices, per, width)
    count = entries * devices // width
    late_vec = jnp.concatenate([jnp.zeros((2, width), F32), gvec[2:count]], 0).reshape(devices, 1, entries)
    late_vec = jnp.pad(late_vec, ((0, 0), (0, 7), (0, width - entries)))
    late = jnp.pad(late, ((0, 0), (0, -per % 8), (0, 0)))
    summed = lax.psum_scatter(jnp.concatenate([late, late_vec], 1), ("ctx", "blk"), scatter_dimension=0, tiled=False)

    dq, dk, dv = attend_back(qa, doa, qt, dot_t, kta, vta, kn)
    gw, part = unproject(dq, dk, dv, ln, w_input, (blk_size, owners, per))
    layer_grad, gw_in, gvec_in = finish(ctx_size, blk_size, rows_all, gmid, dq, part, gw, w_input[:width], vec_in)
    matrices_grad = jnp.where(flat < in_rows // per, gw_in[:per], summed[:per])
    early = jnp.pad(gvec_in[:2].reshape(-1), (0, entries * devices - 2 * width))
    vectors_grad = summed[per + -per % 8, :entries] + lax.dynamic_slice_in_dim(early, flat * entries, entries)
    return layer_out, layer_grad, matrices_grad, vectors_grad


def solution(mesh):
    rows = P("ctx", "blk", None)
    flat = P(("ctx", "blk"))
    return jax.shard_map(
        functools.partial(per_device, mesh.shape["ctx"], mesh.shape["blk"]),
        mesh=mesh,
        in_specs=(rows, flat, flat, rows),
        out_specs=(rows, rows, flat, flat),
        check_vma=False,
    )
```

```python
import functools
import math

import jax
import jax.numpy as jnp
from jax import lax
from jax.experimental import pallas as pl
from jax.experimental.pallas import tpu as pltpu
from jax.sharding import PartitionSpec as P

HEADS = 4
EPSILON = 1e-05
LOG2E = math.log2(math.e)
LN2 = math.log(2.0)
AUG = 80
SAFE_BOUND = 90.0
BF = jnp.bfloat16
F32 = jnp.float32
NT = (((1,), (1,)), ((), ()))
TN = (((0,), (0,)), ((), ()))


def dot(a, b):
    return jnp.dot(a, b, preferred_element_type=F32)


def dot_nt(a, b):
    return lax.dot_general(a, b, NT, preferred_element_type=F32)


def dot_tn(a, b):
    return lax.dot_general(a, b, TN, preferred_element_type=F32)


def params(**kw):
    return pltpu.CompilerParams(vmem_limit_bytes=60 << 20, **kw)


def whole(*shape):
    return pl.BlockSpec(shape, lambda *_: (0,) * len(shape))


def normalize(inputs):
    centre = jnp.mean(inputs, -1, keepdims=True)
    shifted = inputs - centre
    inverse = lax.rsqrt(jnp.mean(shifted * shifted, -1, keepdims=True) + EPSILON)
    return shifted * inverse, inverse


def normalize_back(grad_hat, normed, inverse):
    return inverse * (
        grad_hat
        - jnp.mean(grad_hat, -1, keepdims=True)
        - normed * jnp.mean(grad_hat * normed, -1, keepdims=True)
    )


MESH = pl.DeviceIdType.MESH


def send(source, target, sent, received, device):
    copy = pltpu.make_async_remote_copy(
        src_ref=source, dst_ref=target, send_sem=sent, recv_sem=received, device_id=device, device_id_type=MESH
    )
    copy.start()
    return copy


def greet(devices):
    barrier = pltpu.get_barrier_semaphore()
    for device in devices:
        pl.semaphore_signal(barrier, inc=1, device_id=device, device_id_type=MESH)
    pl.semaphore_wait(barrier, len(devices))


def partners(blk_size):
    ctx, blk = lax.axis_index("ctx"), lax.axis_index("blk")
    half = blk_size // 2
    return ctx, blk, blk + 1 - 2 * lax.rem(blk, 2), lax.rem(blk + half, blk_size), lax.div(blk, half)


def exchange_kernel(
    ctx_size, blk_size, x_ref, w_ref, rows_ref, all_ref,
    far_sent, far_got, near_sent, near_got, relay_sent, relay_got, own_sem,
    first_sent, first_got, second_sent, second_got, third_sent, third_got, keep_sem,
):
    ctx, blk, near, far, mine = partners(blk_size)
    length = x_ref.shape[1]
    owners = all_ref.shape[0] // blk_size
    chunks = far_sent.shape[0]
    size = length // chunks
    others = [lax.rem(ctx + step, ctx_size) for step in range(1, ctx_size)]
    greet([(ctx, near), (ctx, far)] + [(other, blk) for other in others])

    @pl.when(ctx < owners)
    def _():
        keep = pltpu.make_async_copy(w_ref, all_ref.at[ctx * blk_size + blk], keep_sem)
        keep.start()
        for step, other in enumerate(others):
            send(w_ref, all_ref.at[ctx * blk_size + blk], first_sent.at[step], first_got.at[ctx], (other, blk))

    far_copies = []
    for c in range(chunks):
        part = pl.ds(c * size, size)
        far_copies.append(
            send(x_ref.at[1 - mine, part], rows_ref.at[pl.ds(length + c * size, size)], far_sent.at[c], far_got.at[c], (ctx, far))
        )
    near_copy = send(x_ref.at[mine], rows_ref.at[pl.ds(2 * length, length)], near_sent, near_got, (ctx, near))
    own_copy = pltpu.make_async_copy(x_ref.at[mine], rows_ref.at[pl.ds(0, length)], own_sem)
    own_copy.start()

    @pl.when(ctx < owners)
    def _():
        pltpu.make_async_copy(w_ref, all_ref.at[ctx * blk_size + blk], keep_sem).wait()

    def copy_of(slot, sent, got, device):
        return pltpu.make_async_remote_copy(
            src_ref=all_ref.at[slot], dst_ref=all_ref.at[slot], send_sem=sent, recv_sem=got,
            device_id=device, device_id_type=MESH,
        )

    for o in range(owners):
        @pl.when(ctx != o)
        def _():
            copy_of(o * blk_size + blk, first_sent.at[0], first_got.at[o], (ctx, near)).wait_recv()

        copy_of(o * blk_size + blk, second_sent.at[o], second_got.at[o], (ctx, far)).start()
        copy_of(o * blk_size + blk, third_sent.at[o], third_got.at[o], (ctx, near)).start()
    relays = []
    for c in range(chunks):
        far_copies[c].wait_recv()
        here = rows_ref.at[pl.ds(length + c * size, size)]
        there = rows_ref.at[pl.ds(3 * length + c * size, size)]
        relays.append(send(here, there, relay_sent.at[c], relay_got.at[c], (ctx, near)))
    for o in range(owners):
        copy_of(o * blk_size + far, second_sent.at[o], second_got.at[o], (ctx, far)).wait_recv()
        copy_of(o * blk_size + far, third_sent.at[owners + o], third_got.at[owners + o], (ctx, near)).start()

    for o in range(owners):
        copy_of(o * blk_size + blk, second_sent.at[o], second_got.at[o], (ctx, far)).wait_send()
        for turn in range(2):
            copy_of(o * blk_size + blk, third_sent.at[turn * owners + o], third_got.at[turn * owners + o], (ctx, near)).wait()
    for c in range(chunks):
        far_copies[c].wait_send()
        relays[c].wait()
    near_copy.wait()
    own_copy.wait()

    @pl.when(ctx < owners)
    def _():
        for step, other in enumerate(others):
            pltpu.make_async_remote_copy(
                src_ref=w_ref, dst_ref=all_ref.at[ctx * blk_size + blk], send_sem=first_sent.at[step],
                recv_sem=first_got.at[ctx], device_id=(other, blk), device_id_type=MESH,
            ).wait_send()


def exchange(ctx_size, blk_size, layer_in, block, owners):
    seq_count, length, width = layer_in.shape
    chunks = 4 if length % 64 == 0 else 1
    dma = pltpu.SemaphoreType.DMA
    place = pl.BlockSpec(memory_space=pl.ANY)
    return pl.pallas_call(
        functools.partial(exchange_kernel, ctx_size, blk_size),
        in_specs=[place] * 2,
        out_specs=[place] * 2,
        out_shape=[
            jax.ShapeDtypeStruct((4 * length, width), BF),
            jax.ShapeDtypeStruct((owners * blk_size, *block.shape), BF),
        ],
        scratch_shapes=[
            dma((chunks,)), dma((chunks,)), dma, dma, dma((chunks,)), dma((chunks,)), dma,
            dma((ctx_size - 1,)) if ctx_size > 1 else dma((1,)), dma((owners,)), dma((owners,)), dma((owners,)),
            dma((2 * owners,)), dma((2 * owners,)), dma,
        ],
        compiler_params=params(collective_id=1, has_side_effects=True),
        name="exchange",
    )(layer_in, block)


def prep_kernel(own_steps, x_ref, w_ref, vec_ref, ln_ref, qt_ref, kn_ref, kta_ref, vta_ref, wt, wkp):
    width = x_ref.shape[1]
    head = width // HEADS
    step = pl.program_id(0)

    @pl.when(step == 0)
    def _():
        for index in range(3):
            piece = w_ref[index * width : (index + 1) * width, :].astype(F32)
            wt[index * width : (index + 1) * width, :] = piece.T.astype(BF)
        wk = w_ref[width : 2 * width, :].astype(F32)
        for h in range(HEADS):
            wide = jnp.concatenate([wk[:, h * head : (h + 1) * head], jnp.zeros((width, 128 - head), F32)], 1)
            wkp[:, h * 128 : (h + 1) * 128] = wide.astype(BF)

    normed, _ = normalize(x_ref[...].astype(F32))
    ln = (normed * vec_ref[0:1, :] + vec_ref[1:2, :]).astype(BF)
    ln_ref[...] = ln
    rows = ln.shape[0]
    extra = (lax.broadcasted_iota(jnp.int32, (AUG - head, rows), 0) < 3).astype(F32).astype(BF)

    kt = dot_nt(wt[width : 2 * width, :], ln).astype(BF)
    vt = dot_nt(wt[2 * width : 3 * width, :], ln).astype(BF)
    kn = dot(ln, wkp[...]).astype(BF)
    for h in range(HEADS):
        kta_ref[h, :head, :] = kt[h * head : (h + 1) * head, :]
        kta_ref[h, head:, :] = extra
        vta_ref[h, :head, :] = vt[h * head : (h + 1) * head, :]
        vta_ref[h, head:, :] = extra
        kn_ref[h] = kn[:, h * 128 : (h + 1) * 128]

    @pl.when(step < own_steps)
    def _():
        qt = dot_nt(wt[0:width, :], ln) * (LOG2E / math.sqrt(head))
        for h in range(HEADS):
            qt_ref[h] = qt[h * head : (h + 1) * head, :].astype(BF)


def prep(rows_all, own, w_input, vec):
    total, width = rows_all.shape
    head = width // HEADS
    block = min(512, own)
    steps, own_steps = total // block, own // block
    last = own_steps - 1
    return pl.pallas_call(
        functools.partial(prep_kernel, own_steps),
        grid=(steps,),
        in_specs=[
            pl.BlockSpec((block, width), lambda i: (i, 0)),
            whole(3 * width, width),
            whole(*vec.shape),
        ],
        out_specs=[
            pl.BlockSpec((block, width), lambda i: (i, 0)),
            pl.BlockSpec((HEADS, head, block), lambda i: (0, 0, jnp.minimum(i, last))),
            pl.BlockSpec((HEADS, block, 128), lambda i: (0, i, 0)),
            pl.BlockSpec((HEADS, AUG, block), lambda i: (0, 0, i)),
            pl.BlockSpec((HEADS, AUG, block), lambda i: (0, 0, i)),
        ],
        out_shape=[
            jax.ShapeDtypeStruct((total, width), BF),
            jax.ShapeDtypeStruct((HEADS, head, own), BF),
            jax.ShapeDtypeStruct((HEADS, total, 128), BF),
            jax.ShapeDtypeStruct((HEADS, AUG, total), BF),
            jax.ShapeDtypeStruct((HEADS, AUG, total), BF),
        ],
        scratch_shapes=[pltpu.VMEM((3 * width, width), BF), pltpu.VMEM((width, HEADS * 128), BF)],
        compiler_params=params(),
        name="project",
    )(rows_all, w_input, vec)


def attend_kernel(qt_ref, kn_ref, kta_ref, vta_ref, att_ref, lse_ref):
    head, own = qt_ref.shape[1:]
    total = kn_ref.shape[1]
    tq = min(1024, own)
    tk = min(256, total)
    count = total // tk

    def longest(rows):
        rows = rows.astype(F32)
        return jnp.max(jnp.sum(rows * rows, 0, keepdims=True))

    bound = longest(qt_ref[0]) * longest(kta_ref[0, :head, :])

    def finish(where, summed, top):
        totals = summed[head : head + 1, :]
        att_ref[0, :, where] = summed[:head, :] / totals
        level = jnp.log2(totals)
        lse_ref[0, :, where] = jnp.broadcast_to(level if top is None else level + top, (8, tq))

    def scores(queries, j):
        return dot(kn_ref[0, j * tk : (j + 1) * tk, :head], queries)

    @pl.when(bound <= SAFE_BOUND * SAFE_BOUND)
    def _():
        @pl.loop(0, own // tq)
        def _(i):
            where = pl.ds(pl.multiple_of(i * tq, tq), tq)
            queries = qt_ref[0, :, where]
            summed = jnp.zeros((AUG, tq), F32)
            now = scores(queries, 0)
            for j in range(count):
                expo = jnp.exp2(now).astype(BF)
                if j + 1 < count:
                    now = scores(queries, j + 1)
                summed = summed + dot(vta_ref[0, :, j * tk : (j + 1) * tk], expo)
            finish(where, summed, None)

    @pl.when(jnp.logical_not(bound <= SAFE_BOUND * SAFE_BOUND))
    def _():
        @pl.loop(0, own // tq)
        def _(i):
            where = pl.ds(pl.multiple_of(i * tq, tq), tq)
            queries = qt_ref[0, :, where]

            def absorb(j, carry):
                summed, top = carry
                part = pl.ds(pl.multiple_of(j * tk, tk), tk)
                now = dot(kn_ref[0, part, :head], queries)
                higher = jnp.maximum(top, jnp.max(now, 0, keepdims=True))
                expo = jnp.exp2(now - higher).astype(BF)
                summed = summed * jnp.exp2(top - higher) + dot(vta_ref[0, :, part], expo)
                return summed, higher

            start = (jnp.zeros((AUG, tq), F32), jnp.full((1, tq), -1e30, F32))
            summed, top = lax.fori_loop(0, count, absorb, start)
            finish(where, summed, top)


def attend(qt, kn, kta, vta):
    _, head, own = qt.shape
    total = kn.shape[1]
    per_head = lambda *shape: pl.BlockSpec((1, *shape), lambda h: (h, 0, 0))
    return pl.pallas_call(
        attend_kernel,
        grid=(HEADS,),
        in_specs=[per_head(head, own), per_head(total, 128), per_head(AUG, total), per_head(AUG, total)],
        out_specs=[per_head(head, own), per_head(8, own)],
        out_shape=[
            jax.ShapeDtypeStruct((HEADS, head, own), F32),
            jax.ShapeDtypeStruct((HEADS, 8, own), F32),
        ],
        compiler_params=params(),
        name="attend",
    )(qt, kn, kta, vta)


def gelu_both(value):
    square = value * value
    density = jnp.exp(-0.5 * square)
    place = pl.reciprocal(1.0 + (0.3275911 / math.sqrt(2.0)) * jnp.abs(value), approx=True)
    series = 1.061405429 * place - 1.453152027
    series = series * place + 1.421413741
    series = series * place - 0.284496736
    series = series * place + 0.254829592
    tail = 0.5 * series * place * density
    below = jnp.where(value >= 0.0, 1.0 - tail, tail)
    return value * below, below + value * density * (1.0 / math.sqrt(2.0 * math.pi))


def split_rows(level, count):
    high = level.astype(BF).astype(F32)
    middle = (level - high).astype(BF).astype(F32)
    low = level - high - middle
    place = lax.broadcasted_iota(jnp.int32, (count, level.shape[1]), 0)
    rows = jnp.where(place == 0, high, jnp.where(place == 1, middle, jnp.where(place == 2, low, 0.0)))
    return rows


def middle_kernel(
    per, x_ref, g_ref, att_ref, lse_ref, qt_ref, w_ref, vec_ref,
    out_ref, gmid_ref, qa_ref, doa_ref, dot_ref, late_ref, gvec_ref, gwo_ref, gup_ref, gdown_ref,
):
    width = x_ref.shape[1]
    head = width // HEADS
    rows = x_ref.shape[0]
    hidden_width = (w_ref.shape[0] - width) // 2
    wo = w_ref[:width, :]
    up = w_ref[width : width + hidden_width, :]
    down = w_ref[width + hidden_width :, :]
    pieces = hidden_width // width
    up_bias = jnp.concatenate([vec_ref[4 + p : 5 + p, :] for p in range(pieces)], 1)
    down_bias = vec_ref[4 + pieces : 5 + pieces, :]
    gain, bias = vec_ref[2:3, :], vec_ref[3:4, :]

    @pl.when(pl.program_id(0) == 0)
    def _():
        gwo_ref[...] = jnp.zeros_like(gwo_ref)
        gup_ref[...] = jnp.zeros_like(gup_ref)
        gdown_ref[...] = jnp.zeros_like(gdown_ref)
        gvec_ref[...] = jnp.zeros_like(gvec_ref)

    att = att_ref[...].reshape(width, rows)
    att_low = att.astype(BF)
    grad = g_ref[...]
    gradf = grad.astype(F32)
    middle = x_ref[...].astype(F32) + dot_tn(att_low, wo)
    normed, inverse = normalize(middle)
    ln_mid = (normed * gain + bias).astype(BF)
    upper = dot_nt(ln_mid, up) + up_bias
    grad_hidden = dot_nt(grad, down)
    activated, slope = gelu_both(upper)
    hidden = activated.astype(BF)
    grad_upper = (grad_hidden * slope).astype(BF)
    out_ref[...] = (middle + dot(hidden, down) + down_bias).astype(BF)
    gdown_ref[...] += dot_tn(grad, hidden)
    gup_ref[...] += dot_tn(ln_mid, grad_upper)
    grad_ln = dot(grad_upper, up)
    total_up = jnp.sum(grad_upper.astype(F32), 0, keepdims=True)
    gvec_ref[2:3, :] += jnp.sum(grad_ln * normed, 0, keepdims=True)
    gvec_ref[3:4, :] += jnp.sum(grad_ln, 0, keepdims=True)
    for p in range(pieces):
        gvec_ref[4 + p : 5 + p, :] += total_up[:, p * width : (p + 1) * width]
    gvec_ref[4 + pieces : 5 + pieces, :] += jnp.sum(gradf, 0, keepdims=True)
    grad_mid = gradf + normalize_back(grad_ln * gain, normed, inverse)
    gmid_ref[...] = grad_mid
    branch = grad_mid.astype(BF)
    gwo_ref[...] += dot(att_low, branch)
    grad_att = dot_nt(wo, branch).astype(BF)
    spare = jnp.zeros((128 - AUG, rows), F32)
    for h in range(HEADS):
        mine = slice(h * head, (h + 1) * head)
        grad_head = grad_att[mine, :]
        dot_ref[h] = grad_head
        delta = jnp.sum(grad_head.astype(F32) * att[mine, :], 0, keepdims=True)
        wide = jnp.concatenate([grad_head.astype(F32), split_rows(-delta, AUG - head), spare], 0)
        doa_ref[h] = wide.T.astype(BF)
        level = lse_ref[h, 0:1, :]
        wide = jnp.concatenate([qt_ref[h].astype(F32), split_rows(-level, AUG - head), spare], 0)
        qa_ref[h] = wide.T.astype(BF)

    @pl.when(pl.program_id(0) == pl.num_programs(0) - 1)
    def _():
        grads = jnp.concatenate([gwo_ref[...], gup_ref[...].T, gdown_ref[...].T], 0)
        into_slots(late_ref, grads, per)


def into_slots(slots_ref, grads, per):
    blk_size, owners, padded, width = slots_ref.shape
    filler = jnp.zeros((padded - per, width), F32)
    for slot in range(blk_size * owners):
        piece = grads[slot * per : (slot + 1) * per, :]
        if padded > per:
            piece = jnp.concatenate([piece, filler], 0)
        slots_ref[slot % blk_size, slot // blk_size] = piece.astype(BF)


def between(x, grad, att, lse, qt, weights, vec, blk_size, per):
    own, width = grad.shape
    head = width // HEADS
    hidden_width = (weights.shape[0] - width) // 2
    block = min(512, own)
    rows = lambda i: (i, 0)
    lanes = lambda i: (0, 0, i)
    tall = lambda i: (0, i, 0)
    slots = (blk_size, weights.shape[0] // (blk_size * per), -(-per // 16) * 16, width)
    return pl.pallas_call(
        functools.partial(middle_kernel, per),
        grid=(own // block,),
        in_specs=[
            pl.BlockSpec((block, width), rows),
            pl.BlockSpec((block, width), rows),
            pl.BlockSpec((HEADS, head, block), lanes),
            pl.BlockSpec((HEADS, 8, block), lanes),
            pl.BlockSpec((HEADS, head, block), lanes),
            whole(*weights.shape),
            whole(*vec.shape),
        ],
        out_specs=[
            pl.BlockSpec((block, width), rows),
            pl.BlockSpec((block, width), rows),
            pl.BlockSpec((HEADS, block, 128), tall),
            pl.BlockSpec((HEADS, block, 128), tall),
            pl.BlockSpec((HEADS, head, block), lanes),
            whole(*slots),
            whole(16, width),
        ],
        out_shape=[
            jax.ShapeDtypeStruct((own, width), BF),
            jax.ShapeDtypeStruct((own, width), F32),
            jax.ShapeDtypeStruct((HEADS, own, 128), BF),
            jax.ShapeDtypeStruct((HEADS, own, 128), BF),
            jax.ShapeDtypeStruct((HEADS, head, own), BF),
            jax.ShapeDtypeStruct(slots, BF),
            jax.ShapeDtypeStruct((16, width), F32),
        ],
        scratch_shapes=[
            pltpu.VMEM((width, width), F32), pltpu.VMEM((width, hidden_width), F32), pltpu.VMEM((width, hidden_width), F32),
        ],
        compiler_params=params(),
        name="between",
    )(x, grad, att, lse, qt, weights, vec)


def back_kernel(
    ctx_size, blk_size, per,
    qa_hbm, doa_hbm, qt_hbm, dot_hbm, kta_hbm, vta_hbm, kn_hbm, ln_hbm, x_hbm, gmid_hbm, out_hbm, late_hbm,
    gvec_in, w_ref, vec_ref,
    grad_ref, out_ref, gw_ref, gvec_ref,
    qa, doa, qt, dot_t, kta, vta, kn, ln, x, gmid, made,
    dq_sum, dk_sum, dv_sum, gq, gk, gv, part, part_out, part_in, wqt,
    late_own, late_one, late_pass, late_two, late_sum, late_three,
    early, early_one, early_pass, early_two, early_sum, early_three,
    vec_own, vec_one, vec_pair, vec_two, vec_sum, vec_three,
    head_sem, load_sem, out_sent, out_got, keep_sem, grad_sent, grad_got, part_sent, part_got,
    l1_sent, l1_got, l2_sent, l2_got, l3_sent, l3_got,
    e1_sent, e1_got, e2_sent, e2_got, e3_sent, e3_got,
    v1_sent, v1_got, v2_sent, v2_got, v3_sent, v3_got,
):
    ctx, blk, near, far, mine = partners(blk_size)
    core = lax.rem(blk, 2)
    own, width = x.shape
    length = own // 2
    head = width // HEADS
    owners = early.shape[1]
    groups = ctx_size // owners
    late_count = late_own.shape[1]
    group, place = lax.div(ctx, owners), lax.rem(ctx, owners)
    others = [lax.rem(ctx + step, ctx_size) for step in range(1, ctx_size)]
    peers = [lax.rem(place + step, owners) for step in range(1, owners)]

    def remote(source, target, sent, got, device):
        return pltpu.make_async_remote_copy(
            src_ref=source, dst_ref=target, send_sem=sent, recv_sem=got, device_id=device, device_id_type=MESH
        )

    to_near, to_far = (ctx, near), (ctx, far)
    local = pltpu.make_async_copy

    def head_loads(h):
        pairs = ((qa_hbm, qa), (doa_hbm, doa), (qt_hbm, qt), (dot_hbm, dot_t), (kta_hbm, kta), (vta_hbm, vta), (kn_hbm, kn))
        return [local(a.at[h], b.at[h], head_sem.at[i, h]) for i, (a, b) in enumerate(pairs)]

    loads = [
        local(ln_hbm, ln, load_sem.at[0]),
        local(x_hbm.at[pl.ds(0, own)], x, load_sem.at[1]),
        local(gmid_hbm, gmid, load_sem.at[2]),
    ]
    late_loads = [local(late_hbm.at[2 * y + core], late_own.at[y], load_sem.at[3 + y]) for y in range(2)]
    out_keep = local(out_hbm.at[pl.ds(0, length)], out_ref.at[mine], keep_sem.at[0])
    out_send = remote(out_hbm.at[pl.ds(length, length)], out_ref.at[mine], out_sent, out_got, to_far)

    late_first = [
        remote(late_hbm.at[2 * y + 1 - core], late_one.at[y], l1_sent.at[y], l1_got.at[y], to_near) for y in range(2)
    ]
    late_second = remote(late_pass.at[1 - mine], late_two, l2_sent, l2_got, to_far)

    def late_third(step):
        other = others[step]
        return remote(
            late_sum.at[jnp.maximum(other - owners, 0)], late_three.at[ctx], l3_sent.at[step], l3_got.at[ctx], (other, blk)
        )

    def late_third_from(other):
        return remote(late_sum.at[0], late_three.at[other], l3_sent.at[0], l3_got.at[other], to_near)

    def grad_send(half, c, size):
        return remote(
            made.at[pl.ds(half * length + c * size, size)], grad_ref.at[mine, pl.ds(c * size, size)],
            grad_sent.at[c], grad_got.at[c], to_far,
        )

    def grad_keep(c, size):
        return local(made.at[pl.ds(c * size, size)], grad_ref.at[mine, pl.ds(c * size, size)], keep_sem.at[1 + c])

    def part_send(half):
        return remote(part_out.at[half], part_in.at[half], part_sent.at[half], part_got.at[half], to_near)

    early_first = [
        remote(early.at[2 * y + 1 - core], early_one.at[y], e1_sent.at[y], e1_got.at[y], to_near) for y in range(2)
    ]
    vec_first = remote(vec_own, vec_one, v1_sent, v1_got, to_near)
    here = mine * owners + place
    plane = [(1 - mine, place, to_far)]
    for peer in peers:
        plane.append((mine, peer, (group * owners + peer, blk)))
        plane.append((1 - mine, peer, (group * owners + peer, far)))
    early_second = [
        remote(early_pass.at[y, r], early_two.at[here], e2_sent.at[i], e2_got.at[here], device)
        for i, (y, r, device) in enumerate(plane)
    ]
    vec_second = [
        remote(vec_pair, vec_two.at[here], v2_sent.at[i], v2_got.at[here], device) for i, (y, r, device) in enumerate(plane)
    ]
    plane_slots = [y * owners + r for y, r, _ in plane]
    early_third = remote(early_sum, early_three.at[jnp.maximum(group - 1, 0)], e3_sent, e3_got.at[jnp.maximum(group - 1, 0)], (place, blk))
    other_groups = [lax.rem(group + step, groups) for step in range(1, groups)]
    vec_third = [
        remote(vec_sum, vec_three.at[group], v3_sent.at[i], v3_got.at[group], (other * owners + place, blk))
        for i, other in enumerate(other_groups)
    ]

    greet([to_near, to_far] + [(other, blk) for other in others] + [(group * owners + peer, far) for peer in peers])
    for h in range(HEADS):
        for load in head_loads(h):
            load.start()
    for copy in late_first + late_loads + [out_send, out_keep] + loads:
        copy.start()
    dq_sum[...] = jnp.zeros_like(dq_sum)
    dk_sum[...] = jnp.zeros_like(dk_sum)
    dv_sum[...] = jnp.zeros_like(dv_sum)
    gq[...] = jnp.zeros_like(gq)
    gk[...] = jnp.zeros_like(gk)
    gv[...] = jnp.zeros_like(gv)
    vec_own[...] = gvec_in[...]

    tk = min(256, length)
    wk, wv = w_ref[width : 2 * width, :], w_ref[2 * width : 3 * width, :]
    gain = vec_ref[0:1, :]
    size = min(512, length)
    chunks = length // size

    def terms(half):
        for core_rows in range(2):
            low = core_rows * own + half * length
            rows = slice(low, low + length)
            dk = (dk_sum[:, :, rows] * LN2).astype(BF).reshape(width, length)
            dv = dv_sum[:, :, rows].astype(BF).reshape(width, length)
            gk[...] += dot(dk, ln[rows, :])
            gv[...] += dot(dv, ln[rows, :])
            both = dot(wk, dk) + dot(wv, dv)
            if core_rows == 0:
                part[half] = both
            else:
                part_out[half] = both.astype(BF)
                part_send(half).start()
        rows = slice(half * length, (half + 1) * length)
        gq[...] += dot_tn(ln[rows, :], query_grads(rows))

    def query_grads(rows):
        return jnp.concatenate([(dq_sum[h, rows, :] * (1.0 / math.sqrt(head))).astype(BF) for h in range(HEADS)], 1)

    def rows_back(half):
        for c in range(chunks):
            rows = slice(half * length + c * size, half * length + (c + 1) * size)
            lanes = slice(c * size, (c + 1) * size)
            grad_ln = dot(query_grads(rows), wqt[...]) + (part[half, :, lanes] + part_in[half, :, lanes].astype(F32)).T
            normed, inverse = normalize(x[rows, :].astype(F32))
            vec_own[0:1, :] += jnp.sum(grad_ln * normed, 0, keepdims=True)
            vec_own[1:2, :] += jnp.sum(grad_ln, 0, keepdims=True)
            made[rows, :] = (gmid[rows, :] + normalize_back(grad_ln * gain, normed, inverse)).astype(BF)
            (grad_send(half, c, size) if half else grad_keep(c, size)).start()

    @pl.loop(0, 4 * HEADS)
    def _(t):
        block, h = lax.div(t, HEADS), lax.rem(t, HEADS)

        @pl.when(block == 0)
        def _():
            for load in head_loads(h):
                load.wait()

        @pl.when(t == 2)
        def _():
            for y in range(2):
                late_loads[y].wait()
                late_first[y].wait_recv()
                late_pass[y] = (late_own[y].astype(F32) + late_one[y].astype(F32)).astype(BF)
            late_second.start()

        @pl.when(t == 5)
        def _():
            late_second.wait_recv()
            late_sum[...] = (late_pass[mine].astype(F32) + late_two[...].astype(F32)).astype(BF)
            for step, other in enumerate(others):
                @pl.when(other >= owners)
                def _():
                    late_third(step).start()

        @pl.when(t == 3 * HEADS)
        def _():
            turned = w_ref[:width, :].astype(F32).T
            for head_index in range(HEADS):
                low = head_index * 128
                wqt[low : low + head, :] = turned[head_index * head : (head_index + 1) * head, :].astype(BF)
                wqt[low + head : low + 128, :] = jnp.zeros((128 - head, width), BF)
            for load in loads:
                load.wait()
            terms(1)

        @pl.when(t == 3 * HEADS + 1)
        def _():
            part_send(1).wait_recv()
            rows_back(1)

        first_half = jnp.logical_or(block == 0, block == 3)
        where = pl.ds(pl.multiple_of(jnp.where(first_half, 0, length), length), length)
        base = jnp.where(block < 2, length, 0)
        queries, grads = qa[h, where, :AUG], doa[h, where, :AUG]
        queries_t, grads_t = qt[h, :, where], dot_t[h, :, where]
        parts = []
        for offset in (0, own):
            for low in range(0, length, tk):
                parts.append(pl.ds(pl.multiple_of(base + (offset + low), tk), tk))

        def pair(part):
            return dot(queries, kta[h, :, part]), dot(grads, vta[h, :, part])

        grad_query = jnp.zeros((length, 128), F32)
        level, change = pair(parts[0])
        for j, part_now in enumerate(parts):
            probs = jnp.exp2(level)
            probs_low = probs.astype(BF)
            grad_scores = (probs * change).astype(BF)
            if j + 1 < len(parts):
                level, change = pair(parts[j + 1])
            dv_sum[h, :, part_now] += dot(grads_t, probs_low)
            dk_sum[h, :, part_now] += dot(queries_t, grad_scores)
            grad_query = grad_query + dot(grad_scores, kn[h, part_now, :])
        dq_sum[h, where, :] += grad_query

    terms(0)
    grads = jnp.concatenate([jnp.concatenate([gq[:, h * 128 : h * 128 + head] for h in range(HEADS)], 1), gk[...].T, gv[...].T], 0)
    into_slots(early, grads, per)
    for copy in early_first:
        copy.start()
    part_send(0).wait_recv()
    rows_back(0)
    vec_first.start()
    for y in range(2):
        early_first[y].wait_recv()
        early_pass[y] = (early[2 * y + core].astype(F32) + early_one[y].astype(F32)).astype(BF)
    for copy in early_second:
        copy.start()
    vec_first.wait_recv()
    vec_pair[...] = vec_own[...] + vec_one[...]
    for copy in vec_second:
        copy.start()

    @pl.when(ctx >= owners)
    def _():
        total = late_sum[jnp.maximum(ctx - owners, 0)].astype(F32)
        for other in others:
            late_third_from(other).wait_recv()
            total = total + late_three[other].astype(F32)
        gw_ref[...] = total

    def from_plane(slot, holder, got):
        return remote(holder.at[slot], holder.at[slot], got.at[slot], got.at[slot], to_near)

    total = early_pass[mine, place].astype(F32)
    for slot in plane_slots:
        from_plane(slot, early_two, e2_got).wait_recv()
        total = total + early_two[slot].astype(F32)
    early_sum[...] = total.astype(BF)
    if groups > 1:
        @pl.when(group > 0)
        def _():
            early_third.start()

    vec_total = vec_pair[...]
    for slot in plane_slots:
        from_plane(slot, vec_two, v2_got).wait_recv()
        vec_total = vec_total + vec_two[slot]
    vec_sum[...] = vec_total
    for copy in vec_third:
        copy.start()

    @pl.when(group == 0)
    def _():
        whole_sum = total
        for slot in range(groups - 1):
            from_plane(slot, early_three, e3_got).wait_recv()
            whole_sum = whole_sum + early_three[slot].astype(F32)
        gw_ref[...] = whole_sum

    for other in other_groups:
        from_plane(other, vec_three, v3_got).wait_recv()
        vec_total = vec_total + vec_three[other]
    gvec_ref[...] = vec_total

    for copy in late_first + [late_second, part_send(0), part_send(1), vec_first] + early_first + early_second + vec_second + vec_third:
        copy.wait_send()
    for step, other in enumerate(others):
        @pl.when(other >= owners)
        def _():
            late_third(step).wait_send()

    if groups > 1:
        @pl.when(group > 0)
        def _():
            early_third.wait_send()

    out_keep.wait()
    out_send.wait()
    for c in range(chunks):
        grad_keep(c, size).wait()
        grad_send(1, c, size).wait()


def back(ctx_size, blk_size, per, owners, qa, doa, qt, dot_t, kta, vta, kn, ln, rows_all, gmid, out, late, gvec, w_input, vec):
    own, width = gmid.shape
    head = width // HEADS
    total = 2 * own
    length = own // 2
    groups = ctx_size // owners
    _, late_count, padded, _ = late.shape
    dma = pltpu.SemaphoreType.DMA
    place = pl.BlockSpec(memory_space=pl.ANY)
    vmem = pl.BlockSpec(memory_space=pltpu.VMEM)
    chunks = length // min(512, length)
    low = lambda *shape: pltpu.VMEM(shape, BF)
    single = lambda *shape: pltpu.VMEM(shape, F32)
    plane = 2 * owners
    some = lambda count: dma((max(count, 1),))
    return pl.pallas_call(
        functools.partial(back_kernel, ctx_size, blk_size, per),
        in_specs=[place] * 12 + [vmem] * 3,
        out_specs=[place, place, vmem, vmem],
        out_shape=[
            jax.ShapeDtypeStruct((2, length, width), BF),
            jax.ShapeDtypeStruct((2, length, width), BF),
            jax.ShapeDtypeStruct((padded, width), F32),
            jax.ShapeDtypeStruct((16, width), F32),
        ],
        scratch_shapes=[
            low(HEADS, own, 128), low(HEADS, own, 128), low(HEADS, head, own), low(HEADS, head, own),
            low(HEADS, AUG, total), low(HEADS, AUG, total), low(HEADS, total, 128), low(total, width),
            low(own, width), single(own, width), low(own, width),
            single(HEADS, own, 128), single(HEADS, head, total), single(HEADS, head, total),
            single(width, HEADS * 128), single(width, width), single(width, width),
            single(2, width, length), low(2, width, length), low(2, width, length), low(HEADS * 128, width),
            low(2, late_count, padded, width), low(2, late_count, padded, width), low(2, late_count, padded, width),
            low(late_count, padded, width), low(late_count, padded, width), low(ctx_size, padded, width),
            low(blk_size, owners, padded, width), low(2, owners, padded, width), low(2, owners, padded, width),
            low(plane, padded, width), low(padded, width), low(max(groups - 1, 1), padded, width),
            single(16, width), single(16, width), single(16, width), single(plane, 16, width), single(16, width),
            single(groups, 16, width),
            dma((7, HEADS)), dma((5,)), dma, dma, dma((1 + chunks,)), dma((chunks,)), dma((chunks,)), dma((2,)), dma((2,)),
            dma((2,)), dma((2,)), dma, dma, some(ctx_size - 1), dma((ctx_size,)),
            dma((2,)), dma((2,)), some(plane - 1), dma((plane,)), dma, some(groups - 1),
            dma, dma, some(plane - 1), dma((plane,)), some(groups - 1), dma((groups,)),
        ],
        compiler_params=params(collective_id=2, has_side_effects=True),
        name="back",
    )(qa, doa, qt, dot_t, kta, vta, kn, ln, rows_all, gmid, out, late, gvec, w_input, vec)


def per_device(ctx_size, blk_size, layer_in, matrices, vectors, out_grad):
    seq_count, local_rows, width = layer_in.shape
    per, entries = matrices.shape[0], vectors.shape[0]
    slots = -(-per // 16) * 16
    devices = ctx_size * blk_size
    flat = lax.axis_index("ctx") * blk_size + lax.axis_index("blk")
    mine = lax.axis_index("blk") // (blk_size // seq_count)
    far = [(b, (b + blk_size // 2) % blk_size) for b in range(blk_size)]
    in_rows = 3 * width
    owners = max(-(-in_rows // (per * blk_size)), -(-2 * width // (entries * blk_size)))

    block = jnp.concatenate(
        [
            jnp.pad(matrices, ((0, slots - per), (0, 0))),
            jnp.pad(vectors.reshape(1, entries), ((0, 15), (0, width - entries))),
        ],
        0,
    )
    rows_all, first = exchange(ctx_size, blk_size, layer_in, block, owners)
    w_input = first[:, :per].reshape(-1, width)[:in_rows]
    vec_in = first[:, slots, :entries].reshape(-1)[: 2 * width].reshape(2, width).astype(F32)
    vec_in = jnp.pad(vec_in, ((0, 6), (0, 0)))

    every = lax.all_gather(block, ("ctx", "blk"), axis=0)
    weights = every[:, :per].reshape(-1, width)[in_rows:]
    vec = every[:, slots, :entries].reshape(-1, width).astype(F32)
    vec = jnp.pad(vec, ((0, 16 - vec.shape[0]), (0, 0)))

    rows_all, out_grad = lax.optimization_barrier((rows_all, out_grad))
    kept = lax.dynamic_index_in_dim(out_grad, mine, 0, keepdims=False)
    sent = lax.dynamic_index_in_dim(out_grad, 1 - mine, 0, keepdims=False)
    grad = jnp.concatenate([kept, lax.ppermute(sent, "blk", far)], 0)

    own = 2 * local_rows
    ln, qt, kn, kta, vta = prep(rows_all, own, w_input, vec_in)
    att, lse = attend(qt, kn, kta, vta)
    out, gmid, qa, doa, dot_t, late, gvec = between(rows_all, grad, att, lse, qt, weights, vec, blk_size, per)
    layer_grad, layer_out, matrices_grad, vecs = back(
        ctx_size, blk_size, per, owners, qa, doa, qt, dot_t, kta, vta, kn, ln, rows_all, gmid, out, late, gvec, w_input, vec_in
    )
    vectors_grad = lax.dynamic_slice_in_dim(vecs.reshape(-1), flat * entries, entries)
    return layer_out, layer_grad, matrices_grad[:per], vectors_grad


def solution(mesh):
    rows = P("ctx", "blk", None)
    flat = P(("ctx", "blk"))
    return jax.shard_map(
        functools.partial(per_device, mesh.shape["ctx"], mesh.shape["blk"]),
        mesh=mesh,
        in_specs=(rows, flat, flat, rows),
        out_specs=(rows, rows, flat, flat),
        check_vma=False,
    )
```

```python
import functools
import math

import jax
import jax.numpy as jnp
from jax import lax
from jax.experimental import pallas as pl
from jax.experimental.pallas import tpu as pltpu
from jax.sharding import PartitionSpec as P

HEADS = 4
EPSILON = 1e-05
LOG2E = math.log2(math.e)
LN2 = math.log(2.0)
AUG = 80
SAFE_BOUND = 90.0
BF = jnp.bfloat16
F32 = jnp.float32
F8 = jnp.float8_e4m3fn
PIECES = (256.0, 16.0, 1.0, 0.0625)
NT = (((1,), (1,)), ((), ()))
TN = (((0,), (0,)), ((), ()))


def dot(a, b):
    return jnp.dot(a, b, preferred_element_type=F32)


def dot_nt(a, b):
    return lax.dot_general(a, b, NT, preferred_element_type=F32)


def dot_tn(a, b):
    return lax.dot_general(a, b, TN, preferred_element_type=F32)


def params(**kw):
    return pltpu.CompilerParams(vmem_limit_bytes=60 << 20, **kw)


def whole(*shape):
    return pl.BlockSpec(shape, lambda *_: (0,) * len(shape))


def normalize(inputs):
    centre = jnp.mean(inputs, -1, keepdims=True)
    shifted = inputs - centre
    inverse = lax.rsqrt(jnp.mean(shifted * shifted, -1, keepdims=True) + EPSILON)
    return shifted * inverse, inverse


def normalize_back(grad_hat, normed, inverse):
    return inverse * (
        grad_hat
        - jnp.mean(grad_hat, -1, keepdims=True)
        - normed * jnp.mean(grad_hat * normed, -1, keepdims=True)
    )


MESH = pl.DeviceIdType.MESH


def greet(devices):
    barrier = pltpu.get_barrier_semaphore()
    for device in devices:
        pl.semaphore_signal(barrier, inc=1, device_id=device, device_id_type=MESH)
    pl.semaphore_wait(barrier, len(devices))


def partners(blk_size):
    ctx, blk = lax.axis_index("ctx"), lax.axis_index("blk")
    half = blk_size // 2
    return ctx, blk, blk + 1 - 2 * lax.rem(blk, 2), lax.rem(blk + half, blk_size), lax.div(blk, half)


def start_kernel(
    ctx_size, blk_size, per,
    x_hbm, w_hbm, v_ref,
    rows_out, ln_out, qt_out, kn_out, kta_out, vta_out, vec_ref,
    x, ln, qt, kn, kta, vta, w_slots, w_all, wt, wkp, v_own, v_slots,
    x_sem, far_sent, far_got, near_sent, near_got, relay_sent, relay_got, keep_sem,
    w1_sent, w1_got, w2_sent, w2_got, w3_sent, w3_got, v1_sent, v1_got, v2_sent, v2_got, v3_sent, v3_got,
    rows_sem, out_sem,
):
    ctx, blk, near, far, mine = partners(blk_size)
    _, length, width = x_hbm.shape
    head = width // HEADS
    entries = v_ref.shape[1]
    owners = w_slots.shape[0] // blk_size
    chunks = far_sent.shape[0]
    size = length // chunks
    to_near, to_far = (ctx, near), (ctx, far)
    others = [lax.rem(ctx + step, ctx_size) for step in range(1, ctx_size)]

    def remote(source, target, sent, got, device):
        return pltpu.make_async_remote_copy(
            src_ref=source, dst_ref=target, send_sem=sent, recv_sem=got, device_id=device, device_id_type=MESH
        )

    local = pltpu.make_async_copy
    own_rows = local(x_hbm.at[mine], x.at[pl.ds(0, length)], x_sem)
    near_rows = remote(x_hbm.at[mine], x.at[pl.ds(2 * length, length)], near_sent, near_got, to_near)
    far_rows = [
        remote(x_hbm.at[1 - mine, pl.ds(c * size, size)], x.at[pl.ds(length + c * size, size)], far_sent.at[c], far_got.at[c], to_far)
        for c in range(chunks)
    ]
    relay_rows = [
        remote(
            x.at[pl.ds(length + c * size, size)], x.at[pl.ds(3 * length + c * size, size)],
            relay_sent.at[c], relay_got.at[c], to_near,
        )
        for c in range(chunks)
    ]
    groups = ctx_size // owners
    group, place = lax.div(ctx, owners), lax.rem(ctx, owners)
    peers = [lax.rem(place + step, owners) for step in range(1, owners)]
    mine_slot = place * blk_size + blk
    keep_w = local(w_hbm, w_slots.at[mine_slot], keep_sem)
    w_first = [
        remote(w_hbm, w_slots.at[mine_slot], w1_sent.at[g - 1], w1_got, (g * owners + place, blk)) for g in range(1, groups)
    ]
    plane = [(place, far, to_far)]
    for peer in peers:
        plane += [(peer, blk, (group * owners + peer, blk)), (peer, far, (group * owners + peer, far))]
    here = place * 2 + mine
    w_second = [
        remote(w_slots.at[mine_slot], w_slots.at[mine_slot], w2_sent.at[i], w2_got.at[here], device)
        for i, (_, _, device) in enumerate(plane)
    ]
    w_third = [
        remote(w_slots.at[r * blk_size + b], w_slots.at[r * blk_size + b], w3_sent.at[i], w3_got.at[i], to_near)
        for i, (r, b, _) in enumerate([(place, blk, None)] + plane)
    ]
    v_first = [remote(v_own, v_slots.at[blk, ctx], v1_sent.at[i], v1_got.at[ctx], (other, blk)) for i, other in enumerate(others)]
    v_second = remote(v_slots.at[blk], v_slots.at[blk], v2_sent, v2_got, to_far)
    v_third = [remote(v_slots.at[b], v_slots.at[b], v3_sent.at[i], v3_got.at[i], to_near) for i, b in enumerate((blk, far))]
    rows_keep = local(x.at[pl.ds(0, 2 * length)], rows_out, rows_sem)

    greet([to_near, to_far] + [(other, blk) for other in others] + [(group * owners + peer, far) for peer in peers])
    v_own[...] = jnp.zeros_like(v_own)
    v_own[0:1, :entries] = v_ref[...].astype(F32)

    @pl.when(group == 0)
    def _():
        keep_w.start()
        for copy in w_first:
            copy.start()

    early = max(chunks // 2, 1)
    for copy in far_rows[:early]:
        copy.start()
    own_rows.start()
    near_rows.start()
    for copy in v_first:
        copy.start()
    v_slots[blk, ctx] = v_own[...]

    @pl.when(group == 0)
    def _():
        keep_w.wait()

    if groups > 1:
        @pl.when(group > 0)
        def _():
            w_first[0].wait_recv()

    for copy in w_second:
        copy.start()
    w_third[0].start()
    for other in others:
        remote(v_own, v_slots.at[blk, other], v1_sent.at[0], v1_got.at[other], to_far).wait_recv()
    v_second.start()
    v_third[0].start()
    for copy in far_rows[early:]:
        copy.start()
    for i, (r, b, _) in enumerate(plane):
        slot = r * blk_size + b
        remote(w_slots.at[slot], w_slots.at[slot], w2_sent.at[0], w2_got.at[r * 2 + lax.div(b, 2)], to_far).wait_recv()
        w_third[i + 1].start()
    remote(v_slots.at[far], v_slots.at[far], v2_sent, v2_got, to_far).wait_recv()
    v_third[1].start()
    for c in range(early):
        far_rows[c].wait_recv()
        relay_rows[c].start()
    for copy in w_third + v_third:
        copy.wait_recv()

    total = jnp.zeros((16, width), F32)
    place = lax.broadcasted_iota(jnp.int32, (16, width), 0)
    lane = lax.broadcasted_iota(jnp.int32, (16, width), 1)
    for o in range(ctx_size * blk_size):
        row, shift = (o * entries) // width, (o * entries) % width
        piece = jnp.concatenate([v_slots[o % blk_size, o // blk_size], jnp.zeros((8, width - 128), F32)], 1)
        if shift:
            piece = pltpu.roll(piece, shift, 1)
        piece = jnp.broadcast_to(piece[0:1, :], (16, width))
        total = total + jnp.where((place == row) & (lane >= shift), piece, 0.0)
        if shift + entries > width:
            total = total + jnp.where((place == row + 1) & (lane < shift), piece, 0.0)
    vec_ref[...] = total
    for slot in range(w_slots.shape[0]):
        w_all[slot * per : (slot + 1) * per, :] = w_slots[slot, :per, :].astype(F32)
    for index in range(3):
        wt[index * width : (index + 1) * width, :] = w_all[index * width : (index + 1) * width, :].T.astype(BF)
    wk = w_all[width : 2 * width, :]
    for h in range(HEADS):
        wide = jnp.concatenate([wk[:, h * head : (h + 1) * head], jnp.zeros((width, 128 - head), F32)], 1)
        wkp[:, h * 128 : (h + 1) * 128] = wide.astype(BF)
    own_rows.wait()

    block = min(512, length)
    per_quarter = length // block
    extra = (lax.broadcasted_iota(jnp.int32, (AUG - head, block), 0) < 3).astype(F32).astype(BF)

    def out_copies(base, index):
        rows = pl.ds(base, block)
        pairs = ((ln, ln_out), (kn, kn_out), (kta, kta_out), (vta, vta_out))
        copies = []
        for i, (a, b) in enumerate(pairs):
            if i == 0:
                copies.append(local(a.at[rows], b.at[rows], out_sem.at[i, index]))
            elif i == 1:
                copies.append(local(a.at[:, rows], b.at[:, rows], out_sem.at[i, index]))
            else:
                copies.append(local(a.at[:, :, rows], b.at[:, :, rows], out_sem.at[i, index]))
        return copies

    def first_row(index):
        quarter = lax.div(index, per_quarter)
        order = lax.rem(quarter, 2) * 2 + lax.div(quarter, 2)
        return pl.multiple_of(order * length + lax.rem(index, per_quarter) * block, block)

    @pl.loop(0, 4 * per_quarter)
    def _(index):
        quarter = lax.div(index, per_quarter)

        @pl.when(index == per_quarter)
        def _():
            near_rows.wait_recv()

        @pl.when(index == 2 * per_quarter)
        def _():
            for c in range(early, chunks):
                far_rows[c].wait_recv()
                relay_rows[c].start()
            rows_keep.start()

        @pl.when(index == 3 * per_quarter)
        def _():
            for c in range(chunks):
                relay_rows[c].wait_recv()

        base = first_row(index)
        rows = pl.ds(base, block)
        normed, _ = normalize(x[rows, :].astype(F32))
        low = (normed * vec_ref[0:1, :] + vec_ref[1:2, :]).astype(BF)
        ln[rows, :] = low
        kt = dot_nt(wt[width : 2 * width, :], low).astype(BF)
        vt = dot_nt(wt[2 * width : 3 * width, :], low).astype(BF)
        wide = dot(low, wkp[...]).astype(BF)
        for h in range(HEADS):
            kta[h, :head, rows] = kt[h * head : (h + 1) * head, :]
            kta[h, head:, rows] = extra
            vta[h, :head, rows] = vt[h * head : (h + 1) * head, :]
            vta[h, head:, rows] = extra
            kn[h, rows, :] = wide[:, h * 128 : (h + 1) * 128]

        @pl.when(lax.rem(quarter, 2) == 0)
        def _():
            queries = dot_nt(wt[0:width, :], low) * (LOG2E / math.sqrt(head))
            for h in range(HEADS):
                qt[h, :, rows] = queries[h * head : (h + 1) * head, :].astype(BF)

        for copy in out_copies(base, index):
            copy.start()

    qt_copy = local(qt, qt_out, x_sem)
    qt_copy.start()

    @pl.loop(0, 4 * per_quarter)
    def _(index):
        for copy in out_copies(first_row(index), index):
            copy.wait()

    qt_copy.wait()
    rows_keep.wait()

    @pl.when(group == 0)
    def _():
        for copy in w_first:
            copy.wait_send()

    for copy in v_first + [v_second] + v_third + far_rows + relay_rows + [near_rows] + w_second + w_third:
        copy.wait_send()


def start(ctx_size, blk_size, layer_in, matrices, vectors, owners):
    seq_count, length, width = layer_in.shape
    per, entries = matrices.shape[0], vectors.shape[0]
    padded = -(-per // 16) * 16
    if padded > per:
        matrices = jnp.pad(matrices, ((0, padded - per), (0, 0)))
    head = width // HEADS
    own, total = 2 * length, 4 * length
    chunks = 4 if length % 64 == 0 else 1
    blocks = total // min(512, length)
    dma = pltpu.SemaphoreType.DMA
    place = pl.BlockSpec(memory_space=pl.ANY)
    vmem = pl.BlockSpec(memory_space=pltpu.VMEM)
    low = lambda *shape: pltpu.VMEM(shape, BF)
    single = lambda *shape: pltpu.VMEM(shape, F32)
    some = dma((max(ctx_size - 1, 1),))
    shapes = [(own, width), (total, width), (HEADS, head, own), (HEADS, total, 128), (HEADS, AUG, total), (HEADS, AUG, total)]
    return pl.pallas_call(
        functools.partial(start_kernel, ctx_size, blk_size, per),
        in_specs=[place, place, vmem],
        out_specs=[place] * 6 + [vmem],
        out_shape=[jax.ShapeDtypeStruct(shape, BF) for shape in shapes] + [jax.ShapeDtypeStruct((16, width), F32)],
        scratch_shapes=[
            low(total, width), low(total, width), low(HEADS, head, own), low(HEADS, total, 128),
            low(HEADS, AUG, total), low(HEADS, AUG, total),
            low(owners * blk_size, padded, width), single(owners * blk_size * per, width),
            low(3 * width, width), low(width, HEADS * 128), single(8, 128), single(blk_size, ctx_size, 8, 128),
            dma, dma((chunks,)), dma((chunks,)), dma, dma, dma((chunks,)), dma((chunks,)), dma,
            dma((max(ctx_size // owners - 1, 1),)), dma, dma((2 * owners,)), dma((2 * owners,)), dma((2 * owners,)), dma((2 * owners,)),
            some, dma((ctx_size,)), dma, dma, dma((2,)), dma((2,)),
            dma, dma((4, blocks)),
        ],
        compiler_params=params(collective_id=1, has_side_effects=True),
        name="start",
    )(layer_in, matrices, vectors.reshape(1, entries))


def scale_of(values):
    peak = jnp.max(jnp.max(jnp.abs(values), 0, keepdims=True), 1, keepdims=True)
    return jnp.exp2(4.0 - jnp.ceil(jnp.log2(jnp.clip(peak, 1e-30, 1e30))))


def two_parts(values):
    high = values.astype(F8).astype(F32)
    return high, (values - high).astype(F8).astype(F32)


def attend_kernel(qt_ref, kn_ref, kta_ref, vta_ref, att_ref, lse_ref, v8_ref, scale_ref):
    head, own = qt_ref.shape[1:]
    total = kn_ref.shape[1]
    values = vta_ref[0, :head, :].astype(F32)
    scale = scale_of(values)
    scale_ref[0] = jnp.broadcast_to(scale, (8, 128))
    high, low = two_parts(values * scale)
    place = lax.broadcasted_iota(jnp.int32, (head, total), 0)
    ones = jnp.zeros((head, total), F32)
    for index, piece in enumerate(PIECES):
        ones = jnp.where(place == index, piece, ones)
    for index, rows in enumerate((high, high, low, ones)):
        v8_ref[0, index * head : (index + 1) * head, :] = rows.astype(F8)
    tq = min(1024, own)
    tk = min(256, total)
    count = total // tk

    def longest(rows):
        rows = rows.astype(F32)
        return jnp.max(jnp.sum(rows * rows, 0, keepdims=True))

    bound = longest(qt_ref[0]) * longest(kta_ref[0, :head, :])

    def finish(where, summed, top):
        totals = summed[head : head + 1, :]
        att_ref[0, :, where] = summed[:head, :] / totals
        level = jnp.log2(totals)
        lse_ref[0, :, where] = jnp.broadcast_to(level if top is None else level + top, (8, tq))

    def scores(queries, j):
        return dot(kn_ref[0, j * tk : (j + 1) * tk, :head], queries)

    @pl.when(bound <= SAFE_BOUND * SAFE_BOUND)
    def _():
        @pl.loop(0, own // tq)
        def _(i):
            where = pl.ds(pl.multiple_of(i * tq, tq), tq)
            queries = qt_ref[0, :, where]
            summed = jnp.zeros((AUG, tq), F32)
            now = scores(queries, 0)
            for j in range(count):
                expo = jnp.exp2(now).astype(BF)
                if j + 1 < count:
                    now = scores(queries, j + 1)
                summed = summed + dot(vta_ref[0, :, j * tk : (j + 1) * tk], expo)
            finish(where, summed, None)

    @pl.when(jnp.logical_not(bound <= SAFE_BOUND * SAFE_BOUND))
    def _():
        @pl.loop(0, own // tq)
        def _(i):
            where = pl.ds(pl.multiple_of(i * tq, tq), tq)
            queries = qt_ref[0, :, where]

            def absorb(j, carry):
                summed, top = carry
                part = pl.ds(pl.multiple_of(j * tk, tk), tk)
                now = dot(kn_ref[0, part, :head], queries)
                higher = jnp.maximum(top, jnp.max(now, 0, keepdims=True))
                expo = jnp.exp2(now - higher).astype(BF)
                summed = summed * jnp.exp2(top - higher) + dot(vta_ref[0, :, part], expo)
                return summed, higher

            start = (jnp.zeros((AUG, tq), F32), jnp.full((1, tq), -1e30, F32))
            summed, top = lax.fori_loop(0, count, absorb, start)
            finish(where, summed, top)


def attend(qt, kn, kta, vta):
    _, head, own = qt.shape
    total = kn.shape[1]
    per_head = lambda *shape: pl.BlockSpec((1, *shape), lambda h: (h, 0, 0))
    return pl.pallas_call(
        attend_kernel,
        grid=(HEADS,),
        in_specs=[per_head(head, own), per_head(total, 128), per_head(AUG, total), per_head(AUG, total)],
        out_specs=[per_head(head, own), per_head(8, own), per_head(4 * head, total), per_head(8, 128)],
        out_shape=[
            jax.ShapeDtypeStruct((HEADS, head, own), F32),
            jax.ShapeDtypeStruct((HEADS, 8, own), F32),
            jax.ShapeDtypeStruct((HEADS, 4 * head, total), F8),
            jax.ShapeDtypeStruct((HEADS, 8, 128), F32),
        ],
        compiler_params=params(),
        name="attend",
    )(qt, kn, kta, vta)


def gelu_both(value):
    root = math.sqrt(2.0 * math.pi)
    density = jnp.exp2(value * value * (-0.5 * LOG2E) - math.log2(root))
    place = pl.reciprocal((0.3275911 / math.sqrt(2.0)) * jnp.abs(value) + 1.0, approx=True)
    half = 0.5 * root
    series = (1.061405429 * half) * place - 1.453152027 * half
    series = series * place + 1.421413741 * half
    series = series * place - 0.284496736 * half
    series = series * place + 0.254829592 * half
    tail = series * place * density
    below = jnp.where(value >= 0.0, 1.0 - tail, tail)
    return value * below, below + value * density


def split_rows(level, count):
    high = level.astype(BF).astype(F32)
    middle = (level - high).astype(BF).astype(F32)
    low = level - high - middle
    place = lax.broadcasted_iota(jnp.int32, (count, level.shape[1]), 0)
    rows = jnp.where(place == 0, high, jnp.where(place == 1, middle, jnp.where(place == 2, low, 0.0)))
    return rows


def middle_kernel(
    per, mine_ref, x_ref, near_ref, far_ref, att_ref, lse_ref, qt_ref, scale_ref, w_ref, vec_ref,
    out_ref, gmid_ref, qa_ref, do8_ref, dot_ref, qs_ref, unscale_ref, late_ref, gvec_ref, gwo_ref, gup_ref, gdown_ref,
):
    width = x_ref.shape[1]
    head = width // HEADS
    rows = x_ref.shape[0]
    hidden_width = (w_ref.shape[0] - 4 * width) // 2
    wo = w_ref[3 * width : 4 * width, :]
    pieces = hidden_width // width
    down_bias = vec_ref[4 + pieces : 5 + pieces, :]
    gain, bias = vec_ref[2:3, :], vec_ref[3:4, :]

    @pl.when(pl.program_id(0) == 0)
    def _():
        gwo_ref[...] = jnp.zeros_like(gwo_ref)
        gup_ref[...] = jnp.zeros_like(gup_ref)
        gdown_ref[...] = jnp.zeros_like(gdown_ref)
        gvec_ref[...] = jnp.zeros_like(gvec_ref)

    att = att_ref[...].reshape(width, rows)
    att_low = att.astype(BF)
    grad = jnp.where(pl.program_id(0) < pl.num_programs(0) // 2, near_ref[0], far_ref[0])
    gradf = grad.astype(F32)
    grad_t = gradf.T.astype(BF)
    middle = x_ref[...].astype(F32) + dot_tn(att_low, wo)
    normed, inverse = normalize(middle)
    ln_mid = (normed * gain + bias).astype(BF)
    ln_mid_t = ln_mid.astype(F32).T.astype(BF)
    result = middle + down_bias
    grad_ln = jnp.zeros((rows, width), F32)
    for p in range(pieces):
        columns = slice(p * width, (p + 1) * width)
        up = w_ref[(4 + p) * width : (5 + p) * width, :]
        down = w_ref[(4 + pieces + p) * width : (5 + pieces + p) * width, :]
        upper = dot_nt(ln_mid, up) + vec_ref[4 + p : 5 + p, :]
        activated, slope = gelu_both(upper)
        hidden = activated.astype(BF)
        grad_upper = dot_nt(grad, down) * slope
        grad_low = grad_upper.astype(BF)
        result = result + dot(hidden, down)
        grad_ln = grad_ln + dot(grad_low, up)
        gdown_ref[:, columns] += dot(grad_t, hidden)
        gup_ref[:, columns] += dot(ln_mid_t, grad_low)
        gvec_ref[4 + p : 5 + p, :] += jnp.sum(grad_low.astype(F32), 0, keepdims=True)
    out_ref[...] = result.astype(BF)
    gvec_ref[2:3, :] += jnp.sum(grad_ln * normed, 0, keepdims=True)
    gvec_ref[3:4, :] += jnp.sum(grad_ln, 0, keepdims=True)
    gvec_ref[4 + pieces : 5 + pieces, :] += jnp.sum(gradf, 0, keepdims=True)
    grad_mid = gradf + normalize_back(grad_ln * gain, normed, inverse)
    gmid_ref[...] = grad_mid
    branch = grad_mid.astype(BF)
    gwo_ref[...] += dot(att_low, branch)
    grad_att = dot_nt(wo, branch).astype(BF)
    spare = jnp.zeros((128 - AUG, rows), F32)
    place = lax.broadcasted_iota(jnp.int32, (head, rows), 0)
    for h in range(HEADS):
        mine = slice(h * head, (h + 1) * head)
        grad_head = grad_att[mine, :]
        dot_ref[h] = grad_head
        grad_head = grad_head.astype(F32)
        delta = jnp.sum(grad_head * att[mine, :], 0, keepdims=True)
        scale = scale_of(grad_head)
        both = scale * scale_ref[h, 0:1, 0:1]
        high, low = two_parts(grad_head * scale)
        left = -delta * both
        folded = jnp.zeros((head, rows), F32)
        for index, piece in enumerate(PIECES):
            part = (left * (1.0 / piece)).astype(F8).astype(F32)
            left = left - part * piece
            folded = jnp.where(place == index, part, folded)
        do8_ref[h, :, : 2 * head] = jnp.concatenate([high, low], 0).T.astype(F8)
        do8_ref[h, :, 2 * head :] = jnp.concatenate([high, folded], 0).T.astype(F8)
        unscale_ref[0, h * 8 : (h + 1) * 8, :] = jnp.broadcast_to(1.0 / both, (8, 128))
        queries = qt_ref[h].astype(F32)
        qs_ref[h] = (queries / both).astype(BF)
        level = lse_ref[h, 0:1, :]
        wide = jnp.concatenate([queries, split_rows(-level, AUG - head), spare], 0)
        qa_ref[h] = wide.T.astype(BF)

    @pl.when(pl.program_id(0) == pl.num_programs(0) - 1)
    def _():
        grads = jnp.concatenate([gwo_ref[...], gup_ref[...].T, gdown_ref[...].T], 0)
        into_slots(late_ref, grads, per)


def into_slots(slots_ref, grads, per):
    blk_size, owners, padded, width = slots_ref.shape
    filler = jnp.zeros((padded - per, width), F32)
    for slot in range(blk_size * owners):
        piece = grads[slot * per : (slot + 1) * per, :]
        if padded > per:
            piece = jnp.concatenate([piece, filler], 0)
        slots_ref[slot % blk_size, slot // blk_size] = piece.astype(BF)


def between(x, mine, grad_near, grad_far, att, lse, qt, scale, weights, vec, blk_size, per):
    own, width = x.shape
    head = width // HEADS
    hidden_width = (weights.shape[0] - 4 * width) // 2
    block = min(512, own // 2)
    half = own // 2 // block
    rows = lambda i, m: (i, 0)
    lanes = lambda i, m: (0, 0, i)
    tall = lambda i, m: (0, i, 0)
    slots = (blk_size, (weights.shape[0] - 3 * width) // (blk_size * per), -(-per // 16) * 16, width)
    grid_spec = pltpu.PrefetchScalarGridSpec(
        num_scalar_prefetch=1,
        grid=(own // block,),
        in_specs=[
            pl.BlockSpec((block, width), rows),
            pl.BlockSpec((1, block, width), lambda i, m: (m[0], jnp.minimum(i, half - 1), 0)),
            pl.BlockSpec((1, block, width), lambda i, m: (m[0], jnp.maximum(i - half, 0), 0)),
            pl.BlockSpec((HEADS, head, block), lanes),
            pl.BlockSpec((HEADS, 8, block), lanes),
            pl.BlockSpec((HEADS, head, block), lanes),
            whole(*scale.shape),
            whole(*weights.shape),
            whole(*vec.shape),
        ],
        out_specs=[
            pl.BlockSpec((block, width), rows),
            pl.BlockSpec((block, width), rows),
            pl.BlockSpec((HEADS, block, 128), tall),
            pl.BlockSpec((HEADS, block, 4 * head), tall),
            pl.BlockSpec((HEADS, head, block), lanes),
            pl.BlockSpec((HEADS, head, block), lanes),
            pl.BlockSpec((1, HEADS * 8, 128), lambda i, m: (i, 0, 0)),
            whole(*slots),
            whole(16, width),
        ],
        scratch_shapes=[
            pltpu.VMEM((width, width), F32), pltpu.VMEM((width, hidden_width), F32), pltpu.VMEM((width, hidden_width), F32),
        ],
    )
    return pl.pallas_call(
        functools.partial(middle_kernel, per),
        grid_spec=grid_spec,
        out_shape=[
            jax.ShapeDtypeStruct((own, width), BF),
            jax.ShapeDtypeStruct((own, width), F32),
            jax.ShapeDtypeStruct((HEADS, own, 128), BF),
            jax.ShapeDtypeStruct((HEADS, own, 4 * head), F8),
            jax.ShapeDtypeStruct((HEADS, head, own), BF),
            jax.ShapeDtypeStruct((HEADS, head, own), BF),
            jax.ShapeDtypeStruct((own // block, HEADS * 8, 128), F32),
            jax.ShapeDtypeStruct(slots, BF),
            jax.ShapeDtypeStruct((16, width), F32),
        ],
        compiler_params=params(),
        name="between",
    )(mine, x, grad_near, grad_far, att, lse, qt, scale, weights, vec)


def back_kernel(
    ctx_size, blk_size, per,
    qa_hbm, do8_hbm, qs_hbm, dot_hbm, kta_hbm, v8_hbm, kn_hbm, ln_hbm, x_hbm, gmid_hbm, out_hbm, late_hbm,
    unscale_ref, gvec_in, w_ref, vec_ref,
    grad_ref, out_ref, gw_ref, gvec_ref,
    qa, do8, qs, dot_t, kta, v8, kn, ln, x, gmid, made,
    dq_sum, dk_sum, dv_sum, gq, gk, gv, part, part_out, part_in, wqt,
    late_own, late_one, late_pass, late_two, late_sum, late_three,
    early, early_one, early_pass, early_two, early_sum, early_three,
    vec_own, vec_one, vec_pair, vec_two, vec_sum, vec_three,
    head_sem, load_sem, out_sent, out_got, keep_sem, grad_sent, grad_got, part_sent, part_got,
    l1_sent, l1_got, l2_sent, l2_got, l3_sent, l3_got,
    e1_sent, e1_got, e2_sent, e2_got, e3_sent, e3_got,
    v1_sent, v1_got, v2_sent, v2_got, v3_sent, v3_got,
):
    ctx, blk, near, far, mine = partners(blk_size)
    core = lax.rem(blk, 2)
    own, width = x.shape
    length = own // 2
    head = width // HEADS
    owners = early.shape[1]
    groups = ctx_size // owners
    late_count = late_own.shape[1]
    group, place = lax.div(ctx, owners), lax.rem(ctx, owners)
    others = [lax.rem(ctx + step, ctx_size) for step in range(1, ctx_size)]
    peers = [lax.rem(place + step, owners) for step in range(1, owners)]

    def remote(source, target, sent, got, device):
        return pltpu.make_async_remote_copy(
            src_ref=source, dst_ref=target, send_sem=sent, recv_sem=got, device_id=device, device_id_type=MESH
        )

    to_near, to_far = (ctx, near), (ctx, far)
    local = pltpu.make_async_copy

    def head_loads(h):
        pairs = ((qa_hbm, qa), (do8_hbm, do8), (qs_hbm, qs), (dot_hbm, dot_t), (kta_hbm, kta), (v8_hbm, v8), (kn_hbm, kn))
        return [local(a.at[h], b.at[h], head_sem.at[i, h]) for i, (a, b) in enumerate(pairs)]

    loads = [
        local(ln_hbm, ln, load_sem.at[0]),
        local(x_hbm.at[pl.ds(0, own)], x, load_sem.at[1]),
        local(gmid_hbm, gmid, load_sem.at[2]),
    ]
    late_loads = [local(late_hbm.at[2 * y + core], late_own.at[y], load_sem.at[3 + y]) for y in range(2)]
    out_keep = local(out_hbm.at[pl.ds(0, length)], out_ref.at[mine], keep_sem.at[0])
    out_send = remote(out_hbm.at[pl.ds(length, length)], out_ref.at[mine], out_sent, out_got, to_far)

    late_first = [
        remote(late_hbm.at[2 * y + 1 - core], late_one.at[y], l1_sent.at[y], l1_got.at[y], to_near) for y in range(2)
    ]
    late_second = remote(late_pass.at[1 - mine], late_two, l2_sent, l2_got, to_far)

    def late_third(step):
        other = others[step]
        return remote(
            late_sum.at[jnp.maximum(other - owners, 0)], late_three.at[ctx], l3_sent.at[step], l3_got.at[ctx], (other, blk)
        )

    def late_third_from(other):
        return remote(late_sum.at[0], late_three.at[other], l3_sent.at[0], l3_got.at[other], to_near)

    def grad_send(half, c, size):
        return remote(
            made.at[pl.ds(half * length + c * size, size)], grad_ref.at[mine, pl.ds(c * size, size)],
            grad_sent.at[c], grad_got.at[c], to_far,
        )

    def grad_keep(c, size):
        return local(made.at[pl.ds(c * size, size)], grad_ref.at[mine, pl.ds(c * size, size)], keep_sem.at[1 + c])

    def part_send(half):
        return remote(part_out.at[half], part_in.at[half], part_sent.at[half], part_got.at[half], to_near)

    early_first = [
        remote(early.at[2 * y + 1 - core], early_one.at[y], e1_sent.at[y], e1_got.at[y], to_near) for y in range(2)
    ]
    vec_first = remote(vec_own, vec_one, v1_sent, v1_got, to_near)
    here = mine * owners + place
    plane = [(1 - mine, place, to_far)]
    for peer in peers:
        plane.append((mine, peer, (group * owners + peer, blk)))
        plane.append((1 - mine, peer, (group * owners + peer, far)))
    early_second = [
        remote(early_pass.at[y, r], early_two.at[here], e2_sent.at[i], e2_got.at[here], device)
        for i, (y, r, device) in enumerate(plane)
    ]
    vec_second = [
        remote(vec_pair, vec_two.at[here], v2_sent.at[i], v2_got.at[here], device) for i, (y, r, device) in enumerate(plane)
    ]
    plane_slots = [y * owners + r for y, r, _ in plane]
    early_third = remote(early_sum, early_three.at[jnp.maximum(group - 1, 0)], e3_sent, e3_got.at[jnp.maximum(group - 1, 0)], (place, blk))
    other_groups = [lax.rem(group + step, groups) for step in range(1, groups)]
    vec_third = [
        remote(vec_sum, vec_three.at[group], v3_sent.at[i], v3_got.at[group], (other * owners + place, blk))
        for i, other in enumerate(other_groups)
    ]

    greet([to_near, to_far] + [(other, blk) for other in others] + [(group * owners + peer, far) for peer in peers])
    for h in range(HEADS):
        for load in head_loads(h):
            load.start()
    for copy in late_first + late_loads + [out_send, out_keep] + loads:
        copy.start()
    dq_sum[...] = jnp.zeros_like(dq_sum)
    dk_sum[...] = jnp.zeros_like(dk_sum)
    dv_sum[...] = jnp.zeros_like(dv_sum)
    gq[...] = jnp.zeros_like(gq)
    gk[...] = jnp.zeros_like(gk)
    gv[...] = jnp.zeros_like(gv)
    vec_own[...] = gvec_in[...]

    tk = min(256, length)
    wk, wv = w_ref[width : 2 * width, :], w_ref[2 * width : 3 * width, :]
    gain = vec_ref[0:1, :]
    size = min(512, length)
    chunks = length // size

    def terms(half):
        for core_rows in range(2):
            low = core_rows * own + half * length
            rows = slice(low, low + length)
            dk = (dk_sum[:, :, rows] * LN2).astype(BF).reshape(width, length)
            dv = dv_sum[:, :, rows].astype(BF).reshape(width, length)
            gk[...] += dot(dk, ln[rows, :])
            gv[...] += dot(dv, ln[rows, :])
            both = dot(wk, dk) + dot(wv, dv)
            if core_rows == 0:
                part[half] = both
            else:
                part_out[half] = both.astype(BF)
                part_send(half).start()
        for c in range(chunks):
            low = half * length + c * size
            gq[...] += dot_tn(ln[low : low + size, :], query_grads(low))

    def query_grads(low):
        unscale = unscale_ref[low // size] * (1.0 / math.sqrt(head))
        return jnp.concatenate(
            [(dq_sum[h, low : low + size, :] * unscale[h * 8 : h * 8 + 1, :]).astype(BF) for h in range(HEADS)], 1
        )

    def rows_back(half):
        for c in range(chunks):
            rows = slice(half * length + c * size, half * length + (c + 1) * size)
            lanes = slice(c * size, (c + 1) * size)
            grad_ln = dot(query_grads(half * length + c * size), wqt[...]) + (part[half, :, lanes] + part_in[half, :, lanes].astype(F32)).T
            normed, inverse = normalize(x[rows, :].astype(F32))
            vec_own[0:1, :] += jnp.sum(grad_ln * normed, 0, keepdims=True)
            vec_own[1:2, :] += jnp.sum(grad_ln, 0, keepdims=True)
            made[rows, :] = (gmid[rows, :] + normalize_back(grad_ln * gain, normed, inverse)).astype(BF)
            (grad_send(half, c, size) if half else grad_keep(c, size)).start()

    @pl.loop(0, 4 * HEADS)
    def _(t):
        block, h = lax.div(t, HEADS), lax.rem(t, HEADS)

        @pl.when(block == 0)
        def _():
            for load in head_loads(h):
                load.wait()

        @pl.when(t == 2)
        def _():
            for y in range(2):
                late_loads[y].wait()
                late_first[y].wait_recv()
                late_pass[y] = (late_own[y].astype(F32) + late_one[y].astype(F32)).astype(BF)
            late_second.start()

        @pl.when(t == 5)
        def _():
            late_second.wait_recv()
            late_sum[...] = (late_pass[mine].astype(F32) + late_two[...].astype(F32)).astype(BF)
            for step, other in enumerate(others):
                @pl.when(other >= owners)
                def _():
                    late_third(step).start()

        @pl.when(t == 3 * HEADS)
        def _():
            turned = w_ref[:width, :].astype(F32).T
            for head_index in range(HEADS):
                low = head_index * 128
                wqt[low : low + head, :] = turned[head_index * head : (head_index + 1) * head, :].astype(BF)
                wqt[low + head : low + 128, :] = jnp.zeros((128 - head, width), BF)
            for load in loads:
                load.wait()
            terms(1)

        @pl.when(t == 3 * HEADS + 1)
        def _():
            part_send(1).wait_recv()
            rows_back(1)

        first_half = jnp.logical_or(block == 0, block == 3)
        where = pl.ds(pl.multiple_of(jnp.where(first_half, 0, length), length), length)
        base = jnp.where(block < 2, length, 0)
        queries, grads = qa[h, where, :AUG], do8[h, where, :]
        queries_t, grads_t = qs[h, :, where], dot_t[h, :, where]
        parts = []
        for offset in (0, own):
            for low in range(0, length, tk):
                parts.append(pl.ds(pl.multiple_of(base + (offset + low), tk), tk))

        def pair(part):
            return dot(queries, kta[h, :, part]), dot(grads, v8[h, :, part])

        grad_query = jnp.zeros((length, 128), F32)
        level, change = pair(parts[0])
        for j, part_now in enumerate(parts):
            probs = jnp.exp2(level)
            probs_low = probs.astype(BF)
            grad_scores = (probs * change).astype(BF)
            if j + 1 < len(parts):
                level, change = pair(parts[j + 1])
            dv_sum[h, :, part_now] += dot(grads_t, probs_low)
            dk_sum[h, :, part_now] += dot(queries_t, grad_scores)
            grad_query = grad_query + dot(grad_scores, kn[h, part_now, :])
        dq_sum[h, where, :] += grad_query

    terms(0)
    grads = jnp.concatenate([jnp.concatenate([gq[:, h * 128 : h * 128 + head] for h in range(HEADS)], 1), gk[...].T, gv[...].T], 0)
    into_slots(early, grads, per)
    for copy in early_first:
        copy.start()
    part_send(0).wait_recv()
    rows_back(0)
    vec_first.start()
    for y in range(2):
        early_first[y].wait_recv()
        early_pass[y] = (early[2 * y + core].astype(F32) + early_one[y].astype(F32)).astype(BF)
    for copy in early_second:
        copy.start()
    vec_first.wait_recv()
    vec_pair[...] = vec_own[...] + vec_one[...]
    for copy in vec_second:
        copy.start()

    @pl.when(ctx >= owners)
    def _():
        total = late_sum[jnp.maximum(ctx - owners, 0)].astype(F32)
        for other in others:
            late_third_from(other).wait_recv()
            total = total + late_three[other].astype(F32)
        gw_ref[...] = total

    def from_plane(slot, holder, got):
        return remote(holder.at[slot], holder.at[slot], got.at[slot], got.at[slot], to_near)

    total = early_pass[mine, place].astype(F32)
    for slot in plane_slots:
        from_plane(slot, early_two, e2_got).wait_recv()
        total = total + early_two[slot].astype(F32)
    early_sum[...] = total.astype(BF)
    if groups > 1:
        @pl.when(group > 0)
        def _():
            early_third.start()

    vec_total = vec_pair[...]
    for slot in plane_slots:
        from_plane(slot, vec_two, v2_got).wait_recv()
        vec_total = vec_total + vec_two[slot]
    vec_sum[...] = vec_total
    for copy in vec_third:
        copy.start()

    @pl.when(group == 0)
    def _():
        whole_sum = total
        for slot in range(groups - 1):
            from_plane(slot, early_three, e3_got).wait_recv()
            whole_sum = whole_sum + early_three[slot].astype(F32)
        gw_ref[...] = whole_sum

    for other in other_groups:
        from_plane(other, vec_three, v3_got).wait_recv()
        vec_total = vec_total + vec_three[other]
    gvec_ref[...] = vec_total

    for copy in late_first + [late_second, part_send(0), part_send(1), vec_first] + early_first + early_second + vec_second + vec_third:
        copy.wait_send()
    for step, other in enumerate(others):
        @pl.when(other >= owners)
        def _():
            late_third(step).wait_send()

    if groups > 1:
        @pl.when(group > 0)
        def _():
            early_third.wait_send()

    out_keep.wait()
    out_send.wait()
    for c in range(chunks):
        grad_keep(c, size).wait()
        grad_send(1, c, size).wait()


def back(ctx_size, blk_size, per, owners, qa, do8, qs, dot_t, kta, v8, kn, ln, rows_all, gmid, out, late, unscale, gvec, w_input, vec):
    own, width = gmid.shape
    head = width // HEADS
    total = 2 * own
    length = own // 2
    groups = ctx_size // owners
    _, late_count, padded, _ = late.shape
    dma = pltpu.SemaphoreType.DMA
    place = pl.BlockSpec(memory_space=pl.ANY)
    vmem = pl.BlockSpec(memory_space=pltpu.VMEM)
    chunks = length // min(512, length)
    low = lambda *shape: pltpu.VMEM(shape, BF)
    single = lambda *shape: pltpu.VMEM(shape, F32)
    plane = 2 * owners
    some = lambda count: dma((max(count, 1),))
    return pl.pallas_call(
        functools.partial(back_kernel, ctx_size, blk_size, per),
        in_specs=[place] * 12 + [vmem] * 4,
        out_specs=[place, place, vmem, vmem],
        out_shape=[
            jax.ShapeDtypeStruct((2, length, width), BF),
            jax.ShapeDtypeStruct((2, length, width), BF),
            jax.ShapeDtypeStruct((padded, width), F32),
            jax.ShapeDtypeStruct((16, width), F32),
        ],
        scratch_shapes=[
            low(HEADS, own, 128), pltpu.VMEM((HEADS, own, 4 * head), F8), low(HEADS, head, own), low(HEADS, head, own),
            low(HEADS, AUG, total), pltpu.VMEM((HEADS, 4 * head, total), F8), low(HEADS, total, 128), low(total, width),
            low(own, width), single(own, width), low(own, width),
            single(HEADS, own, 128), single(HEADS, head, total), single(HEADS, head, total),
            single(width, HEADS * 128), single(width, width), single(width, width),
            single(2, width, length), low(2, width, length), low(2, width, length), low(HEADS * 128, width),
            low(2, late_count, padded, width), low(2, late_count, padded, width), low(2, late_count, padded, width),
            low(late_count, padded, width), low(late_count, padded, width), low(ctx_size, padded, width),
            low(blk_size, owners, padded, width), low(2, owners, padded, width), low(2, owners, padded, width),
            low(plane, padded, width), low(padded, width), low(max(groups - 1, 1), padded, width),
            single(16, width), single(16, width), single(16, width), single(plane, 16, width), single(16, width),
            single(groups, 16, width),
            dma((7, HEADS)), dma((5,)), dma, dma, dma((1 + chunks,)), dma((chunks,)), dma((chunks,)), dma((2,)), dma((2,)),
            dma((2,)), dma((2,)), dma, dma, some(ctx_size - 1), dma((ctx_size,)),
            dma((2,)), dma((2,)), some(plane - 1), dma((plane,)), dma, some(groups - 1),
            dma, dma, some(plane - 1), dma((plane,)), some(groups - 1), dma((groups,)),
        ],
        compiler_params=params(collective_id=2, has_side_effects=True),
        name="back",
    )(qa, do8, qs, dot_t, kta, v8, kn, ln, rows_all, gmid, out, late, unscale, gvec, w_input, vec)


def per_device(ctx_size, blk_size, layer_in, matrices, vectors, out_grad):
    seq_count, local_rows, width = layer_in.shape
    per, entries = matrices.shape[0], vectors.shape[0]
    flat = lax.axis_index("ctx") * blk_size + lax.axis_index("blk")
    mine = lax.axis_index("blk") // (blk_size // seq_count)
    far = [(b, (b + blk_size // 2) % blk_size) for b in range(blk_size)]
    owners = 3 * width // (per * blk_size)
    weights = lax.all_gather(matrices, ("ctx", "blk"), axis=0, tiled=True)
    rows, ln, qt, kn, kta, vta, vec = start(ctx_size, blk_size, layer_in, matrices, vectors, owners)

    out_grad, qt = lax.optimization_barrier((out_grad, qt))
    grad_far = lax.ppermute(out_grad, "blk", far)
    att, lse, v8, scale = attend(qt, kn, kta, vta)
    out, gmid, qa, do8, dot_t, qs, unscale, late, gvec = between(
        rows, jnp.reshape(mine, (1,)).astype(jnp.int32), out_grad, grad_far, att, lse, qt, scale, weights, vec, blk_size, per
    )
    layer_grad, layer_out, matrices_grad, vecs = back(
        ctx_size, blk_size, per, owners, qa, do8, qs, dot_t, kta, v8, kn, ln, rows, gmid, out, late, unscale, gvec, weights, vec
    )
    vectors_grad = lax.dynamic_slice_in_dim(vecs.reshape(-1), flat * entries, entries)
    return layer_out, layer_grad, matrices_grad[:per], vectors_grad


def solution(mesh):
    rows = P("ctx", "blk", None)
    flat = P(("ctx", "blk"))
    return jax.shard_map(
        functools.partial(per_device, mesh.shape["ctx"], mesh.shape["blk"]),
        mesh=mesh,
        in_specs=(rows, flat, flat, rows),
        out_specs=(rows, rows, flat, flat),
        check_vma=False,
    )
```

```python
import functools
import math

import jax
import jax.numpy as jnp
from jax import lax
from jax.experimental import pallas as pl
from jax.experimental.pallas import tpu as pltpu
from jax.sharding import PartitionSpec as P

HEADS = 4
EPSILON = 1e-05
LOG2E = math.log2(math.e)
LN2 = math.log(2.0)
AUG = 80
SAFE_BOUND = 90.0
BF = jnp.bfloat16
F32 = jnp.float32
NT = (((1,), (1,)), ((), ()))
TN = (((0,), (0,)), ((), ()))


def dot(a, b):
    return jnp.dot(a, b, preferred_element_type=F32)


def dot_nt(a, b):
    return lax.dot_general(a, b, NT, preferred_element_type=F32)


def dot_tn(a, b):
    return lax.dot_general(a, b, TN, preferred_element_type=F32)


def params(**kw):
    return pltpu.CompilerParams(vmem_limit_bytes=60 << 20, **kw)


def whole(*shape):
    return pl.BlockSpec(shape, lambda *_: (0,) * len(shape))


def normalize(inputs):
    centre = jnp.mean(inputs, -1, keepdims=True)
    shifted = inputs - centre
    inverse = lax.rsqrt(jnp.mean(shifted * shifted, -1, keepdims=True) + EPSILON)
    return shifted * inverse, inverse


def normalize_back(grad_hat, normed, inverse):
    return inverse * (
        grad_hat
        - jnp.mean(grad_hat, -1, keepdims=True)
        - normed * jnp.mean(grad_hat * normed, -1, keepdims=True)
    )


MESH = pl.DeviceIdType.MESH


def greet(devices):
    barrier = pltpu.get_barrier_semaphore()
    for device in devices:
        pl.semaphore_signal(barrier, inc=1, device_id=device, device_id_type=MESH)
    pl.semaphore_wait(barrier, len(devices))


def partners(blk_size):
    ctx, blk = lax.axis_index("ctx"), lax.axis_index("blk")
    half = blk_size // 2
    return ctx, blk, blk + 1 - 2 * lax.rem(blk, 2), lax.rem(blk + half, blk_size), lax.div(blk, half)


def start_kernel(
    ctx_size, blk_size, per,
    x_hbm, w_hbm, v_ref,
    rows_out, ln_out, qt_out, kn_out, kta_out, vta_out, vec_ref,
    x, ln, qt, kn, kta, vta, w_slots, w_all, wt, wkp, v_own, v_slots,
    x_sem, far_sent, far_got, near_sent, near_got, relay_sent, relay_got, keep_sem,
    w1_sent, w1_got, w2_sent, w2_got, w3_sent, w3_got, v1_sent, v1_got, v2_sent, v2_got, v3_sent, v3_got,
    rows_sem, out_sem,
):
    ctx, blk, near, far, mine = partners(blk_size)
    _, length, width = x_hbm.shape
    head = width // HEADS
    entries = v_ref.shape[1]
    owners = w_slots.shape[0] // blk_size
    chunks = far_sent.shape[0]
    size = length // chunks
    to_near, to_far = (ctx, near), (ctx, far)
    others = [lax.rem(ctx + step, ctx_size) for step in range(1, ctx_size)]

    def remote(source, target, sent, got, device):
        return pltpu.make_async_remote_copy(
            src_ref=source, dst_ref=target, send_sem=sent, recv_sem=got, device_id=device, device_id_type=MESH
        )

    local = pltpu.make_async_copy
    own_rows = local(x_hbm.at[mine], x.at[pl.ds(0, length)], x_sem)
    near_rows = remote(x_hbm.at[mine], x.at[pl.ds(2 * length, length)], near_sent, near_got, to_near)
    far_rows = [
        remote(x_hbm.at[1 - mine, pl.ds(c * size, size)], x.at[pl.ds(length + c * size, size)], far_sent.at[c], far_got.at[c], to_far)
        for c in range(chunks)
    ]
    relay_rows = [
        remote(
            x.at[pl.ds(length + c * size, size)], x.at[pl.ds(3 * length + c * size, size)],
            relay_sent.at[c], relay_got.at[c], to_near,
        )
        for c in range(chunks)
    ]
    groups = ctx_size // owners
    group, place = lax.div(ctx, owners), lax.rem(ctx, owners)
    peers = [lax.rem(place + step, owners) for step in range(1, owners)]
    mine_slot = place * blk_size + blk
    keep_w = local(w_hbm, w_slots.at[mine_slot], keep_sem)
    w_first = [
        remote(w_hbm, w_slots.at[mine_slot], w1_sent.at[g - 1], w1_got, (g * owners + place, blk)) for g in range(1, groups)
    ]
    plane = [(place, far, to_far)]
    for peer in peers:
        plane += [(peer, blk, (group * owners + peer, blk)), (peer, far, (group * owners + peer, far))]
    here = place * 2 + mine
    w_second = [
        remote(w_slots.at[mine_slot], w_slots.at[mine_slot], w2_sent.at[i], w2_got.at[here], device)
        for i, (_, _, device) in enumerate(plane)
    ]
    w_third = [
        remote(w_slots.at[r * blk_size + b], w_slots.at[r * blk_size + b], w3_sent.at[i], w3_got.at[i], to_near)
        for i, (r, b, _) in enumerate([(place, blk, None)] + plane)
    ]
    v_first = [remote(v_own, v_slots.at[blk, ctx], v1_sent.at[i], v1_got.at[ctx], (other, blk)) for i, other in enumerate(others)]
    v_second = remote(v_slots.at[blk], v_slots.at[blk], v2_sent, v2_got, to_far)
    v_third = [remote(v_slots.at[b], v_slots.at[b], v3_sent.at[i], v3_got.at[i], to_near) for i, b in enumerate((blk, far))]
    rows_keep = local(x.at[pl.ds(0, 2 * length)], rows_out, rows_sem)

    greet([to_near, to_far] + [(other, blk) for other in others] + [(group * owners + peer, far) for peer in peers])
    v_own[...] = jnp.zeros_like(v_own)
    v_own[0:1, :entries] = v_ref[...].astype(F32)

    @pl.when(group == 0)
    def _():
        keep_w.start()
        for copy in w_first:
            copy.start()

    early = max(chunks // 2, 1)
    for copy in far_rows[:early]:
        copy.start()
    own_rows.start()
    near_rows.start()
    for copy in v_first:
        copy.start()
    v_slots[blk, ctx] = v_own[...]

    @pl.when(group == 0)
    def _():
        keep_w.wait()

    if groups > 1:
        @pl.when(group > 0)
        def _():
            w_first[0].wait_recv()

    for copy in w_second:
        copy.start()
    w_third[0].start()
    for other in others:
        remote(v_own, v_slots.at[blk, other], v1_sent.at[0], v1_got.at[other], to_far).wait_recv()
    v_second.start()
    v_third[0].start()
    for copy in far_rows[early:]:
        copy.start()
    for i, (r, b, _) in enumerate(plane):
        slot = r * blk_size + b
        remote(w_slots.at[slot], w_slots.at[slot], w2_sent.at[0], w2_got.at[r * 2 + lax.div(b, 2)], to_far).wait_recv()
        w_third[i + 1].start()
    remote(v_slots.at[far], v_slots.at[far], v2_sent, v2_got, to_far).wait_recv()
    v_third[1].start()
    for c in range(early):
        far_rows[c].wait_recv()
        relay_rows[c].start()
    for copy in w_third + v_third:
        copy.wait_recv()

    total = jnp.zeros((16, width), F32)
    place = lax.broadcasted_iota(jnp.int32, (16, width), 0)
    lane = lax.broadcasted_iota(jnp.int32, (16, width), 1)
    for o in range(ctx_size * blk_size):
        row, shift = (o * entries) // width, (o * entries) % width
        piece = jnp.concatenate([v_slots[o % blk_size, o // blk_size], jnp.zeros((8, width - 128), F32)], 1)
        if shift:
            piece = pltpu.roll(piece, shift, 1)
        piece = jnp.broadcast_to(piece[0:1, :], (16, width))
        total = total + jnp.where((place == row) & (lane >= shift), piece, 0.0)
        if shift + entries > width:
            total = total + jnp.where((place == row + 1) & (lane < shift), piece, 0.0)
    vec_ref[...] = total
    for slot in range(w_slots.shape[0]):
        w_all[slot * per : (slot + 1) * per, :] = w_slots[slot, :per, :].astype(F32)
    for index in range(3):
        wt[index * width : (index + 1) * width, :] = w_all[index * width : (index + 1) * width, :].T.astype(BF)
    wk = w_all[width : 2 * width, :]
    for h in range(HEADS):
        wide = jnp.concatenate([wk[:, h * head : (h + 1) * head], jnp.zeros((width, 128 - head), F32)], 1)
        wkp[:, h * 128 : (h + 1) * 128] = wide.astype(BF)
    own_rows.wait()

    block = min(512, length)
    per_quarter = length // block
    extra = (lax.broadcasted_iota(jnp.int32, (AUG - head, block), 0) < 3).astype(F32).astype(BF)

    def out_copies(base, index):
        rows = pl.ds(base, block)
        pairs = ((ln, ln_out), (kn, kn_out), (kta, kta_out), (vta, vta_out))
        copies = []
        for i, (a, b) in enumerate(pairs):
            if i == 0:
                copies.append(local(a.at[rows], b.at[rows], out_sem.at[i, index]))
            elif i == 1:
                copies.append(local(a.at[:, rows], b.at[:, rows], out_sem.at[i, index]))
            else:
                copies.append(local(a.at[:, :, rows], b.at[:, :, rows], out_sem.at[i, index]))
        return copies

    def first_row(index):
        quarter = lax.div(index, per_quarter)
        order = lax.rem(quarter, 2) * 2 + lax.div(quarter, 2)
        return pl.multiple_of(order * length + lax.rem(index, per_quarter) * block, block)

    @pl.loop(0, 4 * per_quarter)
    def _(index):
        quarter = lax.div(index, per_quarter)

        @pl.when(index == per_quarter)
        def _():
            near_rows.wait_recv()

        @pl.when(index == 2 * per_quarter)
        def _():
            for c in range(early, chunks):
                far_rows[c].wait_recv()
                relay_rows[c].start()
            rows_keep.start()

        @pl.when(index == 3 * per_quarter)
        def _():
            for c in range(chunks):
                relay_rows[c].wait_recv()

        base = first_row(index)
        rows = pl.ds(base, block)
        normed, _ = normalize(x[rows, :].astype(F32))
        low = (normed * vec_ref[0:1, :] + vec_ref[1:2, :]).astype(BF)
        ln[rows, :] = low
        kt = dot_nt(wt[width : 2 * width, :], low).astype(BF)
        vt = dot_nt(wt[2 * width : 3 * width, :], low).astype(BF)
        wide = dot(low, wkp[...]).astype(BF)
        for h in range(HEADS):
            kta[h, :head, rows] = kt[h * head : (h + 1) * head, :]
            kta[h, head:, rows] = extra
            vta[h, :head, rows] = vt[h * head : (h + 1) * head, :]
            vta[h, head:, rows] = extra
            kn[h, rows, :] = wide[:, h * 128 : (h + 1) * 128]

        @pl.when(lax.rem(quarter, 2) == 0)
        def _():
            queries = dot_nt(wt[0:width, :], low)
            for h in range(HEADS):
                qt[h, :, rows] = queries[h * head : (h + 1) * head, :].astype(BF)

        for copy in out_copies(base, index):
            copy.start()

    qt_copy = local(qt, qt_out, x_sem)
    qt_copy.start()

    @pl.loop(0, 4 * per_quarter)
    def _(index):
        for copy in out_copies(first_row(index), index):
            copy.wait()

    qt_copy.wait()
    rows_keep.wait()

    @pl.when(group == 0)
    def _():
        for copy in w_first:
            copy.wait_send()

    for copy in v_first + [v_second] + v_third + far_rows + relay_rows + [near_rows] + w_second + w_third:
        copy.wait_send()


def start(ctx_size, blk_size, layer_in, matrices, vectors, owners):
    seq_count, length, width = layer_in.shape
    per, entries = matrices.shape[0], vectors.shape[0]
    padded = -(-per // 16) * 16
    if padded > per:
        matrices = jnp.pad(matrices, ((0, padded - per), (0, 0)))
    head = width // HEADS
    own, total = 2 * length, 4 * length
    chunks = 4 if length % 64 == 0 else 1
    blocks = total // min(512, length)
    dma = pltpu.SemaphoreType.DMA
    place = pl.BlockSpec(memory_space=pl.ANY)
    vmem = pl.BlockSpec(memory_space=pltpu.VMEM)
    low = lambda *shape: pltpu.VMEM(shape, BF)
    single = lambda *shape: pltpu.VMEM(shape, F32)
    some = dma((max(ctx_size - 1, 1),))
    shapes = [(own, width), (total, width), (HEADS, head, own), (HEADS, total, 128), (HEADS, AUG, total), (HEADS, AUG, total)]
    return pl.pallas_call(
        functools.partial(start_kernel, ctx_size, blk_size, per),
        in_specs=[place, place, vmem],
        out_specs=[place] * 6 + [vmem],
        out_shape=[jax.ShapeDtypeStruct(shape, BF) for shape in shapes] + [jax.ShapeDtypeStruct((16, width), F32)],
        scratch_shapes=[
            low(total, width), low(total, width), low(HEADS, head, own), low(HEADS, total, 128),
            low(HEADS, AUG, total), low(HEADS, AUG, total),
            low(owners * blk_size, padded, width), single(owners * blk_size * per, width),
            low(3 * width, width), low(width, HEADS * 128), single(8, 128), single(blk_size, ctx_size, 8, 128),
            dma, dma((chunks,)), dma((chunks,)), dma, dma, dma((chunks,)), dma((chunks,)), dma,
            dma((max(ctx_size // owners - 1, 1),)), dma, dma((2 * owners,)), dma((2 * owners,)), dma((2 * owners,)), dma((2 * owners,)),
            some, dma((ctx_size,)), dma, dma, dma((2,)), dma((2,)),
            dma, dma((4, blocks)),
        ],
        compiler_params=params(collective_id=1, has_side_effects=True),
        name="start",
    )(layer_in, matrices, vectors.reshape(1, entries))


def attend_kernel(qt_ref, kn_ref, kta_ref, vta_ref, att_ref, lse_ref):
    head, own = qt_ref.shape[1:]
    total = kn_ref.shape[1]
    to_log2 = LOG2E / math.sqrt(head)
    tq = min(1024, own)
    tk = min(256, total)
    count = total // tk

    def longest(rows):
        rows = rows.astype(F32)
        return jnp.max(jnp.sum(rows * rows, 0, keepdims=True))

    bound = longest(qt_ref[0]) * longest(kta_ref[0, :head, :]) * (to_log2 * to_log2)

    def finish(where, summed, top):
        totals = summed[head : head + 1, :]
        att_ref[0, :, where] = summed[:head, :] / totals
        level = jnp.log2(totals)
        lse_ref[0, :, where] = jnp.broadcast_to(level if top is None else level + top, (8, tq))

    def scores(queries, j):
        return dot(kn_ref[0, j * tk : (j + 1) * tk, :head], queries)

    @pl.when(bound <= SAFE_BOUND * SAFE_BOUND)
    def _():
        @pl.loop(0, own // tq)
        def _(i):
            where = pl.ds(pl.multiple_of(i * tq, tq), tq)
            queries = qt_ref[0, :, where]
            summed = jnp.zeros((AUG, tq), F32)
            now = scores(queries, 0)
            for j in range(count):
                expo = jnp.exp2(now * to_log2).astype(BF)
                if j + 1 < count:
                    now = scores(queries, j + 1)
                summed = summed + dot(vta_ref[0, :, j * tk : (j + 1) * tk], expo)
            finish(where, summed, None)

    @pl.when(jnp.logical_not(bound <= SAFE_BOUND * SAFE_BOUND))
    def _():
        @pl.loop(0, own // tq)
        def _(i):
            where = pl.ds(pl.multiple_of(i * tq, tq), tq)
            queries = qt_ref[0, :, where]

            def absorb(j, carry):
                summed, top = carry
                part = pl.ds(pl.multiple_of(j * tk, tk), tk)
                now = dot(kn_ref[0, part, :head], queries) * to_log2
                higher = jnp.maximum(top, jnp.max(now, 0, keepdims=True))
                expo = jnp.exp2(now - higher).astype(BF)
                summed = summed * jnp.exp2(top - higher) + dot(vta_ref[0, :, part], expo)
                return summed, higher

            start = (jnp.zeros((AUG, tq), F32), jnp.full((1, tq), -1e30, F32))
            summed, top = lax.fori_loop(0, count, absorb, start)
            finish(where, summed, top)


def attend(qt, kn, kta, vta):
    _, head, own = qt.shape
    total = kn.shape[1]
    per_head = lambda *shape: pl.BlockSpec((1, *shape), lambda h: (h, 0, 0))
    return pl.pallas_call(
        attend_kernel,
        grid=(HEADS,),
        in_specs=[per_head(head, own), per_head(total, 128), per_head(AUG, total), per_head(AUG, total)],
        out_specs=[per_head(head, own), per_head(8, own)],
        out_shape=[
            jax.ShapeDtypeStruct((HEADS, head, own), F32),
            jax.ShapeDtypeStruct((HEADS, 8, own), F32),
        ],
        compiler_params=params(),
        name="attend",
    )(qt, kn, kta, vta)


def gelu_both(value):
    below = 0.5 + 0.5 * lax.erf(value * math.sqrt(0.5))
    density = jnp.exp2(value * value * (-0.5 * LOG2E) - math.log2(math.sqrt(2.0 * math.pi)))
    return value * below, below + value * density


def split_rows(level, count):
    high = level.astype(BF).astype(F32)
    middle = (level - high).astype(BF).astype(F32)
    low = level - high - middle
    place = lax.broadcasted_iota(jnp.int32, (count, level.shape[1]), 0)
    rows = jnp.where(place == 0, high, jnp.where(place == 1, middle, jnp.where(place == 2, low, 0.0)))
    return rows


def middle_kernel(
    per, mine_ref, x_ref, near_ref, far_ref, att_ref, lse_ref, qt_ref, w_ref, vec_ref,
    out_ref, gmid_ref, qa_ref, doa_ref, dot_ref, late_ref, gvec_ref, gwo_ref, gup_ref, gdown_ref,
):
    width = x_ref.shape[1]
    head = width // HEADS
    rows = x_ref.shape[0]
    hidden_width = (w_ref.shape[0] - 4 * width) // 2
    wo = w_ref[3 * width : 4 * width, :]
    pieces = hidden_width // width
    down_bias = vec_ref[4 + pieces : 5 + pieces, :]
    gain, bias = vec_ref[2:3, :], vec_ref[3:4, :]

    @pl.when(pl.program_id(0) == 0)
    def _():
        gwo_ref[...] = jnp.zeros_like(gwo_ref)
        gup_ref[...] = jnp.zeros_like(gup_ref)
        gdown_ref[...] = jnp.zeros_like(gdown_ref)
        gvec_ref[...] = jnp.zeros_like(gvec_ref)

    att = att_ref[...].reshape(width, rows)
    att_low = att.astype(BF)
    grad = jnp.where(pl.program_id(0) < pl.num_programs(0) // 2, near_ref[0], far_ref[0])
    gradf = grad.astype(F32)
    grad_t = gradf.T.astype(BF)
    middle = x_ref[...].astype(F32) + dot_tn(att_low, wo)
    normed, inverse = normalize(middle)
    ln_mid = (normed * gain + bias).astype(BF)
    ln_mid_t = ln_mid.astype(F32).T.astype(BF)
    result = middle + down_bias
    grad_ln = jnp.zeros((rows, width), F32)
    for p in range(pieces):
        columns = slice(p * width, (p + 1) * width)
        up = w_ref[(4 + p) * width : (5 + p) * width, :]
        down = w_ref[(4 + pieces + p) * width : (5 + pieces + p) * width, :]
        upper = dot_nt(ln_mid, up) + vec_ref[4 + p : 5 + p, :]
        activated, slope = gelu_both(upper)
        hidden = activated.astype(BF)
        grad_upper = dot_nt(grad, down) * slope
        grad_low = grad_upper.astype(BF)
        result = result + dot(hidden, down)
        grad_ln = grad_ln + dot(grad_low, up)
        gdown_ref[:, columns] += dot(grad_t, hidden)
        gup_ref[:, columns] += dot(ln_mid_t, grad_low)
        gvec_ref[4 + p : 5 + p, :] += jnp.sum(grad_low.astype(F32), 0, keepdims=True)
    out_ref[...] = result.astype(BF)
    gvec_ref[2:3, :] += jnp.sum(grad_ln * normed, 0, keepdims=True)
    gvec_ref[3:4, :] += jnp.sum(grad_ln, 0, keepdims=True)
    gvec_ref[4 + pieces : 5 + pieces, :] += jnp.sum(gradf, 0, keepdims=True)
    grad_mid = gradf + normalize_back(grad_ln * gain, normed, inverse)
    gmid_ref[...] = grad_mid
    branch = grad_mid.astype(BF)
    gwo_ref[...] += dot(att_low, branch)
    grad_att = dot_nt(wo, branch).astype(BF)
    spare = jnp.zeros((128 - AUG, rows), F32)
    from_log2 = math.sqrt(head) * LN2
    for h in range(HEADS):
        mine = slice(h * head, (h + 1) * head)
        grad_head = grad_att[mine, :]
        dot_ref[h] = grad_head
        grad_head = grad_head.astype(F32)
        delta = jnp.sum(grad_head * att[mine, :], 0, keepdims=True)
        wide = jnp.concatenate([grad_head, split_rows(-delta, AUG - head), spare], 0)
        doa_ref[h] = wide.T.astype(BF)
        level = lse_ref[h, 0:1, :] * from_log2
        wide = jnp.concatenate([qt_ref[h].astype(F32), split_rows(-level, AUG - head), spare], 0)
        qa_ref[h] = wide.T.astype(BF)

    @pl.when(pl.program_id(0) == pl.num_programs(0) - 1)
    def _():
        grads = jnp.concatenate([gwo_ref[...], gup_ref[...].T, gdown_ref[...].T], 0)
        into_slots(late_ref, grads, per)


def into_slots(slots_ref, grads, per):
    blk_size, owners, padded, width = slots_ref.shape
    filler = jnp.zeros((padded - per, width), F32)
    for slot in range(blk_size * owners):
        piece = grads[slot * per : (slot + 1) * per, :]
        if padded > per:
            piece = jnp.concatenate([piece, filler], 0)
        slots_ref[slot % blk_size, slot // blk_size] = piece.astype(BF)


def between(x, mine, grad_near, grad_far, att, lse, qt, weights, vec, blk_size, per):
    own, width = x.shape
    head = width // HEADS
    hidden_width = (weights.shape[0] - 4 * width) // 2
    block = min(512, own // 2)
    half = own // 2 // block
    rows = lambda i, m: (i, 0)
    lanes = lambda i, m: (0, 0, i)
    tall = lambda i, m: (0, i, 0)
    slots = (blk_size, (weights.shape[0] - 3 * width) // (blk_size * per), -(-per // 16) * 16, width)
    grid_spec = pltpu.PrefetchScalarGridSpec(
        num_scalar_prefetch=1,
        grid=(own // block,),
        in_specs=[
            pl.BlockSpec((block, width), rows),
            pl.BlockSpec((1, block, width), lambda i, m: (m[0], jnp.minimum(i, half - 1), 0)),
            pl.BlockSpec((1, block, width), lambda i, m: (m[0], jnp.maximum(i - half, 0), 0)),
            pl.BlockSpec((HEADS, head, block), lanes),
            pl.BlockSpec((HEADS, 8, block), lanes),
            pl.BlockSpec((HEADS, head, block), lanes),
            whole(*weights.shape),
            whole(*vec.shape),
        ],
        out_specs=[
            pl.BlockSpec((block, width), rows),
            pl.BlockSpec((block, width), rows),
            pl.BlockSpec((HEADS, block, 128), tall),
            pl.BlockSpec((HEADS, block, 128), tall),
            pl.BlockSpec((HEADS, head, block), lanes),
            whole(*slots),
            whole(16, width),
        ],
        scratch_shapes=[
            pltpu.VMEM((width, width), F32), pltpu.VMEM((width, hidden_width), F32), pltpu.VMEM((width, hidden_width), F32),
        ],
    )
    return pl.pallas_call(
        functools.partial(middle_kernel, per),
        grid_spec=grid_spec,
        out_shape=[
            jax.ShapeDtypeStruct((own, width), BF),
            jax.ShapeDtypeStruct((own, width), F32),
            jax.ShapeDtypeStruct((HEADS, own, 128), BF),
            jax.ShapeDtypeStruct((HEADS, own, 128), BF),
            jax.ShapeDtypeStruct((HEADS, head, own), BF),
            jax.ShapeDtypeStruct(slots, BF),
            jax.ShapeDtypeStruct((16, width), F32),
        ],
        compiler_params=params(),
        name="between",
    )(mine, x, grad_near, grad_far, att, lse, qt, weights, vec)


def back_kernel(
    ctx_size, blk_size, per,
    qa_hbm, doa_hbm, qt_hbm, dot_hbm, kta_hbm, vta_hbm, kn_hbm, ln_hbm, x_hbm, gmid_hbm, out_hbm, late_hbm,
    gvec_in, w_ref, vec_ref,
    grad_ref, out_ref, gw_ref, gvec_ref,
    qa, doa, qt, dot_t, kta, vta, kn, ln, x, gmid, made,
    dq_sum, dk_sum, dv_sum, gq, gk, gv, part, part_out, part_in, wqt,
    late_own, late_one, late_pass, late_two, late_sum, late_three,
    early, early_one, early_pass, early_two, early_sum, early_three,
    vec_own, vec_one, vec_pair, vec_two, vec_sum, vec_three,
    head_sem, load_sem, out_sent, out_got, keep_sem, grad_sent, grad_got, part_sent, part_got,
    l1_sent, l1_got, l2_sent, l2_got, l3_sent, l3_got,
    e1_sent, e1_got, e2_sent, e2_got, e3_sent, e3_got,
    v1_sent, v1_got, v2_sent, v2_got, v3_sent, v3_got,
):
    ctx, blk, near, far, mine = partners(blk_size)
    core = lax.rem(blk, 2)
    own, width = x.shape
    length = own // 2
    head = width // HEADS
    owners = early.shape[1]
    groups = ctx_size // owners
    late_count = late_own.shape[1]
    group, place = lax.div(ctx, owners), lax.rem(ctx, owners)
    others = [lax.rem(ctx + step, ctx_size) for step in range(1, ctx_size)]
    peers = [lax.rem(place + step, owners) for step in range(1, owners)]

    def remote(source, target, sent, got, device):
        return pltpu.make_async_remote_copy(
            src_ref=source, dst_ref=target, send_sem=sent, recv_sem=got, device_id=device, device_id_type=MESH
        )

    to_near, to_far = (ctx, near), (ctx, far)
    local = pltpu.make_async_copy

    def head_loads(h):
        pairs = ((qa_hbm, qa), (doa_hbm, doa), (qt_hbm, qt), (dot_hbm, dot_t), (kta_hbm, kta), (vta_hbm, vta), (kn_hbm, kn))
        return [local(a.at[h], b.at[h], head_sem.at[i, h]) for i, (a, b) in enumerate(pairs)]

    loads = [
        local(ln_hbm, ln, load_sem.at[0]),
        local(x_hbm.at[pl.ds(0, own)], x, load_sem.at[1]),
        local(gmid_hbm, gmid, load_sem.at[2]),
    ]
    late_loads = [local(late_hbm.at[2 * y + core], late_own.at[y], load_sem.at[3 + y]) for y in range(2)]
    out_keep = local(out_hbm.at[pl.ds(0, length)], out_ref.at[mine], keep_sem.at[0])
    out_send = remote(out_hbm.at[pl.ds(length, length)], out_ref.at[mine], out_sent, out_got, to_far)

    late_first = [
        remote(late_hbm.at[2 * y + 1 - core], late_one.at[y], l1_sent.at[y], l1_got.at[y], to_near) for y in range(2)
    ]
    late_second = remote(late_pass.at[1 - mine], late_two, l2_sent, l2_got, to_far)

    def late_third(step):
        other = others[step]
        return remote(
            late_sum.at[jnp.maximum(other - owners, 0)], late_three.at[ctx], l3_sent.at[step], l3_got.at[ctx], (other, blk)
        )

    def late_third_from(other):
        return remote(late_sum.at[0], late_three.at[other], l3_sent.at[0], l3_got.at[other], to_near)

    def grad_send(half, c, size):
        return remote(
            made.at[pl.ds(half * length + c * size, size)], grad_ref.at[mine, pl.ds(c * size, size)],
            grad_sent.at[c], grad_got.at[c], to_far,
        )

    def grad_keep(c, size):
        return local(made.at[pl.ds(c * size, size)], grad_ref.at[mine, pl.ds(c * size, size)], keep_sem.at[1 + c])

    def part_send(half):
        return remote(part_out.at[half], part_in.at[half], part_sent.at[half], part_got.at[half], to_near)

    early_first = [
        remote(early.at[2 * y + 1 - core], early_one.at[y], e1_sent.at[y], e1_got.at[y], to_near) for y in range(2)
    ]
    vec_first = remote(vec_own, vec_one, v1_sent, v1_got, to_near)
    here = mine * owners + place
    plane = [(1 - mine, place, to_far)]
    for peer in peers:
        plane.append((mine, peer, (group * owners + peer, blk)))
        plane.append((1 - mine, peer, (group * owners + peer, far)))
    early_second = [
        remote(early_pass.at[y, r], early_two.at[here], e2_sent.at[i], e2_got.at[here], device)
        for i, (y, r, device) in enumerate(plane)
    ]
    vec_second = [
        remote(vec_pair, vec_two.at[here], v2_sent.at[i], v2_got.at[here], device) for i, (y, r, device) in enumerate(plane)
    ]
    plane_slots = [y * owners + r for y, r, _ in plane]
    early_third = remote(early_sum, early_three.at[jnp.maximum(group - 1, 0)], e3_sent, e3_got.at[jnp.maximum(group - 1, 0)], (place, blk))
    other_groups = [lax.rem(group + step, groups) for step in range(1, groups)]
    vec_third = [
        remote(vec_sum, vec_three.at[group], v3_sent.at[i], v3_got.at[group], (other * owners + place, blk))
        for i, other in enumerate(other_groups)
    ]

    greet([to_near, to_far] + [(other, blk) for other in others] + [(group * owners + peer, far) for peer in peers])
    for load in head_loads(0):
        load.start()
    for copy in late_first + late_loads + [out_send, out_keep] + loads:
        copy.start()
    dq_sum[...] = jnp.zeros_like(dq_sum)
    dk_sum[...] = jnp.zeros_like(dk_sum)
    dv_sum[...] = jnp.zeros_like(dv_sum)
    gq[...] = jnp.zeros_like(gq)
    gk[...] = jnp.zeros_like(gk)
    gv[...] = jnp.zeros_like(gv)
    vec_own[...] = gvec_in[...]

    tk = min(256, length)
    inverse_root = 1.0 / math.sqrt(head)
    wk, wv = w_ref[width : 2 * width, :], w_ref[2 * width : 3 * width, :]
    gain = vec_ref[0:1, :]
    size = min(512, length)
    chunks = length // size

    def terms(half):
        for core_rows in (1, 0):
            low = core_rows * own + half * length
            rows = slice(low, low + length)
            dk = (dk_sum[:, :, rows] * inverse_root).astype(BF).reshape(width, length)
            dv = dv_sum[:, :, rows].astype(BF).reshape(width, length)
            both = dot(wk, dk) + dot(wv, dv)
            if core_rows:
                part_out[half] = both.astype(BF)
                part_send(half).start()
            else:
                part[half] = both
            gk[...] += dot(dk, ln[rows, :])
            gv[...] += dot(dv, ln[rows, :])
        for c in range(chunks):
            low = half * length + c * size
            gq[...] += dot_tn(ln[low : low + size, :], query_grads(low))

    def query_grads(low):
        return jnp.concatenate([(dq_sum[h, low : low + size, :] * inverse_root).astype(BF) for h in range(HEADS)], 1)

    def rows_back(half):
        for c in range(chunks):
            rows = slice(half * length + c * size, half * length + (c + 1) * size)
            lanes = slice(c * size, (c + 1) * size)
            grad_ln = dot(query_grads(half * length + c * size), wqt[...]) + (part[half, :, lanes] + part_in[half, :, lanes].astype(F32)).T
            normed, inverse = normalize(x[rows, :].astype(F32))
            vec_own[0:1, :] += jnp.sum(grad_ln * normed, 0, keepdims=True)
            vec_own[1:2, :] += jnp.sum(grad_ln, 0, keepdims=True)
            made[rows, :] = (gmid[rows, :] + normalize_back(grad_ln * gain, normed, inverse)).astype(BF)
            (grad_send(half, c, size) if half else grad_keep(c, size)).start()

    @pl.loop(0, 4 * HEADS)
    def _(t):
        block, h = lax.div(t, HEADS), lax.rem(t, HEADS)

        @pl.when(block == 0)
        def _():
            for load in head_loads(h):
                load.wait()

        @pl.when(t < HEADS - 1)
        def _():
            for load in head_loads(t + 1):
                load.start()

        @pl.when(t == 2)
        def _():
            for y in range(2):
                late_loads[y].wait()
                late_first[y].wait_recv()
                late_pass[y] = (late_own[y].astype(F32) + late_one[y].astype(F32)).astype(BF)
            late_second.start()

        @pl.when(t == 5)
        def _():
            late_second.wait_recv()
            late_sum[...] = (late_pass[mine].astype(F32) + late_two[...].astype(F32)).astype(BF)
            for step, other in enumerate(others):
                @pl.when(other >= owners)
                def _():
                    late_third(step).start()

        @pl.when(t == 3 * HEADS)
        def _():
            turned = w_ref[:width, :].astype(F32).T
            for head_index in range(HEADS):
                low = head_index * 128
                wqt[low : low + head, :] = turned[head_index * head : (head_index + 1) * head, :].astype(BF)
                wqt[low + head : low + 128, :] = jnp.zeros((128 - head, width), BF)
            for load in loads:
                load.wait()
            terms(1)

        @pl.when(t == 3 * HEADS + 1)
        def _():
            part_send(1).wait_recv()
            rows_back(1)

        first_half = jnp.logical_or(block == 0, block == 3)
        where = pl.ds(pl.multiple_of(jnp.where(first_half, 0, length), length), length)
        base = jnp.where(block < 2, length, 0)
        queries, grads = qa[h, where, :AUG], doa[h, where, :AUG]
        queries_t, grads_t = qt[h, :, where], dot_t[h, :, where]
        parts = []
        for offset in (0, own):
            for low in range(0, length, tk):
                parts.append(pl.ds(pl.multiple_of(base + (offset + low), tk), tk))

        def pair(part):
            return dot(queries, kta[h, :, part]), dot(grads, vta[h, :, part])

        grad_query = jnp.zeros((length, 128), F32)
        level, change = pair(parts[0])
        for j, part_now in enumerate(parts):
            probs = jnp.exp2(level * (LOG2E * inverse_root))
            probs_low = probs.astype(BF)
            grad_scores = (probs * change).astype(BF)
            if j + 1 < len(parts):
                level, change = pair(parts[j + 1])
            dv_sum[h, :, part_now] += dot(grads_t, probs_low)
            dk_sum[h, :, part_now] += dot(queries_t, grad_scores)
            grad_query = grad_query + dot(grad_scores, kn[h, part_now, :])
        dq_sum[h, where, :] += grad_query

    terms(0)
    grads = jnp.concatenate([jnp.concatenate([gq[:, h * 128 : h * 128 + head] for h in range(HEADS)], 1), gk[...].T, gv[...].T], 0)
    into_slots(early, grads, per)
    for copy in early_first:
        copy.start()
    part_send(0).wait_recv()
    rows_back(0)
    vec_first.start()
    for y in range(2):
        early_first[y].wait_recv()
        early_pass[y] = (early[2 * y + core].astype(F32) + early_one[y].astype(F32)).astype(BF)
    for copy in early_second:
        copy.start()
    vec_first.wait_recv()
    vec_pair[...] = vec_own[...] + vec_one[...]
    for copy in vec_second:
        copy.start()

    @pl.when(ctx >= owners)
    def _():
        total = late_sum[jnp.maximum(ctx - owners, 0)].astype(F32)
        for other in others:
            late_third_from(other).wait_recv()
            total = total + late_three[other].astype(F32)
        gw_ref[...] = total

    def from_plane(slot, holder, got):
        return remote(holder.at[slot], holder.at[slot], got.at[slot], got.at[slot], to_near)

    total = early_pass[mine, place].astype(F32)
    for slot in plane_slots:
        from_plane(slot, early_two, e2_got).wait_recv()
        total = total + early_two[slot].astype(F32)
    early_sum[...] = total.astype(BF)
    if groups > 1:
        @pl.when(group > 0)
        def _():
            early_third.start()

    vec_total = vec_pair[...]
    for slot in plane_slots:
        from_plane(slot, vec_two, v2_got).wait_recv()
        vec_total = vec_total + vec_two[slot]
    vec_sum[...] = vec_total
    for copy in vec_third:
        copy.start()

    @pl.when(group == 0)
    def _():
        whole_sum = total
        for slot in range(groups - 1):
            from_plane(slot, early_three, e3_got).wait_recv()
            whole_sum = whole_sum + early_three[slot].astype(F32)
        gw_ref[...] = whole_sum

    for other in other_groups:
        from_plane(other, vec_three, v3_got).wait_recv()
        vec_total = vec_total + vec_three[other]
    gvec_ref[...] = vec_total

    for copy in late_first + [late_second, part_send(0), part_send(1), vec_first] + early_first + early_second + vec_second + vec_third:
        copy.wait_send()
    for step, other in enumerate(others):
        @pl.when(other >= owners)
        def _():
            late_third(step).wait_send()

    if groups > 1:
        @pl.when(group > 0)
        def _():
            early_third.wait_send()

    out_keep.wait()
    out_send.wait()
    for c in range(chunks):
        grad_keep(c, size).wait()
        grad_send(1, c, size).wait()


def back(ctx_size, blk_size, per, owners, qa, doa, qt, dot_t, kta, vta, kn, ln, rows_all, gmid, out, late, gvec, w_input, vec):
    own, width = gmid.shape
    head = width // HEADS
    total = 2 * own
    length = own // 2
    groups = ctx_size // owners
    _, late_count, padded, _ = late.shape
    dma = pltpu.SemaphoreType.DMA
    place = pl.BlockSpec(memory_space=pl.ANY)
    vmem = pl.BlockSpec(memory_space=pltpu.VMEM)
    chunks = length // min(512, length)
    low = lambda *shape: pltpu.VMEM(shape, BF)
    single = lambda *shape: pltpu.VMEM(shape, F32)
    plane = 2 * owners
    some = lambda count: dma((max(count, 1),))
    return pl.pallas_call(
        functools.partial(back_kernel, ctx_size, blk_size, per),
        in_specs=[place] * 12 + [vmem] * 3,
        out_specs=[place, place, vmem, vmem],
        out_shape=[
            jax.ShapeDtypeStruct((2, length, width), BF),
            jax.ShapeDtypeStruct((2, length, width), BF),
            jax.ShapeDtypeStruct((padded, width), F32),
            jax.ShapeDtypeStruct((16, width), F32),
        ],
        scratch_shapes=[
            low(HEADS, own, 128), low(HEADS, own, 128), low(HEADS, head, own), low(HEADS, head, own),
            low(HEADS, AUG, total), low(HEADS, AUG, total), low(HEADS, total, 128), low(total, width),
            low(own, width), single(own, width), low(own, width),
            single(HEADS, own, 128), single(HEADS, head, total), single(HEADS, head, total),
            single(width, HEADS * 128), single(width, width), single(width, width),
            single(2, width, length), low(2, width, length), low(2, width, length), low(HEADS * 128, width),
            low(2, late_count, padded, width), low(2, late_count, padded, width), low(2, late_count, padded, width),
            low(late_count, padded, width), low(late_count, padded, width), low(ctx_size, padded, width),
            low(blk_size, owners, padded, width), low(2, owners, padded, width), low(2, owners, padded, width),
            low(plane, padded, width), low(padded, width), low(max(groups - 1, 1), padded, width),
            single(16, width), single(16, width), single(16, width), single(plane, 16, width), single(16, width),
            single(groups, 16, width),
            dma((7, HEADS)), dma((5,)), dma, dma, dma((1 + chunks,)), dma((chunks,)), dma((chunks,)), dma((2,)), dma((2,)),
            dma((2,)), dma((2,)), dma, dma, some(ctx_size - 1), dma((ctx_size,)),
            dma((2,)), dma((2,)), some(plane - 1), dma((plane,)), dma, some(groups - 1),
            dma, dma, some(plane - 1), dma((plane,)), some(groups - 1), dma((groups,)),
        ],
        compiler_params=params(collective_id=2, has_side_effects=True),
        name="back",
    )(qa, doa, qt, dot_t, kta, vta, kn, ln, rows_all, gmid, out, late, gvec, w_input, vec)


def per_device(ctx_size, blk_size, layer_in, matrices, vectors, out_grad):
    seq_count, local_rows, width = layer_in.shape
    per, entries = matrices.shape[0], vectors.shape[0]
    flat = lax.axis_index("ctx") * blk_size + lax.axis_index("blk")
    mine = lax.axis_index("blk") // (blk_size // seq_count)
    far = [(b, (b + blk_size // 2) % blk_size) for b in range(blk_size)]
    owners = 3 * width // (per * blk_size)
    weights = lax.all_gather(matrices, ("ctx", "blk"), axis=0, tiled=True)
    rows, ln, qt, kn, kta, vta, vec = start(ctx_size, blk_size, layer_in, matrices, vectors, owners)

    out_grad, qt = lax.optimization_barrier((out_grad, qt))
    grad_far = lax.ppermute(out_grad, "blk", far)
    att, lse = attend(qt, kn, kta, vta)
    out, gmid, qa, doa, dot_t, late, gvec = between(
        rows, jnp.reshape(mine, (1,)).astype(jnp.int32), out_grad, grad_far, att, lse, qt, weights, vec, blk_size, per
    )
    layer_grad, layer_out, matrices_grad, vecs = back(
        ctx_size, blk_size, per, owners, qa, doa, qt, dot_t, kta, vta, kn, ln, rows, gmid, out, late, gvec, weights, vec
    )
    vectors_grad = lax.dynamic_slice_in_dim(vecs.reshape(-1), flat * entries, entries)
    return layer_out, layer_grad, matrices_grad[:per], vectors_grad


def solution(mesh):
    rows = P("ctx", "blk", None)
    flat = P(("ctx", "blk"))
    return jax.shard_map(
        functools.partial(per_device, mesh.shape["ctx"], mesh.shape["blk"]),
        mesh=mesh,
        in_specs=(rows, flat, flat, rows),
        out_specs=(rows, rows, flat, flat),
        check_vma=False,
    )
```

```python
import functools
import math

import jax
import jax.numpy as jnp
from jax import lax
from jax.experimental import pallas as pl
from jax.experimental.pallas import tpu as pltpu
from jax.sharding import PartitionSpec as P

HEADS = 4
EPSILON = 1e-05
LOG2E = math.log2(math.e)
LN2 = math.log(2.0)
AUG = 80
SAFE_BOUND = 90.0
BF = jnp.bfloat16
F32 = jnp.float32
NT = (((1,), (1,)), ((), ()))
TN = (((0,), (0,)), ((), ()))


def dot(a, b):
    return jnp.dot(a, b, preferred_element_type=F32)


def dot_nt(a, b):
    return lax.dot_general(a, b, NT, preferred_element_type=F32)


def dot_tn(a, b):
    return lax.dot_general(a, b, TN, preferred_element_type=F32)


def params(**kw):
    return pltpu.CompilerParams(vmem_limit_bytes=60 << 20, **kw)


def whole(*shape):
    return pl.BlockSpec(shape, lambda *_: (0,) * len(shape))


def normalize(inputs):
    centre = jnp.mean(inputs, -1, keepdims=True)
    shifted = inputs - centre
    inverse = lax.rsqrt(jnp.mean(shifted * shifted, -1, keepdims=True) + EPSILON)
    return shifted * inverse, inverse


def normalize_back(grad_hat, normed, inverse):
    return inverse * (
        grad_hat
        - jnp.mean(grad_hat, -1, keepdims=True)
        - normed * jnp.mean(grad_hat * normed, -1, keepdims=True)
    )


MESH = pl.DeviceIdType.MESH


def greet(devices):
    barrier = pltpu.get_barrier_semaphore()
    for device in devices:
        pl.semaphore_signal(barrier, inc=1, device_id=device, device_id_type=MESH)
    pl.semaphore_wait(barrier, len(devices))


def partners(blk_size):
    ctx, blk = lax.axis_index("ctx"), lax.axis_index("blk")
    half = blk_size // 2
    return ctx, blk, blk + 1 - 2 * lax.rem(blk, 2), lax.rem(blk + half, blk_size), lax.div(blk, half)


def start_kernel(
    ctx_size, blk_size, per,
    x_hbm, w_hbm, v_ref,
    rows_out, ln_out, qt_out, kn_out, kta_out, vta_out, vec_ref,
    x, norms, ln, qt, kn, kta, vta, w_slots, w_all, wt, wkp, v_own, v_slots,
    x_sem, far_sent, far_got, near_sent, near_got, relay_sent, relay_got, keep_sem,
    w1_sent, w1_got, w2_sent, w2_got, w3_sent, w3_got, v1_sent, v1_got, v2_sent, v2_got, v3_sent, v3_got,
    rows_sem, out_sem,
):
    ctx, blk, near, far, mine = partners(blk_size)
    _, length, width = x_hbm.shape
    head = width // HEADS
    entries = v_ref.shape[1]
    owners = w_slots.shape[0] // blk_size
    chunks = far_sent.shape[0]
    size = length // chunks
    to_near, to_far = (ctx, near), (ctx, far)
    others = [lax.rem(ctx + step, ctx_size) for step in range(1, ctx_size)]

    def remote(source, target, sent, got, device):
        return pltpu.make_async_remote_copy(
            src_ref=source, dst_ref=target, send_sem=sent, recv_sem=got, device_id=device, device_id_type=MESH
        )

    local = pltpu.make_async_copy
    own_rows = local(x_hbm.at[mine], x.at[pl.ds(0, length)], x_sem)
    near_rows = remote(x_hbm.at[mine], x.at[pl.ds(2 * length, length)], near_sent, near_got, to_near)
    far_rows = [
        remote(x_hbm.at[1 - mine, pl.ds(c * size, size)], x.at[pl.ds(length + c * size, size)], far_sent.at[c], far_got.at[c], to_far)
        for c in range(chunks)
    ]
    relay_rows = [
        remote(
            x.at[pl.ds(length + c * size, size)], x.at[pl.ds(3 * length + c * size, size)],
            relay_sent.at[c], relay_got.at[c], to_near,
        )
        for c in range(chunks)
    ]
    groups = ctx_size // owners
    group, place = lax.div(ctx, owners), lax.rem(ctx, owners)
    peers = [lax.rem(place + step, owners) for step in range(1, owners)]
    mine_slot = place * blk_size + blk
    keep_w = local(w_hbm, w_slots.at[mine_slot], keep_sem)
    w_first = [
        remote(w_hbm, w_slots.at[mine_slot], w1_sent.at[g - 1], w1_got, (g * owners + place, blk)) for g in range(1, groups)
    ]
    plane = [(place, far, to_far)]
    for peer in peers:
        plane += [(peer, blk, (group * owners + peer, blk)), (peer, far, (group * owners + peer, far))]
    here = place * 2 + mine
    w_second = [
        remote(w_slots.at[mine_slot], w_slots.at[mine_slot], w2_sent.at[i], w2_got.at[here], device)
        for i, (_, _, device) in enumerate(plane)
    ]
    w_third = [
        remote(w_slots.at[r * blk_size + b], w_slots.at[r * blk_size + b], w3_sent.at[i], w3_got.at[i], to_near)
        for i, (r, b, _) in enumerate([(place, blk, None)] + plane)
    ]
    v_first = [remote(v_own, v_slots.at[blk, ctx], v1_sent.at[i], v1_got.at[ctx], (other, blk)) for i, other in enumerate(others)]
    v_second = remote(v_slots.at[blk], v_slots.at[blk], v2_sent, v2_got, to_far)
    v_third = [remote(v_slots.at[b], v_slots.at[b], v3_sent.at[i], v3_got.at[i], to_near) for i, b in enumerate((blk, far))]
    rows_keep = local(x.at[pl.ds(0, 2 * length)], rows_out, rows_sem)

    greet([to_near, to_far] + [(other, blk) for other in others] + [(group * owners + peer, far) for peer in peers])
    v_own[...] = jnp.zeros_like(v_own)
    v_own[0:1, :entries] = v_ref[...].astype(F32)

    @pl.when(group == 0)
    def _():
        keep_w.start()
        for copy in w_first:
            copy.start()

    early = max(chunks // 2, 1)
    for copy in far_rows[:early]:
        copy.start()
    own_rows.start()
    near_rows.start()
    for copy in v_first:
        copy.start()
    v_slots[blk, ctx] = v_own[...]
    block = min(512, length)

    def norm(low):
        normed, _ = normalize(x[pl.ds(low, block), :].astype(F32))
        norms[pl.ds(low, block), :] = normed

    own_rows.wait()
    for low in range(0, length, block):
        norm(low)

    @pl.when(group == 0)
    def _():
        keep_w.wait()

    if groups > 1:
        @pl.when(group > 0)
        def _():
            w_first[0].wait_recv()

    for copy in w_second:
        copy.start()
    w_third[0].start()
    for other in others:
        remote(v_own, v_slots.at[blk, other], v1_sent.at[0], v1_got.at[other], to_far).wait_recv()
    v_second.start()
    v_third[0].start()
    for copy in far_rows[early:]:
        copy.start()
    for i, (r, b, _) in enumerate(plane):
        slot = r * blk_size + b
        remote(w_slots.at[slot], w_slots.at[slot], w2_sent.at[0], w2_got.at[r * 2 + lax.div(b, 2)], to_far).wait_recv()
        w_third[i + 1].start()
    remote(v_slots.at[far], v_slots.at[far], v2_sent, v2_got, to_far).wait_recv()
    v_third[1].start()
    for c in range(early):
        far_rows[c].wait_recv()
        relay_rows[c].start()
    near_rows.wait_recv()
    for low in range(2 * length, 3 * length, block):
        norm(low)
    for copy in w_third + v_third:
        copy.wait_recv()

    total = jnp.zeros((16, width), F32)
    place = lax.broadcasted_iota(jnp.int32, (16, width), 0)
    lane = lax.broadcasted_iota(jnp.int32, (16, width), 1)
    for o in range(ctx_size * blk_size):
        row, shift = (o * entries) // width, (o * entries) % width
        piece = jnp.concatenate([v_slots[o % blk_size, o // blk_size], jnp.zeros((8, width - 128), F32)], 1)
        if shift:
            piece = pltpu.roll(piece, shift, 1)
        piece = jnp.broadcast_to(piece[0:1, :], (16, width))
        total = total + jnp.where((place == row) & (lane >= shift), piece, 0.0)
        if shift + entries > width:
            total = total + jnp.where((place == row + 1) & (lane < shift), piece, 0.0)
    vec_ref[...] = total
    for slot in range(w_slots.shape[0]):
        w_all[slot * per : (slot + 1) * per, :] = w_slots[slot, :per, :].astype(F32)
    for index in range(3):
        wt[index * width : (index + 1) * width, :] = w_all[index * width : (index + 1) * width, :].T.astype(BF)
    wk = w_all[width : 2 * width, :]
    for h in range(HEADS):
        wide = jnp.concatenate([wk[:, h * head : (h + 1) * head], jnp.zeros((width, 128 - head), F32)], 1)
        wkp[:, h * 128 : (h + 1) * 128] = wide.astype(BF)
    per_quarter = length // block
    extra = (lax.broadcasted_iota(jnp.int32, (AUG - head, block), 0) < 3).astype(F32).astype(BF)

    def out_copies(base, index):
        rows = pl.ds(base, block)
        pairs = ((ln, ln_out), (kn, kn_out), (kta, kta_out), (vta, vta_out))
        copies = []
        for i, (a, b) in enumerate(pairs):
            if i == 0:
                copies.append(local(a.at[rows], b.at[rows], out_sem.at[i, index]))
            elif i == 1:
                copies.append(local(a.at[:, rows], b.at[:, rows], out_sem.at[i, index]))
            else:
                copies.append(local(a.at[:, :, rows], b.at[:, :, rows], out_sem.at[i, index]))
        return copies

    def first_row(index):
        quarter = lax.div(index, per_quarter)
        order = lax.rem(quarter, 2) * 2 + lax.div(quarter, 2)
        return pl.multiple_of(order * length + lax.rem(index, per_quarter) * block, block)

    @pl.loop(0, 4 * per_quarter)
    def _(index):
        quarter = lax.div(index, per_quarter)

        @pl.when(index == 2 * per_quarter)
        def _():
            for c in range(early, chunks):
                far_rows[c].wait_recv()
                relay_rows[c].start()
            rows_keep.start()

        @pl.when(index == 3 * per_quarter)
        def _():
            for c in range(chunks):
                relay_rows[c].wait_recv()

        base = first_row(index)
        rows = pl.ds(base, block)

        @pl.when(quarter >= 2)
        def _():
            norm(base)

        low = (norms[rows, :] * vec_ref[0:1, :] + vec_ref[1:2, :]).astype(BF)
        ln[rows, :] = low
        kt = dot_nt(wt[width : 2 * width, :], low).astype(BF)
        vt = dot_nt(wt[2 * width : 3 * width, :], low).astype(BF)
        wide = dot(low, wkp[...]).astype(BF)
        for h in range(HEADS):
            kta[h, :head, rows] = kt[h * head : (h + 1) * head, :]
            kta[h, head:, rows] = extra
            vta[h, :head, rows] = vt[h * head : (h + 1) * head, :]
            vta[h, head:, rows] = extra
            kn[h, rows, :] = wide[:, h * 128 : (h + 1) * 128]

        @pl.when(lax.rem(quarter, 2) == 0)
        def _():
            queries = dot_nt(wt[0:width, :], low)
            for h in range(HEADS):
                qt[h, :, rows] = queries[h * head : (h + 1) * head, :].astype(BF)

        for copy in out_copies(base, index):
            copy.start()

    qt_copy = local(qt, qt_out, x_sem)
    qt_copy.start()

    @pl.loop(0, 4 * per_quarter)
    def _(index):
        for copy in out_copies(first_row(index), index):
            copy.wait()

    qt_copy.wait()
    rows_keep.wait()

    @pl.when(group == 0)
    def _():
        for copy in w_first:
            copy.wait_send()

    for copy in v_first + [v_second] + v_third + far_rows + relay_rows + [near_rows] + w_second + w_third:
        copy.wait_send()


def start(ctx_size, blk_size, layer_in, matrices, vectors, owners):
    seq_count, length, width = layer_in.shape
    per, entries = matrices.shape[0], vectors.shape[0]
    padded = -(-per // 16) * 16
    if padded > per:
        matrices = jnp.pad(matrices, ((0, padded - per), (0, 0)))
    head = width // HEADS
    own, total = 2 * length, 4 * length
    chunks = 4 if length % 64 == 0 else 1
    blocks = total // min(512, length)
    dma = pltpu.SemaphoreType.DMA
    place = pl.BlockSpec(memory_space=pl.ANY)
    vmem = pl.BlockSpec(memory_space=pltpu.VMEM)
    low = lambda *shape: pltpu.VMEM(shape, BF)
    single = lambda *shape: pltpu.VMEM(shape, F32)
    some = dma((max(ctx_size - 1, 1),))
    shapes = [(own, width), (total, width), (HEADS, head, own), (HEADS, total, 128), (HEADS, AUG, total), (HEADS, AUG, total)]
    return pl.pallas_call(
        functools.partial(start_kernel, ctx_size, blk_size, per),
        in_specs=[place, place, vmem],
        out_specs=[place] * 6 + [vmem],
        out_shape=[jax.ShapeDtypeStruct(shape, BF) for shape in shapes] + [jax.ShapeDtypeStruct((16, width), F32)],
        scratch_shapes=[
            low(total, width), single(total, width), low(total, width), low(HEADS, head, own), low(HEADS, total, 128),
            low(HEADS, AUG, total), low(HEADS, AUG, total),
            low(owners * blk_size, padded, width), single(owners * blk_size * per, width),
            low(3 * width, width), low(width, HEADS * 128), single(8, 128), single(blk_size, ctx_size, 8, 128),
            dma, dma((chunks,)), dma((chunks,)), dma, dma, dma((chunks,)), dma((chunks,)), dma,
            dma((max(ctx_size // owners - 1, 1),)), dma, dma((2 * owners,)), dma((2 * owners,)), dma((2 * owners,)), dma((2 * owners,)),
            some, dma((ctx_size,)), dma, dma, dma((2,)), dma((2,)),
            dma, dma((4, blocks)),
        ],
        compiler_params=params(collective_id=1, has_side_effects=True),
        name="start",
    )(layer_in, matrices, vectors.reshape(1, entries))


def attend_kernel(qt_ref, kn_ref, kta_ref, vta_ref, att_ref, lse_ref):
    head, own = qt_ref.shape[1:]
    total = kn_ref.shape[1]
    to_log2 = LOG2E / math.sqrt(head)
    tq = min(1024, own)
    tk = min(256, total)
    count = total // tk

    def longest(rows):
        rows = rows.astype(F32)
        return jnp.max(jnp.sum(rows * rows, 0, keepdims=True))

    bound = longest(qt_ref[0]) * longest(kta_ref[0, :head, :]) * (to_log2 * to_log2)

    def finish(where, summed, top):
        totals = summed[head : head + 1, :]
        att_ref[0, :, where] = summed[:head, :] / totals
        level = jnp.log2(totals)
        lse_ref[0, :, where] = jnp.broadcast_to(level if top is None else level + top, (8, tq))

    def scores(queries, j):
        return dot(kn_ref[0, j * tk : (j + 1) * tk, :head], queries)

    @pl.when(bound <= SAFE_BOUND * SAFE_BOUND)
    def _():
        @pl.loop(0, own // tq)
        def _(i):
            where = pl.ds(pl.multiple_of(i * tq, tq), tq)
            queries = qt_ref[0, :, where]
            summed = jnp.zeros((AUG, tq), F32)
            now = scores(queries, 0)
            for j in range(count):
                expo = jnp.exp2(now * to_log2).astype(BF)
                if j + 1 < count:
                    now = scores(queries, j + 1)
                summed = summed + dot(vta_ref[0, :, j * tk : (j + 1) * tk], expo)
            finish(where, summed, None)

    @pl.when(jnp.logical_not(bound <= SAFE_BOUND * SAFE_BOUND))
    def _():
        @pl.loop(0, own // tq)
        def _(i):
            where = pl.ds(pl.multiple_of(i * tq, tq), tq)
            queries = qt_ref[0, :, where]

            def absorb(j, carry):
                summed, top = carry
                part = pl.ds(pl.multiple_of(j * tk, tk), tk)
                now = dot(kn_ref[0, part, :head], queries) * to_log2
                higher = jnp.maximum(top, jnp.max(now, 0, keepdims=True))
                expo = jnp.exp2(now - higher).astype(BF)
                summed = summed * jnp.exp2(top - higher) + dot(vta_ref[0, :, part], expo)
                return summed, higher

            start = (jnp.zeros((AUG, tq), F32), jnp.full((1, tq), -1e30, F32))
            summed, top = lax.fori_loop(0, count, absorb, start)
            finish(where, summed, top)


def attend(qt, kn, kta, vta):
    _, head, own = qt.shape
    total = kn.shape[1]
    per_head = lambda *shape: pl.BlockSpec((1, *shape), lambda h: (h, 0, 0))
    return pl.pallas_call(
        attend_kernel,
        grid=(HEADS,),
        in_specs=[per_head(head, own), per_head(total, 128), per_head(AUG, total), per_head(AUG, total)],
        out_specs=[per_head(head, own), per_head(8, own)],
        out_shape=[
            jax.ShapeDtypeStruct((HEADS, head, own), F32),
            jax.ShapeDtypeStruct((HEADS, 8, own), F32),
        ],
        compiler_params=params(),
        name="attend",
    )(qt, kn, kta, vta)


def gelu_both(value):
    below = 0.5 + 0.5 * lax.erf(value * math.sqrt(0.5))
    density = jnp.exp2(value * value * (-0.5 * LOG2E) - math.log2(math.sqrt(2.0 * math.pi)))
    return value * below, below + value * density


def split_rows(level, count):
    high = level.astype(BF).astype(F32)
    middle = (level - high).astype(BF).astype(F32)
    low = level - high - middle
    place = lax.broadcasted_iota(jnp.int32, (count, level.shape[1]), 0)
    rows = jnp.where(place == 0, high, jnp.where(place == 1, middle, jnp.where(place == 2, low, 0.0)))
    return rows


def into_slots(slots_ref, grads, per):
    blk_size, owners, padded, width = slots_ref.shape
    filler = jnp.zeros((padded - per, width), F32)
    for slot in range(blk_size * owners):
        piece = grads[slot * per : (slot + 1) * per, :]
        if padded > per:
            piece = jnp.concatenate([piece, filler], 0)
        slots_ref[slot % blk_size, slot // blk_size] = piece.astype(BF)


def back_kernel(
    ctx_size, blk_size, per, entries,
    att_hbm, lse_hbm, qt_hbm, kta_hbm, vta_hbm, kn_hbm, ln_hbm, x_hbm, near_hbm, far_hbm, w_hbm,
    vec_ref,
    grad_ref, out_ref, gw_ref, gvec_ref,
    w_ref, att, lse, cotangent, gwo, gup, gdown, late,
    qa, doa, qt, dot_t, kta, vta, kn, ln, x, gmid, made,
    dq_sum, dk_sum, dv_sum, gq, gk, gv, part, part_out, part_in, wqt,
    late_one, late_pass, late_two, late_sum, late_three,
    early, early_one, early_pass, early_two, early_sum, early_three,
    vec_own, vec_one, vec_pair, vec_two, vec_sum, vec_three,
    head_sem, load_sem, out_sent, out_got, keep_sem, grad_sent, grad_got, part_sent, part_got,
    l1_sent, l1_got, l2_sent, l2_got, l3_sent, l3_got,
    e1_sent, e1_got, e2_sent, e2_got, e3_sent, e3_got,
    v1_sent, v1_got, v2_sent, v2_got, v3_sent, v3_got,
):
    ctx, blk, near, far, mine = partners(blk_size)
    core = lax.rem(blk, 2)
    own, width = x.shape
    length = own // 2
    head = width // HEADS
    owners = early.shape[1]
    groups = ctx_size // owners
    group, place = lax.div(ctx, owners), lax.rem(ctx, owners)
    others = [lax.rem(ctx + step, ctx_size) for step in range(1, ctx_size)]
    peers = [lax.rem(place + step, owners) for step in range(1, owners)]

    def remote(source, target, sent, got, device):
        return pltpu.make_async_remote_copy(
            src_ref=source, dst_ref=target, send_sem=sent, recv_sem=got, device_id=device, device_id_type=MESH
        )

    to_near, to_far = (ctx, near), (ctx, far)
    local = pltpu.make_async_copy

    def head_loads(h):
        pairs = ((kta_hbm, kta), (vta_hbm, vta), (kn_hbm, kn))
        return [local(a.at[h], b.at[h], head_sem.at[i, h]) for i, (a, b) in enumerate(pairs)]

    middle_loads = [
        local(w_hbm, w_ref, load_sem.at[7]),
        local(att_hbm, att, load_sem.at[0]),
        local(x_hbm, x, load_sem.at[1]),
        local(near_hbm.at[mine], cotangent.at[pl.ds(0, length)], load_sem.at[2]),
        local(far_hbm.at[mine], cotangent.at[pl.ds(length, length)], load_sem.at[3]),
        local(lse_hbm, lse, load_sem.at[4]),
        local(qt_hbm, qt, load_sem.at[5]),
    ]
    ln_load = local(ln_hbm, ln, load_sem.at[6])
    out_keep = local(made.at[pl.ds(0, length)], out_ref.at[mine], keep_sem.at[0])
    out_send = remote(made.at[pl.ds(length, length)], out_ref.at[mine], out_sent, out_got, to_far)

    late_first = [
        remote(late.at[2 * y + 1 - core], late_one.at[y], l1_sent.at[y], l1_got.at[y], to_near) for y in range(2)
    ]
    late_second = remote(late_pass.at[1 - mine], late_two, l2_sent, l2_got, to_far)

    def late_third(step):
        other = others[step]
        return remote(
            late_sum.at[jnp.maximum(other - owners, 0)], late_three.at[ctx], l3_sent.at[step], l3_got.at[ctx], (other, blk)
        )

    def late_third_from(other):
        return remote(late_sum.at[0], late_three.at[other], l3_sent.at[0], l3_got.at[other], to_near)

    def grad_send(half, c, size):
        return remote(
            made.at[pl.ds(half * length + c * size, size)], grad_ref.at[mine, pl.ds(c * size, size)],
            grad_sent.at[c], grad_got.at[c], to_far,
        )

    def grad_keep(c, size):
        return local(made.at[pl.ds(c * size, size)], grad_ref.at[mine, pl.ds(c * size, size)], keep_sem.at[1 + c])

    def part_send(half):
        return remote(part_out.at[half], part_in.at[half], part_sent.at[half], part_got.at[half], to_near)

    early_first = [
        remote(early.at[2 * y + 1 - core], early_one.at[y], e1_sent.at[y], e1_got.at[y], to_near) for y in range(2)
    ]
    vec_first = remote(vec_own, vec_one, v1_sent, v1_got, to_near)
    here = mine * owners + place
    plane = [(1 - mine, place, to_far)]
    for peer in peers:
        plane.append((mine, peer, (group * owners + peer, blk)))
        plane.append((1 - mine, peer, (group * owners + peer, far)))
    early_second = [
        remote(early_pass.at[y, r], early_two.at[here], e2_sent.at[i], e2_got.at[here], device)
        for i, (y, r, device) in enumerate(plane)
    ]
    vec_second = [
        remote(vec_pair, vec_two.at[here], v2_sent.at[i], v2_got.at[here], device) for i, (y, r, device) in enumerate(plane)
    ]
    plane_slots = [y * owners + r for y, r, _ in plane]
    early_third = remote(early_sum, early_three.at[jnp.maximum(group - 1, 0)], e3_sent, e3_got.at[jnp.maximum(group - 1, 0)], (place, blk))
    other_groups = [lax.rem(group + step, groups) for step in range(1, groups)]
    vec_third = [
        remote(vec_sum, vec_three.at[group], v3_sent.at[i], v3_got.at[group], (other * owners + place, blk))
        for i, other in enumerate(other_groups)
    ]

    for load in middle_loads + head_loads(0):
        load.start()
    greet([to_near, to_far] + [(other, blk) for other in others] + [(group * owners + peer, far) for peer in peers])
    for ref in (gwo, gup, gdown, vec_own, gq, gk, gv, dq_sum, dk_sum, dv_sum):
        ref[...] = jnp.zeros_like(ref)
    for load in middle_loads:
        load.wait()
    ln_load.start()

    gain_mid, bias_mid = vec_ref[2:3, :], vec_ref[3:4, :]
    wo = w_ref[3 * width : 4 * width, :]
    pieces = (w_ref.shape[0] - 4 * width) // (2 * width)
    down_bias = vec_ref[4 + pieces : 5 + pieces, :]
    from_log2 = math.sqrt(head) * LN2
    count = min(512, length)

    @pl.loop(0, own // count)
    def _(index):
        rows = pl.ds(pl.multiple_of(index * count, count), count)
        attended = att[:, :, rows].reshape(width, count)
        att_low = attended.astype(BF)
        grad = cotangent[rows, :]
        gradf = grad.astype(F32)
        grad_t = gradf.T.astype(BF)
        middle = x[rows, :].astype(F32) + dot_tn(att_low, wo)
        normed, inverse = normalize(middle)
        ln_mid = (normed * gain_mid + bias_mid).astype(BF)
        ln_mid_t = ln_mid.astype(F32).T.astype(BF)
        result = middle + down_bias
        grad_ln = jnp.zeros((count, width), F32)
        for p in range(pieces):
            columns = slice(p * width, (p + 1) * width)
            up = w_ref[(4 + p) * width : (5 + p) * width, :]
            down = w_ref[(4 + pieces + p) * width : (5 + pieces + p) * width, :]
            upper = dot_nt(ln_mid, up) + vec_ref[4 + p : 5 + p, :]
            activated, slope = gelu_both(upper)
            hidden = activated.astype(BF)
            grad_low = (dot_nt(grad, down) * slope).astype(BF)
            result = result + dot(hidden, down)
            grad_ln = grad_ln + dot(grad_low, up)
            gdown[:, columns] += dot(grad_t, hidden)
            gup[:, columns] += dot(ln_mid_t, grad_low)
            vec_own[4 + p : 5 + p, :] += jnp.sum(grad_low.astype(F32), 0, keepdims=True)
        made[rows, :] = result.astype(BF)
        vec_own[2:3, :] += jnp.sum(grad_ln * normed, 0, keepdims=True)
        vec_own[3:4, :] += jnp.sum(grad_ln, 0, keepdims=True)
        vec_own[4 + pieces : 5 + pieces, :] += jnp.sum(gradf, 0, keepdims=True)
        grad_mid = gradf + normalize_back(grad_ln * gain_mid, normed, inverse)
        gmid[rows, :] = grad_mid
        branch = grad_mid.astype(BF)
        gwo[...] += dot(att_low, branch)
        grad_att = dot_nt(wo, branch).astype(BF)
        spare = jnp.zeros((128 - AUG, count), F32)
        for h in range(HEADS):
            part_of = slice(h * head, (h + 1) * head)
            grad_head = grad_att[part_of, :]
            dot_t[h, :, rows] = grad_head
            grad_head = grad_head.astype(F32)
            delta = jnp.sum(grad_head * attended[part_of, :], 0, keepdims=True)
            wide = jnp.concatenate([grad_head, split_rows(-delta, AUG - head), spare], 0)
            doa[h, rows, :] = wide.T.astype(BF)
            level = lse[h, 0:1, rows] * from_log2
            wide = jnp.concatenate([qt[h, :, rows].astype(F32), split_rows(-level, AUG - head), spare], 0)
            qa[h, rows, :] = wide.T.astype(BF)

    out_send.start()
    out_keep.start()
    into_slots(late, jnp.concatenate([gwo[...], gup[...].T, gdown[...].T], 0), per)
    for copy in late_first:
        copy.start()

    tk = min(256, length)
    inverse_root = 1.0 / math.sqrt(head)
    wk, wv = w_ref[width : 2 * width, :], w_ref[2 * width : 3 * width, :]
    gain = vec_ref[0:1, :]
    size = min(512, length)
    chunks = length // size

    def terms(half):
        for core_rows in (1, 0):
            low = core_rows * own + half * length
            rows = slice(low, low + length)
            dk = (dk_sum[:, :, rows] * inverse_root).astype(BF).reshape(width, length)
            dv = dv_sum[:, :, rows].astype(BF).reshape(width, length)
            both = dot(wk, dk) + dot(wv, dv)
            if core_rows:
                part_out[half] = both.astype(BF)
                part_send(half).start()
            else:
                part[half] = both
            gk[...] += dot(dk, ln[rows, :])
            gv[...] += dot(dv, ln[rows, :])
        for c in range(chunks):
            low = half * length + c * size
            gq[...] += dot_tn(ln[low : low + size, :], query_grads(low))

    def query_grads(low):
        return jnp.concatenate([(dq_sum[h, low : low + size, :] * inverse_root).astype(BF) for h in range(HEADS)], 1)

    def rows_back(half):
        for c in range(chunks):
            rows = slice(half * length + c * size, half * length + (c + 1) * size)
            lanes = slice(c * size, (c + 1) * size)
            grad_ln = dot(query_grads(half * length + c * size), wqt[...]) + (part[half, :, lanes] + part_in[half, :, lanes].astype(F32)).T
            normed, inverse = normalize(x[rows, :].astype(F32))
            vec_own[0:1, :] += jnp.sum(grad_ln * normed, 0, keepdims=True)
            vec_own[1:2, :] += jnp.sum(grad_ln, 0, keepdims=True)
            made[rows, :] = (gmid[rows, :] + normalize_back(grad_ln * gain, normed, inverse)).astype(BF)
            (grad_send(half, c, size) if half else grad_keep(c, size)).start()

    @pl.loop(0, 4 * HEADS)
    def _(t):
        block, h = lax.div(t, HEADS), lax.rem(t, HEADS)

        @pl.when(block == 0)
        def _():
            for load in head_loads(h):
                load.wait()

        @pl.when(t < HEADS - 1)
        def _():
            for load in head_loads(t + 1):
                load.start()

        @pl.when(t == 2)
        def _():
            for y in range(2):
                late_first[y].wait_recv()
                late_pass[y] = (late[2 * y + core].astype(F32) + late_one[y].astype(F32)).astype(BF)
            late_second.start()

        @pl.when(t == 5)
        def _():
            late_second.wait_recv()
            late_sum[...] = (late_pass[mine].astype(F32) + late_two[...].astype(F32)).astype(BF)
            for step, other in enumerate(others):
                @pl.when(other >= owners)
                def _():
                    late_third(step).start()

        @pl.when(t == 3 * HEADS)
        def _():
            turned = w_ref[:width, :].astype(F32).T
            for head_index in range(HEADS):
                low = head_index * 128
                wqt[low : low + head, :] = turned[head_index * head : (head_index + 1) * head, :].astype(BF)
                wqt[low + head : low + 128, :] = jnp.zeros((128 - head, width), BF)
            ln_load.wait()
            out_keep.wait()
            out_send.wait()
            terms(1)

        @pl.when(t == 3 * HEADS + 1)
        def _():
            part_send(1).wait_recv()
            rows_back(1)

        first_half = jnp.logical_or(block == 0, block == 3)
        where = pl.ds(pl.multiple_of(jnp.where(first_half, 0, length), length), length)
        base = jnp.where(block < 2, length, 0)
        queries, grads = qa[h, where, :AUG], doa[h, where, :AUG]
        queries_t, grads_t = qt[h, :, where], dot_t[h, :, where]
        parts = []
        for offset in (0, own):
            for low in range(0, length, tk):
                parts.append(pl.ds(pl.multiple_of(base + (offset + low), tk), tk))

        def pair(part):
            return dot(queries, kta[h, :, part]), dot(grads, vta[h, :, part])

        grad_query = jnp.zeros((length, 128), F32)
        level, change = pair(parts[0])
        for j, part_now in enumerate(parts):
            probs = jnp.exp2(level * (LOG2E * inverse_root))
            probs_low = probs.astype(BF)
            grad_scores = (probs * change).astype(BF)
            if j + 1 < len(parts):
                level, change = pair(parts[j + 1])
            dv_sum[h, :, part_now] += dot(grads_t, probs_low)
            dk_sum[h, :, part_now] += dot(queries_t, grad_scores)
            grad_query = grad_query + dot(grad_scores, kn[h, part_now, :])
        dq_sum[h, where, :] += grad_query

    terms(0)
    grads = jnp.concatenate([jnp.concatenate([gq[:, h * 128 : h * 128 + head] for h in range(HEADS)], 1), gk[...].T, gv[...].T], 0)
    into_slots(early, grads, per)
    for copy in early_first:
        copy.start()
    part_send(0).wait_recv()
    rows_back(0)
    vec_first.start()
    for y in range(2):
        early_first[y].wait_recv()
        early_pass[y] = (early[2 * y + core].astype(F32) + early_one[y].astype(F32)).astype(BF)
    for copy in early_second:
        copy.start()
    vec_first.wait_recv()
    vec_pair[...] = vec_own[...] + vec_one[...]
    for copy in vec_second:
        copy.start()

    @pl.when(ctx >= owners)
    def _():
        total = late_sum[jnp.maximum(ctx - owners, 0)].astype(F32)
        for other in others:
            late_third_from(other).wait_recv()
            total = total + late_three[other].astype(F32)
        gw_ref[...] = total

    def from_plane(slot, holder, got):
        return remote(holder.at[slot], holder.at[slot], got.at[slot], got.at[slot], to_near)

    total = early_pass[mine, place].astype(F32)
    for slot in plane_slots:
        from_plane(slot, early_two, e2_got).wait_recv()
        total = total + early_two[slot].astype(F32)
    early_sum[...] = total.astype(BF)
    if groups > 1:
        @pl.when(group > 0)
        def _():
            early_third.start()

    vec_total = vec_pair[...]
    for slot in plane_slots:
        from_plane(slot, vec_two, v2_got).wait_recv()
        vec_total = vec_total + vec_two[slot]
    vec_sum[...] = vec_total
    for copy in vec_third:
        copy.start()

    @pl.when(group == 0)
    def _():
        whole_sum = total
        for slot in range(groups - 1):
            from_plane(slot, early_three, e3_got).wait_recv()
            whole_sum = whole_sum + early_three[slot].astype(F32)
        gw_ref[...] = whole_sum

    for copy in vec_third:
        copy.wait_send()
    for other in other_groups:
        from_plane(other, vec_three, v3_got).wait_recv()
        vec_total = vec_total + vec_three[other]
    vec_sum[...] = vec_total
    begin = (ctx * blk_size + blk) * entries
    row, shift = lax.div(begin, width), lax.rem(begin, width)
    after = jnp.minimum(row + 1, vec_sum.shape[0] - 1)
    pair_rows = jnp.concatenate([vec_sum[pl.ds(row, 1), :], vec_sum[pl.ds(after, 1), :]], 1)
    pair_rows = jnp.broadcast_to(pair_rows, (8, 2 * width))
    gvec_ref[...] = pltpu.roll(pair_rows, lax.rem(2 * width - shift, 2 * width), 1)[:, :128]

    for copy in late_first + [late_second, part_send(0), part_send(1), vec_first] + early_first + early_second + vec_second:
        copy.wait_send()
    for step, other in enumerate(others):
        @pl.when(other >= owners)
        def _():
            late_third(step).wait_send()

    if groups > 1:
        @pl.when(group > 0)
        def _():
            early_third.wait_send()

    for c in range(chunks):
        grad_keep(c, size).wait()
        grad_send(1, c, size).wait()


def back(ctx_size, blk_size, per, entries, owners, att, lse, qt, kta, vta, kn, ln, rows, grad_near, grad_far, weights, vec):
    own, width = rows.shape
    head = width // HEADS
    total = 2 * own
    length = own // 2
    groups = ctx_size // owners
    hidden_width = (weights.shape[0] - 4 * width) // 2
    late_count = (weights.shape[0] - 3 * width) // (blk_size * per)
    padded = -(-per // 16) * 16
    dma = pltpu.SemaphoreType.DMA
    place = pl.BlockSpec(memory_space=pl.ANY)
    vmem = pl.BlockSpec(memory_space=pltpu.VMEM)
    chunks = length // min(512, length)
    low = lambda *shape: pltpu.VMEM(shape, BF)
    single = lambda *shape: pltpu.VMEM(shape, F32)
    plane = 2 * owners
    some = lambda count: dma((max(count, 1),))
    return pl.pallas_call(
        functools.partial(back_kernel, ctx_size, blk_size, per, entries),
        in_specs=[place] * 11 + [vmem],
        out_specs=[place, place, vmem, vmem],
        out_shape=[
            jax.ShapeDtypeStruct((2, length, width), BF),
            jax.ShapeDtypeStruct((2, length, width), BF),
            jax.ShapeDtypeStruct((padded, width), F32),
            jax.ShapeDtypeStruct((8, 128), F32),
        ],
        scratch_shapes=[
            low(*weights.shape), single(HEADS, head, own), single(HEADS, 8, own), low(own, width), single(width, width), single(width, hidden_width),
            single(width, hidden_width), low(blk_size, late_count, padded, width),
            low(HEADS, own, 128), low(HEADS, own, 128), low(HEADS, head, own), low(HEADS, head, own),
            low(HEADS, AUG, total), low(HEADS, AUG, total), low(HEADS, total, 128), low(total, width),
            low(own, width), single(own, width), low(own, width),
            single(HEADS, own, 128), single(HEADS, head, total), single(HEADS, head, total),
            single(width, HEADS * 128), single(width, width), single(width, width),
            single(2, width, length), low(2, width, length), low(2, width, length), low(HEADS * 128, width),
            low(2, late_count, padded, width), low(2, late_count, padded, width),
            low(late_count, padded, width), low(late_count, padded, width), low(ctx_size, padded, width),
            low(blk_size, owners, padded, width), low(2, owners, padded, width), low(2, owners, padded, width),
            low(plane, padded, width), low(padded, width), low(max(groups - 1, 1), padded, width),
            single(16, width), single(16, width), single(16, width), single(plane, 16, width), single(16, width),
            single(groups, 16, width),
            dma((3, HEADS)), dma((8,)), dma, dma, dma((1 + chunks,)), dma((chunks,)), dma((chunks,)), dma((2,)), dma((2,)),
            dma((2,)), dma((2,)), dma, dma, some(ctx_size - 1), dma((ctx_size,)),
            dma((2,)), dma((2,)), some(plane - 1), dma((plane,)), dma, some(groups - 1),
            dma, dma, some(plane - 1), dma((plane,)), some(groups - 1), dma((groups,)),
        ],
        compiler_params=params(collective_id=2, has_side_effects=True),
        name="back",
    )(att, lse, qt, kta, vta, kn, ln, rows, grad_near, grad_far, weights, vec)


def publish_kernel(grad_ref, out_ref, mats_ref, vec_ref, grad_to, out_to, mats_to, vec_to, grad, out, mats, vecs, sems):
    ways = []
    for a, b, c in ((grad_ref, grad, grad_to), (out_ref, out, out_to)):
        pieces = 2
        size = a.shape[1] // pieces
        for half in range(2):
            for piece in range(pieces):
                part = pl.ds(piece * size, size)
                ways.append((a.at[half, part], b.at[half, part], c.at[half, part]))
    kept = pl.ds(0, mats_to.shape[0])
    ways.append((mats_ref.at[kept], mats.at[kept], mats_to))
    ways.append((vec_ref, vecs, vec_to))
    come = [pltpu.make_async_copy(a, b, sems.at[0, i]) for i, (a, b, _) in enumerate(ways)]
    go = [pltpu.make_async_copy(b, c, sems.at[1, i]) for i, (_, b, c) in enumerate(ways)]
    for copy in come:
        copy.start()
    for first, second in zip(come, go):
        first.wait()
        second.start()
    for copy in go:
        copy.wait()


def publish(grad, out, mats, vecs, per):
    place = pl.BlockSpec(memory_space=pl.ANY)
    shapes = [grad.shape, out.shape, (per, mats.shape[1]) if per % 8 == 0 else mats.shape, vecs.shape]
    types = [BF, BF, F32, F32]
    return pl.pallas_call(
        publish_kernel,
        in_specs=[place] * 4,
        out_specs=[place] * 4,
        out_shape=[jax.ShapeDtypeStruct(shape, kind) for shape, kind in zip(shapes, types)],
        scratch_shapes=[
            pltpu.VMEM(grad.shape, BF), pltpu.VMEM(out.shape, BF), pltpu.VMEM(mats.shape, F32), pltpu.VMEM(vecs.shape, F32),
            pltpu.SemaphoreType.DMA((2, 10)),
        ],
        compiler_params=params(),
        name="publish",
    )(grad, out, mats, vecs)


def per_device(ctx_size, blk_size, layer_in, matrices, vectors, out_grad):
    seq_count, local_rows, width = layer_in.shape
    per, entries = matrices.shape[0], vectors.shape[0]
    far = [(b, (b + blk_size // 2) % blk_size) for b in range(blk_size)]
    owners = 3 * width // (per * blk_size)
    weights = lax.all_gather(matrices, ("ctx", "blk"), axis=0, tiled=True)
    rows, ln, qt, kn, kta, vta, vec = start(ctx_size, blk_size, layer_in, matrices, vectors, owners)

    out_grad, qt = lax.optimization_barrier((out_grad, qt))
    grad_far = lax.ppermute(out_grad, "blk", far)
    att, lse = attend(qt, kn, kta, vta)
    layer_grad, layer_out, matrices_grad, vecs = back(
        ctx_size, blk_size, per, entries, owners, att, lse, qt, kta, vta, kn, ln, rows, out_grad, grad_far, weights, vec
    )
    layer_grad, layer_out, matrices_grad, vecs = publish(layer_grad, layer_out, matrices_grad, vecs, per)
    return layer_out, layer_grad, matrices_grad[:per], vecs[0, :entries]


def solution(mesh):
    rows = P("ctx", "blk", None)
    flat = P(("ctx", "blk"))
    return jax.shard_map(
        functools.partial(per_device, mesh.shape["ctx"], mesh.shape["blk"]),
        mesh=mesh,
        in_specs=(rows, flat, flat, rows),
        out_specs=(rows, rows, flat, flat),
        check_vma=False,
    )
```

```python
import functools
import math

import jax
import jax.numpy as jnp
from jax import lax
from jax.experimental import pallas as pl
from jax.experimental.pallas import tpu as pltpu
from jax.sharding import PartitionSpec as P

HEADS = 4
EPSILON = 1e-05
LOG2E = math.log2(math.e)
LN2 = math.log(2.0)
AUG = 80
SAFE_BOUND = 90.0
BF = jnp.bfloat16
F32 = jnp.float32
NT = (((1,), (1,)), ((), ()))
TN = (((0,), (0,)), ((), ()))


def dot(a, b):
    return jnp.dot(a, b, preferred_element_type=F32)


def dot_nt(a, b):
    return lax.dot_general(a, b, NT, preferred_element_type=F32)


def dot_tn(a, b):
    return lax.dot_general(a, b, TN, preferred_element_type=F32)


def params(**kw):
    return pltpu.CompilerParams(vmem_limit_bytes=60 << 20, **kw)


def whole(*shape):
    return pl.BlockSpec(shape, lambda *_: (0,) * len(shape))


def normalize(inputs):
    centre = jnp.mean(inputs, -1, keepdims=True)
    shifted = inputs - centre
    inverse = lax.rsqrt(jnp.mean(shifted * shifted, -1, keepdims=True) + EPSILON)
    return shifted * inverse, inverse


def normalize_back(grad_hat, normed, inverse):
    return inverse * (
        grad_hat
        - jnp.mean(grad_hat, -1, keepdims=True)
        - normed * jnp.mean(grad_hat * normed, -1, keepdims=True)
    )


MESH = pl.DeviceIdType.MESH


def greet(devices):
    barrier = pltpu.get_barrier_semaphore()
    for device in devices:
        pl.semaphore_signal(barrier, inc=1, device_id=device, device_id_type=MESH)
    pl.semaphore_wait(barrier, len(devices))


def partners(blk_size):
    ctx, blk = lax.axis_index("ctx"), lax.axis_index("blk")
    half = blk_size // 2
    return ctx, blk, blk + 1 - 2 * lax.rem(blk, 2), lax.rem(blk + half, blk_size), lax.div(blk, half)


def start_kernel(
    ctx_size, blk_size, per,
    x_hbm, w_hbm, v_ref,
    rows_out, ln_out, qt_out, kn_out, kta_out, vta_out, vec_ref,
    x, norms, ln, qt, kn, kta, vta, w_slots, w_all, wt, wkp, v_own, v_slots,
    x_sem, far_sent, far_got, near_sent, near_got, relay_sent, relay_got, keep_sem,
    w1_sent, w1_got, w2_sent, w2_got, w3_sent, w3_got, v1_sent, v1_got, v2_sent, v2_got, v3_sent, v3_got,
    rows_sem, out_sem,
):
    ctx, blk, near, far, mine = partners(blk_size)
    _, length, width = x_hbm.shape
    head = width // HEADS
    entries = v_ref.shape[1]
    owners = w_slots.shape[0] // blk_size
    chunks = far_sent.shape[0]
    size = length // chunks
    to_near, to_far = (ctx, near), (ctx, far)
    others = [lax.rem(ctx + step, ctx_size) for step in range(1, ctx_size)]

    def remote(source, target, sent, got, device):
        return pltpu.make_async_remote_copy(
            src_ref=source, dst_ref=target, send_sem=sent, recv_sem=got, device_id=device, device_id_type=MESH
        )

    local = pltpu.make_async_copy
    own_rows = local(x_hbm.at[mine], x.at[pl.ds(0, length)], x_sem)
    near_rows = remote(x_hbm.at[mine], x.at[pl.ds(2 * length, length)], near_sent, near_got, to_near)
    far_rows = [
        remote(x_hbm.at[1 - mine, pl.ds(c * size, size)], x.at[pl.ds(length + c * size, size)], far_sent.at[c], far_got.at[c], to_far)
        for c in range(chunks)
    ]
    relay_rows = [
        remote(
            x.at[pl.ds(length + c * size, size)], x.at[pl.ds(3 * length + c * size, size)],
            relay_sent.at[c], relay_got.at[c], to_near,
        )
        for c in range(chunks)
    ]
    groups = ctx_size // owners
    group, place = lax.div(ctx, owners), lax.rem(ctx, owners)
    peers = [lax.rem(place + step, owners) for step in range(1, owners)]
    mine_slot = place * blk_size + blk
    keep_w = local(w_hbm, w_slots.at[mine_slot], keep_sem)
    w_first = [
        remote(w_hbm, w_slots.at[mine_slot], w1_sent.at[g - 1], w1_got, (g * owners + place, blk)) for g in range(1, groups)
    ]
    plane = [(place, far, to_far)]
    for peer in peers:
        plane += [(peer, blk, (group * owners + peer, blk)), (peer, far, (group * owners + peer, far))]
    here = place * 2 + mine
    w_second = [
        remote(w_slots.at[mine_slot], w_slots.at[mine_slot], w2_sent.at[i], w2_got.at[here], device)
        for i, (_, _, device) in enumerate(plane)
    ]
    w_third = [
        remote(w_slots.at[r * blk_size + b], w_slots.at[r * blk_size + b], w3_sent.at[i], w3_got.at[i], to_near)
        for i, (r, b, _) in enumerate([(place, blk, None)] + plane)
    ]
    v_first = [remote(v_own, v_slots.at[blk, ctx], v1_sent.at[i], v1_got.at[ctx], (other, blk)) for i, other in enumerate(others)]
    v_second = remote(v_slots.at[blk], v_slots.at[blk], v2_sent, v2_got, to_far)
    v_third = [remote(v_slots.at[b], v_slots.at[b], v3_sent.at[i], v3_got.at[i], to_near) for i, b in enumerate((blk, far))]
    rows_keep = local(x.at[pl.ds(0, 2 * length)], rows_out, rows_sem)

    greet([to_near, to_far] + [(other, blk) for other in others] + [(group * owners + peer, far) for peer in peers])
    v_own[...] = jnp.zeros_like(v_own)
    v_own[0:1, :entries] = v_ref[...].astype(F32)

    @pl.when(group == 0)
    def _():
        keep_w.start()
        for copy in w_first:
            copy.start()

    early = max(chunks // 2, 1)
    for copy in far_rows[:early]:
        copy.start()
    own_rows.start()
    near_rows.start()
    for copy in v_first:
        copy.start()
    v_slots[blk, ctx] = v_own[...]
    block = min(512, length)

    def norm(low):
        normed, _ = normalize(x[pl.ds(low, block), :].astype(F32))
        norms[pl.ds(low, block), :] = normed

    own_rows.wait()
    for low in range(0, length, block):
        norm(low)

    @pl.when(group == 0)
    def _():
        keep_w.wait()

    if groups > 1:
        @pl.when(group > 0)
        def _():
            w_first[0].wait_recv()

    for copy in w_second:
        copy.start()
    w_third[0].start()
    for other in others:
        remote(v_own, v_slots.at[blk, other], v1_sent.at[0], v1_got.at[other], to_far).wait_recv()
    v_second.start()
    v_third[0].start()
    for copy in far_rows[early:]:
        copy.start()
    for i, (r, b, _) in enumerate(plane):
        slot = r * blk_size + b
        remote(w_slots.at[slot], w_slots.at[slot], w2_sent.at[0], w2_got.at[r * 2 + lax.div(b, 2)], to_far).wait_recv()
        w_third[i + 1].start()
    remote(v_slots.at[far], v_slots.at[far], v2_sent, v2_got, to_far).wait_recv()
    v_third[1].start()
    for c in range(early):
        far_rows[c].wait_recv()
        relay_rows[c].start()
    near_rows.wait_recv()
    for low in range(2 * length, 3 * length, block):
        norm(low)
    for copy in w_third + v_third:
        copy.wait_recv()

    total = jnp.zeros((16, width), F32)
    place = lax.broadcasted_iota(jnp.int32, (16, width), 0)
    lane = lax.broadcasted_iota(jnp.int32, (16, width), 1)
    for o in range(ctx_size * blk_size):
        row, shift = (o * entries) // width, (o * entries) % width
        piece = jnp.concatenate([v_slots[o % blk_size, o // blk_size], jnp.zeros((8, width - 128), F32)], 1)
        if shift:
            piece = pltpu.roll(piece, shift, 1)
        piece = jnp.broadcast_to(piece[0:1, :], (16, width))
        total = total + jnp.where((place == row) & (lane >= shift), piece, 0.0)
        if shift + entries > width:
            total = total + jnp.where((place == row + 1) & (lane < shift), piece, 0.0)
    vec_ref[...] = total
    for slot in range(w_slots.shape[0]):
        w_all[slot * per : (slot + 1) * per, :] = w_slots[slot, :per, :].astype(F32)
    for index in range(3):
        wt[index * width : (index + 1) * width, :] = w_all[index * width : (index + 1) * width, :].T.astype(BF)
    wk = w_all[width : 2 * width, :]
    for h in range(HEADS):
        wide = jnp.concatenate([wk[:, h * head : (h + 1) * head], jnp.zeros((width, 128 - head), F32)], 1)
        wkp[:, h * 128 : (h + 1) * 128] = wide.astype(BF)
    per_quarter = length // block
    extra = (lax.broadcasted_iota(jnp.int32, (AUG - head, block), 0) < 3).astype(F32).astype(BF)

    def out_copies(base, index):
        rows = pl.ds(base, block)
        pairs = ((ln, ln_out), (kn, kn_out), (kta, kta_out), (vta, vta_out))
        copies = []
        for i, (a, b) in enumerate(pairs):
            if i == 0:
                copies.append(local(a.at[rows], b.at[rows], out_sem.at[i, index]))
            elif i == 1:
                copies.append(local(a.at[:, rows], b.at[:, rows], out_sem.at[i, index]))
            else:
                copies.append(local(a.at[:, :, rows], b.at[:, :, rows], out_sem.at[i, index]))
        return copies

    def query_copy(base, index):
        rows = pl.ds(base, block)
        return local(qt.at[:, :, rows], qt_out.at[:, :, rows], out_sem.at[4, index])

    def first_row(index):
        quarter = lax.div(index, per_quarter)
        order = lax.rem(quarter, 2) * 2 + lax.div(quarter, 2)
        return pl.multiple_of(order * length + lax.rem(index, per_quarter) * block, block)

    @pl.loop(0, 4 * per_quarter)
    def _(index):
        quarter = lax.div(index, per_quarter)

        @pl.when(index == 2 * per_quarter)
        def _():
            for c in range(early, chunks):
                far_rows[c].wait_recv()
                relay_rows[c].start()
            rows_keep.start()

        @pl.when(index == 3 * per_quarter)
        def _():
            for c in range(chunks):
                relay_rows[c].wait_recv()

        base = first_row(index)
        rows = pl.ds(base, block)

        @pl.when(quarter >= 2)
        def _():
            norm(base)

        low = (norms[rows, :] * vec_ref[0:1, :] + vec_ref[1:2, :]).astype(BF)
        ln[rows, :] = low
        kt = dot_nt(wt[width : 2 * width, :], low).astype(BF)
        vt = dot_nt(wt[2 * width : 3 * width, :], low).astype(BF)
        wide = dot(low, wkp[...]).astype(BF)
        for h in range(HEADS):
            kta[h, :head, rows] = kt[h * head : (h + 1) * head, :]
            kta[h, head:, rows] = extra
            vta[h, :head, rows] = vt[h * head : (h + 1) * head, :]
            vta[h, head:, rows] = extra
            kn[h, rows, :] = wide[:, h * 128 : (h + 1) * 128]

        @pl.when(lax.rem(quarter, 2) == 0)
        def _():
            queries = dot_nt(wt[0:width, :], low)
            for h in range(HEADS):
                qt[h, :, rows] = queries[h * head : (h + 1) * head, :].astype(BF)
            query_copy(base, index).start()

        for copy in out_copies(base, index):
            copy.start()

    @pl.loop(0, 4 * per_quarter)
    def _(index):
        base = first_row(index)
        for copy in out_copies(base, index):
            copy.wait()

        @pl.when(lax.rem(lax.div(index, per_quarter), 2) == 0)
        def _():
            query_copy(base, index).wait()

    rows_keep.wait()

    @pl.when(group == 0)
    def _():
        for copy in w_first:
            copy.wait_send()

    for copy in v_first + [v_second] + v_third + far_rows + relay_rows + [near_rows] + w_second + w_third:
        copy.wait_send()


def start(ctx_size, blk_size, layer_in, matrices, vectors, owners):
    seq_count, length, width = layer_in.shape
    per, entries = matrices.shape[0], vectors.shape[0]
    padded = -(-per // 16) * 16
    if padded > per:
        matrices = jnp.pad(matrices, ((0, padded - per), (0, 0)))
    head = width // HEADS
    own, total = 2 * length, 4 * length
    chunks = 4 if length % 64 == 0 else 1
    blocks = total // min(512, length)
    dma = pltpu.SemaphoreType.DMA
    place = pl.BlockSpec(memory_space=pl.ANY)
    vmem = pl.BlockSpec(memory_space=pltpu.VMEM)
    low = lambda *shape: pltpu.VMEM(shape, BF)
    single = lambda *shape: pltpu.VMEM(shape, F32)
    some = dma((max(ctx_size - 1, 1),))
    shapes = [(own, width), (total, width), (HEADS, head, own), (HEADS, total, 128), (HEADS, AUG, total), (HEADS, AUG, total)]
    return pl.pallas_call(
        functools.partial(start_kernel, ctx_size, blk_size, per),
        in_specs=[place, place, vmem],
        out_specs=[place] * 6 + [vmem],
        out_shape=[jax.ShapeDtypeStruct(shape, BF) for shape in shapes] + [jax.ShapeDtypeStruct((16, width), F32)],
        scratch_shapes=[
            low(total, width), single(total, width), low(total, width), low(HEADS, head, own), low(HEADS, total, 128),
            low(HEADS, AUG, total), low(HEADS, AUG, total),
            low(owners * blk_size, padded, width), single(owners * blk_size * per, width),
            low(3 * width, width), low(width, HEADS * 128), single(8, 128), single(blk_size, ctx_size, 8, 128),
            dma, dma((chunks,)), dma((chunks,)), dma, dma, dma((chunks,)), dma((chunks,)), dma,
            dma((max(ctx_size // owners - 1, 1),)), dma, dma((2 * owners,)), dma((2 * owners,)), dma((2 * owners,)), dma((2 * owners,)),
            some, dma((ctx_size,)), dma, dma, dma((2,)), dma((2,)),
            dma, dma((5, blocks)),
        ],
        compiler_params=params(collective_id=1, has_side_effects=True),
        name="start",
    )(layer_in, matrices, vectors.reshape(1, entries))


def attend_kernel(qt_ref, kn_ref, kta_ref, vta_ref, att_ref, lse_ref):
    head, own = qt_ref.shape[1:]
    total = kn_ref.shape[1]
    to_log2 = LOG2E / math.sqrt(head)
    tq = min(1024, own)
    tk = min(256, total)
    count = total // tk

    def longest(rows):
        rows = rows.astype(F32)
        return jnp.max(jnp.sum(rows * rows, 0, keepdims=True))

    bound = longest(qt_ref[0]) * longest(kta_ref[0, :head, :]) * (to_log2 * to_log2)

    def finish(where, summed, top):
        totals = summed[head : head + 1, :]
        att_ref[0, :, where] = summed[:head, :] / totals
        level = jnp.log2(totals)
        lse_ref[0, :, where] = jnp.broadcast_to(level if top is None else level + top, (8, tq))

    def scores(queries, j):
        return dot(kn_ref[0, j * tk : (j + 1) * tk, :head], queries)

    @pl.when(bound <= SAFE_BOUND * SAFE_BOUND)
    def _():
        @pl.loop(0, own // tq)
        def _(i):
            where = pl.ds(pl.multiple_of(i * tq, tq), tq)
            queries = qt_ref[0, :, where]
            summed = jnp.zeros((AUG, tq), F32)
            now = scores(queries, 0)
            for j in range(count):
                expo = jnp.exp2(now * to_log2).astype(BF)
                if j + 1 < count:
                    now = scores(queries, j + 1)
                summed = summed + dot(vta_ref[0, :, j * tk : (j + 1) * tk], expo)
            finish(where, summed, None)

    @pl.when(jnp.logical_not(bound <= SAFE_BOUND * SAFE_BOUND))
    def _():
        @pl.loop(0, own // tq)
        def _(i):
            where = pl.ds(pl.multiple_of(i * tq, tq), tq)
            queries = qt_ref[0, :, where]

            def absorb(j, carry):
                summed, top = carry
                part = pl.ds(pl.multiple_of(j * tk, tk), tk)
                now = dot(kn_ref[0, part, :head], queries) * to_log2
                higher = jnp.maximum(top, jnp.max(now, 0, keepdims=True))
                expo = jnp.exp2(now - higher).astype(BF)
                summed = summed * jnp.exp2(top - higher) + dot(vta_ref[0, :, part], expo)
                return summed, higher

            start = (jnp.zeros((AUG, tq), F32), jnp.full((1, tq), -1e30, F32))
            summed, top = lax.fori_loop(0, count, absorb, start)
            finish(where, summed, top)


def attend(qt, kn, kta, vta):
    _, head, own = qt.shape
    total = kn.shape[1]
    per_head = lambda *shape: pl.BlockSpec((1, *shape), lambda h: (h, 0, 0))
    return pl.pallas_call(
        attend_kernel,
        grid=(HEADS,),
        in_specs=[per_head(head, own), per_head(total, 128), per_head(AUG, total), per_head(AUG, total)],
        out_specs=[per_head(head, own), per_head(8, own)],
        out_shape=[
            jax.ShapeDtypeStruct((HEADS, head, own), F32),
            jax.ShapeDtypeStruct((HEADS, 8, own), F32),
        ],
        compiler_params=params(),
        name="attend",
    )(qt, kn, kta, vta)


def gelu_both(value):
    below = 0.5 + 0.5 * lax.erf(value * math.sqrt(0.5))
    density = jnp.exp2(value * value * (-0.5 * LOG2E) - math.log2(math.sqrt(2.0 * math.pi)))
    return value * below, below + value * density


def split_rows(level, count):
    high = level.astype(BF).astype(F32)
    middle = (level - high).astype(BF).astype(F32)
    low = level - high - middle
    place = lax.broadcasted_iota(jnp.int32, (count, level.shape[1]), 0)
    rows = jnp.where(place == 0, high, jnp.where(place == 1, middle, jnp.where(place == 2, low, 0.0)))
    return rows


def into_slots(slots_ref, grads, per):
    blk_size, owners, padded, width = slots_ref.shape
    filler = jnp.zeros((padded - per, width), F32)
    for slot in range(blk_size * owners):
        piece = grads[slot * per : (slot + 1) * per, :]
        if padded > per:
            piece = jnp.concatenate([piece, filler], 0)
        slots_ref[slot % blk_size, slot // blk_size] = piece.astype(BF)


def back_kernel(
    ctx_size, blk_size, per, entries,
    att_hbm, lse_hbm, qt_hbm, kta_hbm, vta_hbm, ln_hbm, x_hbm, near_hbm, far_hbm, w_hbm,
    vec_ref,
    grad_ref, out_ref, gw_ref, gvec_ref,
    w_ref, att, lse, cotangent, gwo, gup, gdown, late,
    qa_near, doa_near, dot_near, qa_far, doa_far, dot_far, qt, kta, vta, ln, x, gmid, made, turned,
    dq_sum, dk_sum, dv_sum, gq, gk, gv, part, part_out, part_in,
    late_one, late_pass, late_two, late_sum, late_three,
    early, early_one, early_pass, early_two, early_sum, early_three,
    vec_own, vec_one, vec_pair, vec_two, vec_sum, vec_three,
    head_sem, load_sem, out_sent, out_got, keep_sem, grad_sent, grad_got, part_sent, part_got,
    l1_sent, l1_got, l2_sent, l2_got, l3_sent, l3_got,
    e1_sent, e1_got, e2_sent, e2_got, e3_sent, e3_got,
    v1_sent, v1_got, v2_sent, v2_got, v3_sent, v3_got,
):
    ctx, blk, near, far, mine = partners(blk_size)
    core = lax.rem(blk, 2)
    own, width = x.shape
    length = own // 2
    head = width // HEADS
    owners = early.shape[1]
    groups = ctx_size // owners
    group, place = lax.div(ctx, owners), lax.rem(ctx, owners)
    others = [lax.rem(ctx + step, ctx_size) for step in range(1, ctx_size)]
    peers = [lax.rem(place + step, owners) for step in range(1, owners)]

    def remote(source, target, sent, got, device):
        return pltpu.make_async_remote_copy(
            src_ref=source, dst_ref=target, send_sem=sent, recv_sem=got, device_id=device, device_id_type=MESH
        )

    to_near, to_far = (ctx, near), (ctx, far)
    local = pltpu.make_async_copy

    def head_loads(h):
        pairs = ((kta_hbm, kta), (vta_hbm, vta))
        return [local(a.at[h], b.at[h], head_sem.at[i, h]) for i, (a, b) in enumerate(pairs)]

    middle_loads = [
        local(w_hbm, w_ref, load_sem.at[7]),
        local(att_hbm, att, load_sem.at[0]),
        local(x_hbm, x, load_sem.at[1]),
        local(near_hbm.at[mine], cotangent.at[pl.ds(0, length)], load_sem.at[2]),
        local(far_hbm.at[mine], cotangent.at[pl.ds(length, length)], load_sem.at[3]),
        local(lse_hbm, lse, load_sem.at[4]),
        local(qt_hbm, qt, load_sem.at[5]),
    ]
    ln_load = local(ln_hbm, ln, load_sem.at[6])
    out_keep = local(made.at[pl.ds(0, length)], out_ref.at[mine], keep_sem.at[0])
    out_send = remote(made.at[pl.ds(length, length)], out_ref.at[mine], out_sent, out_got, to_far)

    late_first = [
        remote(late.at[2 * y + 1 - core], late_one.at[y], l1_sent.at[y], l1_got.at[y], to_near) for y in range(2)
    ]
    late_second = remote(late_pass.at[1 - mine], late_two, l2_sent, l2_got, to_far)

    def late_third(step):
        other = others[step]
        return remote(
            late_sum.at[jnp.maximum(other - owners, 0)], late_three.at[ctx], l3_sent.at[step], l3_got.at[ctx], (other, blk)
        )

    def late_third_from(other):
        return remote(late_sum.at[0], late_three.at[other], l3_sent.at[0], l3_got.at[other], to_near)

    def grad_send(half, c, size):
        return remote(
            made.at[pl.ds(half * length + c * size, size)], grad_ref.at[mine, pl.ds(c * size, size)],
            grad_sent.at[c], grad_got.at[c], to_far,
        )

    def grad_keep(c, size):
        return local(made.at[pl.ds(c * size, size)], grad_ref.at[mine, pl.ds(c * size, size)], keep_sem.at[1 + c])

    def part_send(half):
        return remote(part_out.at[half], part_in.at[half], part_sent.at[half], part_got.at[half], to_near)

    early_first = [
        remote(early.at[2 * y + 1 - core], early_one.at[y], e1_sent.at[y], e1_got.at[y], to_near) for y in range(2)
    ]
    vec_first = remote(vec_own, vec_one, v1_sent, v1_got, to_near)
    here = mine * owners + place
    plane = [(1 - mine, place, to_far)]
    for peer in peers:
        plane.append((mine, peer, (group * owners + peer, blk)))
        plane.append((1 - mine, peer, (group * owners + peer, far)))
    early_second = [
        remote(early_pass.at[y, r], early_two.at[here], e2_sent.at[i], e2_got.at[here], device)
        for i, (y, r, device) in enumerate(plane)
    ]
    vec_second = [
        remote(vec_pair, vec_two.at[here], v2_sent.at[i], v2_got.at[here], device) for i, (y, r, device) in enumerate(plane)
    ]
    plane_slots = [y * owners + r for y, r, _ in plane]
    early_third = remote(early_sum, early_three.at[jnp.maximum(group - 1, 0)], e3_sent, e3_got.at[jnp.maximum(group - 1, 0)], (place, blk))
    other_groups = [lax.rem(group + step, groups) for step in range(1, groups)]
    vec_third = [
        remote(vec_sum, vec_three.at[group], v3_sent.at[i], v3_got.at[group], (other * owners + place, blk))
        for i, other in enumerate(other_groups)
    ]

    for load in middle_loads + head_loads(0):
        load.start()
    greet([to_near, to_far] + [(other, blk) for other in others] + [(group * owners + peer, far) for peer in peers])
    for ref in (gwo, gup, gdown, vec_own, gq, gk, gv, dq_sum, dk_sum, dv_sum):
        ref[...] = jnp.zeros_like(ref)
    for load in middle_loads:
        load.wait()
    ln_load.start()

    gain_mid, bias_mid = vec_ref[2:3, :], vec_ref[3:4, :]
    wo = w_ref[3 * width : 4 * width, :]
    pieces = (w_ref.shape[0] - 4 * width) // (2 * width)
    down_bias = vec_ref[4 + pieces : 5 + pieces, :]
    from_log2 = math.sqrt(head) * LN2

    def middle_rows(base, low, count, qa, doa, dot_t):
        rows, local_rows = pl.ds(pl.multiple_of(base + low, count), count), pl.ds(pl.multiple_of(low, count), count)
        attended = att[:, :, rows].reshape(width, count)
        att_low = attended.astype(BF)
        grad = cotangent[rows, :]
        gradf = grad.astype(F32)
        grad_t = gradf.T.astype(BF)
        middle = x[rows, :].astype(F32) + dot_tn(att_low, wo)
        normed, inverse = normalize(middle)
        ln_mid = (normed * gain_mid + bias_mid).astype(BF)
        ln_mid_t = ln_mid.astype(F32).T.astype(BF)
        yield
        result = middle + down_bias
        grad_ln = jnp.zeros((count, width), F32)
        for p in range(pieces):
            columns = slice(p * width, (p + 1) * width)
            up = w_ref[(4 + p) * width : (5 + p) * width, :]
            down = w_ref[(4 + pieces + p) * width : (5 + pieces + p) * width, :]
            upper = dot_nt(ln_mid, up) + vec_ref[4 + p : 5 + p, :]
            activated, slope = gelu_both(upper)
            hidden = activated.astype(BF)
            grad_low = (dot_nt(grad, down) * slope).astype(BF)
            result = result + dot(hidden, down)
            grad_ln = grad_ln + dot(grad_low, up)
            gdown[:, columns] += dot(grad_t, hidden)
            gup[:, columns] += dot(ln_mid_t, grad_low)
            vec_own[4 + p : 5 + p, :] += jnp.sum(grad_low.astype(F32), 0, keepdims=True)
            yield
        made[rows, :] = result.astype(BF)
        vec_own[2:3, :] += jnp.sum(grad_ln * normed, 0, keepdims=True)
        vec_own[3:4, :] += jnp.sum(grad_ln, 0, keepdims=True)
        vec_own[4 + pieces : 5 + pieces, :] += jnp.sum(gradf, 0, keepdims=True)
        grad_mid = gradf + normalize_back(grad_ln * gain_mid, normed, inverse)
        gmid[rows, :] = grad_mid
        branch = grad_mid.astype(BF)
        gwo[...] += dot(att_low, branch)
        grad_att = dot_nt(wo, branch).astype(BF)
        spare = jnp.zeros((128 - AUG, count), F32)
        yield
        for h in range(HEADS):
            part_of = slice(h * head, (h + 1) * head)
            grad_head = grad_att[part_of, :]
            dot_t[h, :, local_rows] = grad_head
            grad_head = grad_head.astype(F32)
            delta = jnp.sum(grad_head * attended[part_of, :], 0, keepdims=True)
            wide = jnp.concatenate([grad_head, split_rows(-delta, AUG - head), spare], 0)
            doa[h, local_rows, :] = wide.T.astype(BF)
            level = lse[h, 0:1, rows] * from_log2
            wide = jnp.concatenate([qt[h, :, rows].astype(F32), split_rows(-level, AUG - head), spare], 0)
            qa[h, local_rows, :] = wide.T.astype(BF)
            if h == 1:
                yield

    step_rows = min(512, length)

    @pl.loop(0, length // step_rows)
    def _(index):
        for _ in middle_rows(0, index * step_rows, step_rows, qa_near, doa_near, dot_near):
            pass

    out_keep.start()
    tk = min(256, length)
    inverse_root = 1.0 / math.sqrt(head)
    wq, wk, wv = (w_ref[index * width : (index + 1) * width, :] for index in range(3))
    gain = vec_ref[0:1, :]
    size = min(512, length)
    chunks = length // size

    def terms(half):
        for core_rows in (1, 0):
            low = core_rows * own + half * length
            rows = slice(low, low + length)
            dk = (dk_sum[:, :, rows] * inverse_root).astype(BF).reshape(width, length)
            dv = dv_sum[:, :, rows].astype(BF).reshape(width, length)
            both = dot(wk, dk) + dot(wv, dv)
            if core_rows:
                part_out[half] = both.astype(BF)
                part_send(half).start()
            else:
                dq = (dq_sum[:, :, rows] * inverse_root).astype(BF).reshape(width, length)
                part[half] = both + dot(wq, dq)
                gq[...] += dot(dq, ln[rows, :])
            gk[...] += dot(dk, ln[rows, :])
            gv[...] += dot(dv, ln[rows, :])

    def rows_back(half):
        for c in range(chunks):
            rows = slice(half * length + c * size, half * length + (c + 1) * size)
            lanes = slice(c * size, (c + 1) * size)
            grad_ln = (part[half, :, lanes] + part_in[half, :, lanes].astype(F32)).T
            normed, inverse = normalize(x[rows, :].astype(F32))
            vec_own[0:1, :] += jnp.sum(grad_ln * normed, 0, keepdims=True)
            vec_own[1:2, :] += jnp.sum(grad_ln, 0, keepdims=True)
            made[rows, :] = (gmid[rows, :] + normalize_back(grad_ln * gain, normed, inverse)).astype(BF)
            (grad_send(half, c, size) if half else grad_keep(c, size)).start()

    def attention(h, half, base, qa, doa, dot_t, beside=None):
        beside = beside or iter(())
        queries, grads = qa[h, :, :AUG], doa[h, :, :AUG]
        where = slice(half * length, (half + 1) * length)
        queries_t, grads_t = qt[h, :, where], dot_t[h]
        parts = []
        for offset in (0, own):
            for low in range(0, length, tk):
                parts.append(pl.ds(pl.multiple_of(base + (offset + low), tk), tk))

        def pair(part):
            return dot(queries, kta[h, :, part]), dot(grads, vta[h, :, part])

        grad_query = jnp.zeros((head, length), F32)
        level, change = pair(parts[0])
        for j, part_now in enumerate(parts):
            probs = jnp.exp2(level * (LOG2E * inverse_root))
            probs_low = probs.astype(BF)
            grad_scores = (probs * change).astype(BF)
            if j + 1 < len(parts):
                level, change = pair(parts[j + 1])
            next(beside, None)
            dv_sum[h, :, part_now] += dot(grads_t, probs_low)
            dk_sum[h, :, part_now] += dot(queries_t, grad_scores)
            turned[j % 2] = grad_scores.T
            grad_query = grad_query + dot(kta[h, :head, part_now], turned[j % 2])
        for _ in beside:
            pass
        dq_sum[h, :, where] += grad_query

    piece_rows = length // HEADS

    @pl.loop(0, HEADS)
    def _(h):
        for load in head_loads(h):
            load.wait()

        @pl.when(h < HEADS - 1)
        def _():
            for load in head_loads(h + 1):
                load.start()

        beside = middle_rows(length, h * piece_rows, piece_rows, qa_far, doa_far, dot_far)
        attention(h, 0, length, qa_near, doa_near, dot_near, beside)

    out_send.start()
    into_slots(late, jnp.concatenate([gwo[...], gup[...].T, gdown[...].T], 0), per)
    for copy in late_first:
        copy.start()

    @pl.loop(0, 2 * HEADS)
    def _(t):
        @pl.when(t == 1)
        def _():
            for y in range(2):
                late_first[y].wait_recv()
                late_pass[y] = (late[2 * y + core].astype(F32) + late_one[y].astype(F32)).astype(BF)
            late_second.start()

        @pl.when(t == 4)
        def _():
            late_second.wait_recv()
            late_sum[...] = (late_pass[mine].astype(F32) + late_two[...].astype(F32)).astype(BF)
            for step, other in enumerate(others):
                @pl.when(other >= owners)
                def _():
                    late_third(step).start()

        attention(lax.rem(t, HEADS), 1, jnp.where(t < HEADS, length, 0), qa_far, doa_far, dot_far)

    ln_load.wait()
    out_keep.wait()
    out_send.wait()
    terms(1)

    @pl.loop(0, HEADS)
    def _(h):
        @pl.when(h == 1)
        def _():
            part_send(1).wait_recv()
            rows_back(1)

        attention(h, 0, 0, qa_near, doa_near, dot_near)

    terms(0)
    grads = jnp.concatenate([gq[...].T, gk[...].T, gv[...].T], 0)
    into_slots(early, grads, per)
    for copy in early_first:
        copy.start()
    part_send(0).wait_recv()
    rows_back(0)
    vec_first.start()
    for y in range(2):
        early_first[y].wait_recv()
        early_pass[y] = (early[2 * y + core].astype(F32) + early_one[y].astype(F32)).astype(BF)
    for copy in early_second:
        copy.start()
    vec_first.wait_recv()
    vec_pair[...] = vec_own[...] + vec_one[...]
    for copy in vec_second:
        copy.start()

    @pl.when(ctx >= owners)
    def _():
        total = late_sum[jnp.maximum(ctx - owners, 0)].astype(F32)
        for other in others:
            late_third_from(other).wait_recv()
            total = total + late_three[other].astype(F32)
        gw_ref[...] = total

    def from_plane(slot, holder, got):
        return remote(holder.at[slot], holder.at[slot], got.at[slot], got.at[slot], to_near)

    total = early_pass[mine, place].astype(F32)
    for slot in plane_slots:
        from_plane(slot, early_two, e2_got).wait_recv()
        total = total + early_two[slot].astype(F32)
    early_sum[...] = total.astype(BF)
    if groups > 1:
        @pl.when(group > 0)
        def _():
            early_third.start()

    vec_total = vec_pair[...]
    for slot in plane_slots:
        from_plane(slot, vec_two, v2_got).wait_recv()
        vec_total = vec_total + vec_two[slot]
    vec_sum[...] = vec_total
    for copy in vec_third:
        copy.start()

    @pl.when(group == 0)
    def _():
        whole_sum = total
        for slot in range(groups - 1):
            from_plane(slot, early_three, e3_got).wait_recv()
            whole_sum = whole_sum + early_three[slot].astype(F32)
        gw_ref[...] = whole_sum

    for copy in vec_third:
        copy.wait_send()
    for other in other_groups:
        from_plane(other, vec_three, v3_got).wait_recv()
        vec_total = vec_total + vec_three[other]
    vec_sum[...] = vec_total
    begin = (ctx * blk_size + blk) * entries
    row, shift = lax.div(begin, width), lax.rem(begin, width)
    after = jnp.minimum(row + 1, vec_sum.shape[0] - 1)
    pair_rows = jnp.concatenate([vec_sum[pl.ds(row, 1), :], vec_sum[pl.ds(after, 1), :]], 1)
    pair_rows = jnp.broadcast_to(pair_rows, (8, 2 * width))
    gvec_ref[...] = pltpu.roll(pair_rows, lax.rem(2 * width - shift, 2 * width), 1)[:, :128]

    for copy in late_first + [late_second, part_send(0), part_send(1), vec_first] + early_first + early_second + vec_second:
        copy.wait_send()
    for step, other in enumerate(others):
        @pl.when(other >= owners)
        def _():
            late_third(step).wait_send()

    if groups > 1:
        @pl.when(group > 0)
        def _():
            early_third.wait_send()

    for c in range(chunks):
        grad_keep(c, size).wait()
        grad_send(1, c, size).wait()


def back(ctx_size, blk_size, per, entries, owners, att, lse, qt, kta, vta, ln, rows, grad_near, grad_far, weights, vec):
    own, width = rows.shape
    head = width // HEADS
    total = 2 * own
    length = own // 2
    groups = ctx_size // owners
    hidden_width = (weights.shape[0] - 4 * width) // 2
    late_count = (weights.shape[0] - 3 * width) // (blk_size * per)
    padded = -(-per // 16) * 16
    dma = pltpu.SemaphoreType.DMA
    place = pl.BlockSpec(memory_space=pl.ANY)
    vmem = pl.BlockSpec(memory_space=pltpu.VMEM)
    chunks = length // min(512, length)
    low = lambda *shape: pltpu.VMEM(shape, BF)
    single = lambda *shape: pltpu.VMEM(shape, F32)
    plane = 2 * owners
    some = lambda count: dma((max(count, 1),))
    return pl.pallas_call(
        functools.partial(back_kernel, ctx_size, blk_size, per, entries),
        in_specs=[place] * 10 + [vmem],
        out_specs=[place, place, vmem, vmem],
        out_shape=[
            jax.ShapeDtypeStruct((2, length, width), BF),
            jax.ShapeDtypeStruct((2, length, width), BF),
            jax.ShapeDtypeStruct((padded, width), F32),
            jax.ShapeDtypeStruct((8, 128), F32),
        ],
        scratch_shapes=[
            low(*weights.shape), single(HEADS, head, own), single(HEADS, 8, own), low(own, width), single(width, width), single(width, hidden_width),
            single(width, hidden_width), low(blk_size, late_count, padded, width),
            low(HEADS, length, 128), low(HEADS, length, 128), low(HEADS, head, length),
            low(HEADS, length, 128), low(HEADS, length, 128), low(HEADS, head, length), low(HEADS, head, own),
            low(HEADS, AUG, total), low(HEADS, AUG, total), low(total, width),
            low(own, width), single(own, width), low(own, width), low(2, min(256, length), length),
            single(HEADS, head, own), single(HEADS, head, total), single(HEADS, head, total),
            single(width, width), single(width, width), single(width, width),
            single(2, width, length), low(2, width, length), low(2, width, length),
            low(2, late_count, padded, width), low(2, late_count, padded, width),
            low(late_count, padded, width), low(late_count, padded, width), low(ctx_size, padded, width),
            low(blk_size, owners, padded, width), low(2, owners, padded, width), low(2, owners, padded, width),
            low(plane, padded, width), low(padded, width), low(max(groups - 1, 1), padded, width),
            single(16, width), single(16, width), single(16, width), single(plane, 16, width), single(16, width),
            single(groups, 16, width),
            dma((2, HEADS)), dma((8,)), dma, dma, dma((1 + chunks,)), dma((chunks,)), dma((chunks,)), dma((2,)), dma((2,)),
            dma((2,)), dma((2,)), dma, dma, some(ctx_size - 1), dma((ctx_size,)),
            dma((2,)), dma((2,)), some(plane - 1), dma((plane,)), dma, some(groups - 1),
            dma, dma, some(plane - 1), dma((plane,)), some(groups - 1), dma((groups,)),
        ],
        compiler_params=params(collective_id=2, has_side_effects=True),
        name="back",
    )(att, lse, qt, kta, vta, ln, rows, grad_near, grad_far, weights, vec)


def publish_kernel(grad_ref, out_ref, mats_ref, vec_ref, grad_to, out_to, mats_to, vec_to, grad, out, mats, vecs, sems):
    ways = []
    for a, b, c in ((grad_ref, grad, grad_to), (out_ref, out, out_to)):
        pieces = 2
        size = a.shape[1] // pieces
        for half in range(2):
            for piece in range(pieces):
                part = pl.ds(piece * size, size)
                ways.append((a.at[half, part], b.at[half, part], c.at[half, part]))
    kept = pl.ds(0, mats_to.shape[0])
    ways.append((mats_ref.at[kept], mats.at[kept], mats_to))
    ways.append((vec_ref, vecs, vec_to))
    come = [pltpu.make_async_copy(a, b, sems.at[0, i]) for i, (a, b, _) in enumerate(ways)]
    go = [pltpu.make_async_copy(b, c, sems.at[1, i]) for i, (_, b, c) in enumerate(ways)]
    for copy in come:
        copy.start()
    for first, second in zip(come, go):
        first.wait()
        second.start()
    for copy in go:
        copy.wait()


def publish(grad, out, mats, vecs, per):
    place = pl.BlockSpec(memory_space=pl.ANY)
    shapes = [grad.shape, out.shape, (per, mats.shape[1]) if per % 8 == 0 else mats.shape, vecs.shape]
    types = [BF, BF, F32, F32]
    return pl.pallas_call(
        publish_kernel,
        in_specs=[place] * 4,
        out_specs=[place] * 4,
        out_shape=[jax.ShapeDtypeStruct(shape, kind) for shape, kind in zip(shapes, types)],
        scratch_shapes=[
            pltpu.VMEM(grad.shape, BF), pltpu.VMEM(out.shape, BF), pltpu.VMEM(mats.shape, F32), pltpu.VMEM(vecs.shape, F32),
            pltpu.SemaphoreType.DMA((2, 10)),
        ],
        compiler_params=params(),
        name="publish",
    )(grad, out, mats, vecs)


def per_device(ctx_size, blk_size, layer_in, matrices, vectors, out_grad):
    seq_count, local_rows, width = layer_in.shape
    per, entries = matrices.shape[0], vectors.shape[0]
    far = [(b, (b + blk_size // 2) % blk_size) for b in range(blk_size)]
    owners = 3 * width // (per * blk_size)
    weights = lax.all_gather(matrices, ("ctx", "blk"), axis=0, tiled=True)
    rows, ln, qt, kn, kta, vta, vec = start(ctx_size, blk_size, layer_in, matrices, vectors, owners)

    out_grad, qt = lax.optimization_barrier((out_grad, qt))
    grad_far = lax.ppermute(out_grad, "blk", far)
    att, lse = attend(qt, kn, kta, vta)
    layer_grad, layer_out, matrices_grad, vecs = back(
        ctx_size, blk_size, per, entries, owners, att, lse, qt, kta, vta, ln, rows, out_grad, grad_far, weights, vec
    )
    layer_grad, layer_out, matrices_grad, vecs = publish(layer_grad, layer_out, matrices_grad, vecs, per)
    return layer_out, layer_grad, matrices_grad[:per], vecs[0, :entries]


def solution(mesh):
    rows = P("ctx", "blk", None)
    flat = P(("ctx", "blk"))
    return jax.shard_map(
        functools.partial(per_device, mesh.shape["ctx"], mesh.shape["blk"]),
        mesh=mesh,
        in_specs=(rows, flat, flat, rows),
        out_specs=(rows, rows, flat, flat),
        check_vma=False,
    )
```

```python
import functools
import math

import jax
import jax.numpy as jnp
from jax import lax
from jax.experimental import pallas as pl
from jax.experimental.pallas import tpu as pltpu
from jax.sharding import PartitionSpec as P

HEADS = 4
EPSILON = 1e-05
LOG2E = math.log2(math.e)
LN2 = math.log(2.0)
AUG = 80
SAFE_BOUND = 90.0
BF = jnp.bfloat16
F32 = jnp.float32
NT = (((1,), (1,)), ((), ()))
TN = (((0,), (0,)), ((), ()))


def dot(a, b):
    return jnp.dot(a, b, preferred_element_type=F32)


def dot_nt(a, b):
    return lax.dot_general(a, b, NT, preferred_element_type=F32)


def dot_tn(a, b):
    return lax.dot_general(a, b, TN, preferred_element_type=F32)


def params(**kw):
    return pltpu.CompilerParams(vmem_limit_bytes=60 << 20, **kw)


def whole(*shape):
    return pl.BlockSpec(shape, lambda *_: (0,) * len(shape))


def normalize(inputs):
    centre = jnp.mean(inputs, -1, keepdims=True)
    shifted = inputs - centre
    inverse = lax.rsqrt(jnp.mean(shifted * shifted, -1, keepdims=True) + EPSILON)
    return shifted * inverse, inverse


def normalize_back(grad_hat, normed, inverse):
    return inverse * (
        grad_hat
        - jnp.mean(grad_hat, -1, keepdims=True)
        - normed * jnp.mean(grad_hat * normed, -1, keepdims=True)
    )


MESH = pl.DeviceIdType.MESH


def greet(devices):
    barrier = pltpu.get_barrier_semaphore()
    for device in devices:
        pl.semaphore_signal(barrier, inc=1, device_id=device, device_id_type=MESH)
    pl.semaphore_wait(barrier, len(devices))


def partners(blk_size):
    ctx, blk = lax.axis_index("ctx"), lax.axis_index("blk")
    half = blk_size // 2
    return ctx, blk, blk + 1 - 2 * lax.rem(blk, 2), lax.rem(blk + half, blk_size), lax.div(blk, half)


def start_kernel(
    ctx_size, blk_size, per,
    x_hbm, w_hbm, v_ref,
    rows_out, ln_out, qt_out, kn_out, kta_out, vta_out, vec_ref,
    x, norms, ln, qt, kn, kta, vta, w_slots, w_all, wt, wkp, v_own, v_slots,
    x_sem, far_sent, far_got, near_sent, near_got, relay_sent, relay_got, keep_sem,
    w1_sent, w1_got, w2_sent, w2_got, w3_sent, w3_got, v1_sent, v1_got, v2_sent, v2_got, v3_sent, v3_got,
    rows_sem, out_sem,
):
    ctx, blk, near, far, mine = partners(blk_size)
    _, length, width = x_hbm.shape
    head = width // HEADS
    entries = v_ref.shape[1]
    owners = w_slots.shape[0] // blk_size
    chunks = far_sent.shape[0]
    size = length // chunks
    to_near, to_far = (ctx, near), (ctx, far)
    others = [lax.rem(ctx + step, ctx_size) for step in range(1, ctx_size)]

    def remote(source, target, sent, got, device):
        return pltpu.make_async_remote_copy(
            src_ref=source, dst_ref=target, send_sem=sent, recv_sem=got, device_id=device, device_id_type=MESH
        )

    local = pltpu.make_async_copy
    own_rows = local(x_hbm.at[mine], x.at[pl.ds(0, length)], x_sem)
    near_rows = remote(x_hbm.at[mine], x.at[pl.ds(2 * length, length)], near_sent, near_got, to_near)
    far_rows = [
        remote(x_hbm.at[1 - mine, pl.ds(c * size, size)], x.at[pl.ds(length + c * size, size)], far_sent.at[c], far_got.at[c], to_far)
        for c in range(chunks)
    ]
    relay_rows = [
        remote(
            x.at[pl.ds(length + c * size, size)], x.at[pl.ds(3 * length + c * size, size)],
            relay_sent.at[c], relay_got.at[c], to_near,
        )
        for c in range(chunks)
    ]
    groups = ctx_size // owners
    group, place = lax.div(ctx, owners), lax.rem(ctx, owners)
    peers = [lax.rem(place + step, owners) for step in range(1, owners)]
    mine_slot = place * blk_size + blk
    keep_w = local(w_hbm, w_slots.at[mine_slot], keep_sem)
    w_first = [
        remote(w_hbm, w_slots.at[mine_slot], w1_sent.at[g - 1], w1_got, (g * owners + place, blk)) for g in range(1, groups)
    ]
    plane = [(place, far, to_far)]
    for peer in peers:
        plane += [(peer, blk, (group * owners + peer, blk)), (peer, far, (group * owners + peer, far))]
    here = place * 2 + mine
    w_second = [
        remote(w_slots.at[mine_slot], w_slots.at[mine_slot], w2_sent.at[i], w2_got.at[here], device)
        for i, (_, _, device) in enumerate(plane)
    ]
    w_third = [
        remote(w_slots.at[r * blk_size + b], w_slots.at[r * blk_size + b], w3_sent.at[i], w3_got.at[i], to_near)
        for i, (r, b, _) in enumerate([(place, blk, None)] + plane)
    ]
    v_first = [remote(v_own, v_slots.at[blk, ctx], v1_sent.at[i], v1_got.at[ctx], (other, blk)) for i, other in enumerate(others)]
    v_second = remote(v_slots.at[blk], v_slots.at[blk], v2_sent, v2_got, to_far)
    v_third = [remote(v_slots.at[b], v_slots.at[b], v3_sent.at[i], v3_got.at[i], to_near) for i, b in enumerate((blk, far))]
    rows_keep = local(x.at[pl.ds(0, 2 * length)], rows_out, rows_sem)

    greet([to_near, to_far] + [(other, blk) for other in others] + [(group * owners + peer, far) for peer in peers])
    v_own[...] = jnp.zeros_like(v_own)
    v_own[0:1, :entries] = v_ref[...].astype(F32)

    @pl.when(group == 0)
    def _():
        keep_w.start()
        for copy in w_first:
            copy.start()

    early = max(chunks // 2, 1)
    for copy in far_rows[:early]:
        copy.start()
    own_rows.start()
    near_rows.start()
    for copy in v_first:
        copy.start()
    v_slots[blk, ctx] = v_own[...]
    block = min(512, length)

    def norm(low):
        normed, _ = normalize(x[pl.ds(low, block), :].astype(F32))
        norms[pl.ds(low, block), :] = normed

    own_rows.wait()
    for low in range(0, length, block):
        norm(low)

    @pl.when(group == 0)
    def _():
        keep_w.wait()

    if groups > 1:
        @pl.when(group > 0)
        def _():
            w_first[0].wait_recv()

    for copy in w_second:
        copy.start()
    w_third[0].start()
    for other in others:
        remote(v_own, v_slots.at[blk, other], v1_sent.at[0], v1_got.at[other], to_far).wait_recv()
    v_second.start()
    v_third[0].start()
    for copy in far_rows[early:]:
        copy.start()
    for i, (r, b, _) in enumerate(plane):
        slot = r * blk_size + b
        remote(w_slots.at[slot], w_slots.at[slot], w2_sent.at[0], w2_got.at[r * 2 + lax.div(b, 2)], to_far).wait_recv()
        w_third[i + 1].start()
    remote(v_slots.at[far], v_slots.at[far], v2_sent, v2_got, to_far).wait_recv()
    v_third[1].start()
    for c in range(early):
        far_rows[c].wait_recv()
        relay_rows[c].start()
    near_rows.wait_recv()
    for low in range(2 * length, 3 * length, block):
        norm(low)
    for copy in w_third + v_third:
        copy.wait_recv()

    total = jnp.zeros((16, width), F32)
    place = lax.broadcasted_iota(jnp.int32, (16, width), 0)
    lane = lax.broadcasted_iota(jnp.int32, (16, width), 1)
    for o in range(ctx_size * blk_size):
        row, shift = (o * entries) // width, (o * entries) % width
        piece = jnp.concatenate([v_slots[o % blk_size, o // blk_size], jnp.zeros((8, width - 128), F32)], 1)
        if shift:
            piece = pltpu.roll(piece, shift, 1)
        piece = jnp.broadcast_to(piece[0:1, :], (16, width))
        total = total + jnp.where((place == row) & (lane >= shift), piece, 0.0)
        if shift + entries > width:
            total = total + jnp.where((place == row + 1) & (lane < shift), piece, 0.0)
    vec_ref[...] = total
    for slot in range(w_slots.shape[0]):
        w_all[slot * per : (slot + 1) * per, :] = w_slots[slot, :per, :].astype(F32)
    for index in range(3):
        wt[index * width : (index + 1) * width, :] = w_all[index * width : (index + 1) * width, :].T.astype(BF)
    wk = w_all[width : 2 * width, :]
    for h in range(HEADS):
        wide = jnp.concatenate([wk[:, h * head : (h + 1) * head], jnp.zeros((width, 128 - head), F32)], 1)
        wkp[:, h * 128 : (h + 1) * 128] = wide.astype(BF)
    per_quarter = length // block
    extra = (lax.broadcasted_iota(jnp.int32, (AUG - head, block), 0) < 3).astype(F32).astype(BF)

    def out_copies(base, index):
        rows = pl.ds(base, block)
        pairs = ((ln, ln_out), (kn, kn_out), (kta, kta_out), (vta, vta_out))
        copies = []
        for i, (a, b) in enumerate(pairs):
            if i == 0:
                copies.append(local(a.at[rows], b.at[rows], out_sem.at[i, index]))
            elif i == 1:
                copies.append(local(a.at[:, rows], b.at[:, rows], out_sem.at[i, index]))
            else:
                copies.append(local(a.at[:, :, rows], b.at[:, :, rows], out_sem.at[i, index]))
        return copies

    def query_copy(base, index):
        rows = pl.ds(base, block)
        return local(qt.at[:, :, rows], qt_out.at[:, :, rows], out_sem.at[4, index])

    def first_row(index):
        quarter = lax.div(index, per_quarter)
        order = lax.rem(quarter, 2) * 2 + lax.div(quarter, 2)
        return pl.multiple_of(order * length + lax.rem(index, per_quarter) * block, block)

    @pl.loop(0, 4 * per_quarter)
    def _(index):
        quarter = lax.div(index, per_quarter)

        @pl.when(index == 2 * per_quarter)
        def _():
            for c in range(early, chunks):
                far_rows[c].wait_recv()
                relay_rows[c].start()
            rows_keep.start()

        @pl.when(index == 3 * per_quarter)
        def _():
            for c in range(chunks):
                relay_rows[c].wait_recv()

        base = first_row(index)
        rows = pl.ds(base, block)

        @pl.when(quarter >= 2)
        def _():
            norm(base)

        low = (norms[rows, :] * vec_ref[0:1, :] + vec_ref[1:2, :]).astype(BF)
        ln[rows, :] = low
        kt = dot_nt(wt[width : 2 * width, :], low).astype(BF)
        vt = dot_nt(wt[2 * width : 3 * width, :], low).astype(BF)
        wide = dot(low, wkp[...]).astype(BF)
        for h in range(HEADS):
            kta[h, :head, rows] = kt[h * head : (h + 1) * head, :]
            kta[h, head:, rows] = extra
            vta[h, :head, rows] = vt[h * head : (h + 1) * head, :]
            vta[h, head:, rows] = extra
            kn[h, rows, :] = wide[:, h * 128 : (h + 1) * 128]

        @pl.when(lax.rem(quarter, 2) == 0)
        def _():
            queries = dot_nt(wt[0:width, :], low)
            for h in range(HEADS):
                qt[h, :, rows] = queries[h * head : (h + 1) * head, :].astype(BF)
            query_copy(base, index).start()

        for copy in out_copies(base, index):
            copy.start()

    @pl.loop(0, 4 * per_quarter)
    def _(index):
        base = first_row(index)
        for copy in out_copies(base, index):
            copy.wait()

        @pl.when(lax.rem(lax.div(index, per_quarter), 2) == 0)
        def _():
            query_copy(base, index).wait()

    rows_keep.wait()

    @pl.when(group == 0)
    def _():
        for copy in w_first:
            copy.wait_send()

    for copy in v_first + [v_second] + v_third + far_rows + relay_rows + [near_rows] + w_second + w_third:
        copy.wait_send()


def start(ctx_size, blk_size, layer_in, matrices, vectors, owners):
    seq_count, length, width = layer_in.shape
    per, entries = matrices.shape[0], vectors.shape[0]
    padded = -(-per // 16) * 16
    if padded > per:
        matrices = jnp.pad(matrices, ((0, padded - per), (0, 0)))
    head = width // HEADS
    own, total = 2 * length, 4 * length
    chunks = 4 if length % 64 == 0 else 1
    blocks = total // min(512, length)
    dma = pltpu.SemaphoreType.DMA
    place = pl.BlockSpec(memory_space=pl.ANY)
    vmem = pl.BlockSpec(memory_space=pltpu.VMEM)
    low = lambda *shape: pltpu.VMEM(shape, BF)
    single = lambda *shape: pltpu.VMEM(shape, F32)
    some = dma((max(ctx_size - 1, 1),))
    shapes = [(own, width), (total, width), (HEADS, head, own), (HEADS, total, 128), (HEADS, AUG, total), (HEADS, AUG, total)]
    return pl.pallas_call(
        functools.partial(start_kernel, ctx_size, blk_size, per),
        in_specs=[place, place, vmem],
        out_specs=[place] * 6 + [vmem],
        out_shape=[jax.ShapeDtypeStruct(shape, BF) for shape in shapes] + [jax.ShapeDtypeStruct((16, width), F32)],
        scratch_shapes=[
            low(total, width), single(total, width), low(total, width), low(HEADS, head, own), low(HEADS, total, 128),
            low(HEADS, AUG, total), low(HEADS, AUG, total),
            low(owners * blk_size, padded, width), single(owners * blk_size * per, width),
            low(3 * width, width), low(width, HEADS * 128), single(8, 128), single(blk_size, ctx_size, 8, 128),
            dma, dma((chunks,)), dma((chunks,)), dma, dma, dma((chunks,)), dma((chunks,)), dma,
            dma((max(ctx_size // owners - 1, 1),)), dma, dma((2 * owners,)), dma((2 * owners,)), dma((2 * owners,)), dma((2 * owners,)),
            some, dma((ctx_size,)), dma, dma, dma((2,)), dma((2,)),
            dma, dma((5, blocks)),
        ],
        compiler_params=params(collective_id=1, has_side_effects=True),
        name="start",
    )(layer_in, matrices, vectors.reshape(1, entries))


def attend_kernel(qt_ref, kn_ref, kta_ref, vta_ref, att_ref, lse_ref):
    head, own = qt_ref.shape[1:]
    total = kn_ref.shape[1]
    to_log2 = LOG2E / math.sqrt(head)
    tq = min(1024, own)
    tk = min(256, total)
    count = total // tk

    def longest(rows):
        rows = rows.astype(F32)
        return jnp.max(jnp.sum(rows * rows, 0, keepdims=True))

    bound = longest(qt_ref[0]) * longest(kta_ref[0, :head, :]) * (to_log2 * to_log2)

    def finish(where, summed, totals, top):
        att_ref[0, :, where] = summed[:head, :] / totals
        level = jnp.log2(totals)
        lse_ref[0, :, where] = jnp.broadcast_to(level if top is None else level + top, (8, tq))

    @pl.when(bound <= SAFE_BOUND * SAFE_BOUND)
    def _():
        @pl.loop(0, own // tq)
        def _(i):
            where = pl.ds(pl.multiple_of(i * tq, tq), tq)
            queries = qt_ref[0, :, where]
            some = min(256, tq)
            blocks = [slice(low, low + some) for low in range(0, tq, some)]
            summed = [jnp.zeros((head, some), F32) for _ in blocks]
            sums = [jnp.zeros((8, some), F32) for _ in blocks]
            before = None
            for j in range(count + 1):
                made = []
                for c, columns in enumerate(blocks):
                    if j < count:
                        now = dot(kn_ref[0, j * tk : (j + 1) * tk, :head], queries[:, columns])
                    if j > 0:
                        values = vta_ref[0, :head, (j - 1) * tk : j * tk]
                        summed[c] = summed[c] + dot(values, before[c])
                    if j < count:
                        expo = jnp.exp2(now * to_log2)
                        sums[c] = sums[c] + jnp.sum(expo.reshape(tk // 8, 8, some), 0)
                        made.append(expo.astype(BF))
                before = made
            totals = jnp.sum(jnp.concatenate(sums, 1), 0, keepdims=True)
            finish(where, jnp.concatenate(summed, 1), totals, None)

    @pl.when(jnp.logical_not(bound <= SAFE_BOUND * SAFE_BOUND))
    def _():
        @pl.loop(0, own // tq)
        def _(i):
            where = pl.ds(pl.multiple_of(i * tq, tq), tq)
            queries = qt_ref[0, :, where]

            def absorb(j, carry):
                summed, top = carry
                part = pl.ds(pl.multiple_of(j * tk, tk), tk)
                now = dot(kn_ref[0, part, :head], queries) * to_log2
                higher = jnp.maximum(top, jnp.max(now, 0, keepdims=True))
                expo = jnp.exp2(now - higher).astype(BF)
                summed = summed * jnp.exp2(top - higher) + dot(vta_ref[0, :, part], expo)
                return summed, higher

            start = (jnp.zeros((AUG, tq), F32), jnp.full((1, tq), -1e30, F32))
            summed, top = lax.fori_loop(0, count, absorb, start)
            finish(where, summed, summed[head : head + 1, :], top)


def attend(qt, kn, kta, vta):
    _, head, own = qt.shape
    total = kn.shape[1]
    per_head = lambda *shape: pl.BlockSpec((1, *shape), lambda h: (h, 0, 0))
    return pl.pallas_call(
        attend_kernel,
        grid=(HEADS,),
        in_specs=[per_head(head, own), per_head(total, 128), per_head(AUG, total), per_head(AUG, total)],
        out_specs=[per_head(head, own), per_head(8, own)],
        out_shape=[
            jax.ShapeDtypeStruct((HEADS, head, own), F32),
            jax.ShapeDtypeStruct((HEADS, 8, own), F32),
        ],
        compiler_params=params(),
        name="attend",
    )(qt, kn, kta, vta)


def gelu_both(value):
    below = 0.5 + 0.5 * lax.erf(value * math.sqrt(0.5))
    density = jnp.exp2(value * value * (-0.5 * LOG2E) - math.log2(math.sqrt(2.0 * math.pi)))
    return value * below, below + value * density


def split_rows(level, count):
    high = level.astype(BF).astype(F32)
    middle = (level - high).astype(BF).astype(F32)
    low = level - high - middle
    place = lax.broadcasted_iota(jnp.int32, (count, level.shape[1]), 0)
    rows = jnp.where(place == 0, high, jnp.where(place == 1, middle, jnp.where(place == 2, low, 0.0)))
    return rows


def into_slots(slots_ref, grads, per):
    blk_size, owners, padded, width = slots_ref.shape
    filler = jnp.zeros((padded - per, width), F32)
    for slot in range(blk_size * owners):
        piece = grads[slot * per : (slot + 1) * per, :]
        if padded > per:
            piece = jnp.concatenate([piece, filler], 0)
        slots_ref[slot % blk_size, slot // blk_size] = piece.astype(BF)


def back_kernel(
    ctx_size, blk_size, per, entries,
    att_hbm, lse_hbm, qt_hbm, kta_hbm, vta_hbm, ln_hbm, x_hbm, near_hbm, far_hbm, w_hbm,
    vec_ref,
    grad_ref, out_ref, gw_ref, gvec_ref,
    w_ref, att, lse, cotangent, gwo, gup, gdown, late,
    qa_near, doa_near, dot_near, qa_far, doa_far, dot_far, qt, kta, vta, ln, x, gmid, made, turned,
    dq_sum, dk_sum, dv_sum, gq, gk, gv, part, part_out, part_in,
    late_one, late_pass, late_two, late_sum, late_three,
    early, early_one, early_pass, early_two, early_sum, early_three,
    vec_own, vec_one, vec_pair, vec_two, vec_sum, vec_three,
    head_sem, load_sem, out_sent, out_got, keep_sem, grad_sent, grad_got, part_sent, part_got,
    l1_sent, l1_got, l2_sent, l2_got, l3_sent, l3_got,
    e1_sent, e1_got, e2_sent, e2_got, e3_sent, e3_got,
    v1_sent, v1_got, v2_sent, v2_got, v3_sent, v3_got,
):
    ctx, blk, near, far, mine = partners(blk_size)
    core = lax.rem(blk, 2)
    own, width = x.shape
    length = own // 2
    head = width // HEADS
    owners = early.shape[1]
    groups = ctx_size // owners
    group, place = lax.div(ctx, owners), lax.rem(ctx, owners)
    others = [lax.rem(ctx + step, ctx_size) for step in range(1, ctx_size)]
    peers = [lax.rem(place + step, owners) for step in range(1, owners)]

    def remote(source, target, sent, got, device):
        return pltpu.make_async_remote_copy(
            src_ref=source, dst_ref=target, send_sem=sent, recv_sem=got, device_id=device, device_id_type=MESH
        )

    to_near, to_far = (ctx, near), (ctx, far)
    local = pltpu.make_async_copy

    def head_loads(h):
        pairs = ((kta_hbm, kta), (vta_hbm, vta))
        return [local(a.at[h], b.at[h], head_sem.at[i, h]) for i, (a, b) in enumerate(pairs)]

    def middle_loads(half):
        rows = pl.ds(half * length, length)
        given = far_hbm if half else near_hbm
        return [
            local(att_hbm.at[:, :, rows], att.at[:, :, rows], load_sem.at[half, 0]),
            local(x_hbm.at[rows], x.at[rows], load_sem.at[half, 1]),
            local(given.at[mine], cotangent.at[rows], load_sem.at[half, 2]),
            local(lse_hbm.at[:, :, rows], lse.at[:, :, rows], load_sem.at[half, 3]),
            local(qt_hbm.at[:, :, rows], qt.at[:, :, rows], load_sem.at[half, 4]),
        ]

    w_load = local(w_hbm, w_ref, load_sem.at[0, 5])
    ln_load = local(ln_hbm, ln, load_sem.at[1, 5])
    out_keep = local(made.at[pl.ds(0, length)], out_ref.at[mine], keep_sem.at[0])
    out_send = remote(made.at[pl.ds(length, length)], out_ref.at[mine], out_sent, out_got, to_far)

    late_first = [
        remote(late.at[2 * y + 1 - core], late_one.at[y], l1_sent.at[y], l1_got.at[y], to_near) for y in range(2)
    ]
    late_second = remote(late_pass.at[1 - mine], late_two, l2_sent, l2_got, to_far)

    def late_third(step):
        other = others[step]
        return remote(
            late_sum.at[jnp.maximum(other - owners, 0)], late_three.at[ctx], l3_sent.at[step], l3_got.at[ctx], (other, blk)
        )

    def late_third_from(other):
        return remote(late_sum.at[0], late_three.at[other], l3_sent.at[0], l3_got.at[other], to_near)

    def grad_send(half, c, size):
        return remote(
            made.at[pl.ds(half * length + c * size, size)], grad_ref.at[mine, pl.ds(c * size, size)],
            grad_sent.at[c], grad_got.at[c], to_far,
        )

    def grad_keep(c, size):
        return local(made.at[pl.ds(c * size, size)], grad_ref.at[mine, pl.ds(c * size, size)], keep_sem.at[1 + c])

    def part_send(half):
        return remote(part_out.at[half], part_in.at[half], part_sent.at[half], part_got.at[half], to_near)

    early_first = [
        remote(early.at[2 * y + 1 - core], early_one.at[y], e1_sent.at[y], e1_got.at[y], to_near) for y in range(2)
    ]
    vec_first = remote(vec_own, vec_one, v1_sent, v1_got, to_near)
    here = mine * owners + place
    plane = [(1 - mine, place, to_far)]
    for peer in peers:
        plane.append((mine, peer, (group * owners + peer, blk)))
        plane.append((1 - mine, peer, (group * owners + peer, far)))
    early_second = [
        remote(early_pass.at[y, r], early_two.at[here], e2_sent.at[i], e2_got.at[here], device)
        for i, (y, r, device) in enumerate(plane)
    ]
    vec_second = [
        remote(vec_pair, vec_two.at[here], v2_sent.at[i], v2_got.at[here], device) for i, (y, r, device) in enumerate(plane)
    ]
    plane_slots = [y * owners + r for y, r, _ in plane]
    early_third = remote(early_sum, early_three.at[jnp.maximum(group - 1, 0)], e3_sent, e3_got.at[jnp.maximum(group - 1, 0)], (place, blk))
    other_groups = [lax.rem(group + step, groups) for step in range(1, groups)]
    vec_third = [
        remote(vec_sum, vec_three.at[group], v3_sent.at[i], v3_got.at[group], (other * owners + place, blk))
        for i, other in enumerate(other_groups)
    ]

    for load in [w_load] + middle_loads(0) + middle_loads(1) + head_loads(0):
        load.start()
    greet([to_near, to_far] + [(other, blk) for other in others] + [(group * owners + peer, far) for peer in peers])
    for ref in (gwo, gup, gdown, vec_own, gq, gk, gv, dq_sum, dk_sum, dv_sum):
        ref[...] = jnp.zeros_like(ref)
    for load in [w_load] + middle_loads(0):
        load.wait()
    ln_load.start()

    gain_mid, bias_mid = vec_ref[2:3, :], vec_ref[3:4, :]
    wo = w_ref[3 * width : 4 * width, :]
    pieces = (w_ref.shape[0] - 4 * width) // (2 * width)
    down_bias = vec_ref[4 + pieces : 5 + pieces, :]
    from_log2 = math.sqrt(head) * LN2

    def middle_rows(base, low, count, qa, doa, dot_t):
        rows, local_rows = pl.ds(pl.multiple_of(base + low, count), count), pl.ds(pl.multiple_of(low, count), count)
        attended = att[:, :, rows].reshape(width, count)
        att_low = attended.astype(BF)
        grad = cotangent[rows, :]
        gradf = grad.astype(F32)
        grad_t = gradf.T.astype(BF)
        middle = x[rows, :].astype(F32) + dot_tn(att_low, wo)
        normed, inverse = normalize(middle)
        ln_mid = (normed * gain_mid + bias_mid).astype(BF)
        ln_mid_t = ln_mid.astype(F32).T.astype(BF)
        yield
        result = middle + down_bias
        grad_ln = jnp.zeros((count, width), F32)
        for p in range(pieces):
            columns = slice(p * width, (p + 1) * width)
            up = w_ref[(4 + p) * width : (5 + p) * width, :]
            down = w_ref[(4 + pieces + p) * width : (5 + pieces + p) * width, :]
            upper = dot_nt(ln_mid, up) + vec_ref[4 + p : 5 + p, :]
            activated, slope = gelu_both(upper)
            hidden = activated.astype(BF)
            grad_low = (dot_nt(grad, down) * slope).astype(BF)
            result = result + dot(hidden, down)
            grad_ln = grad_ln + dot(grad_low, up)
            gdown[:, columns] += dot(grad_t, hidden)
            gup[:, columns] += dot(ln_mid_t, grad_low)
            vec_own[4 + p : 5 + p, :] += jnp.sum(grad_low.astype(F32), 0, keepdims=True)
            yield
        made[rows, :] = result.astype(BF)
        vec_own[2:3, :] += jnp.sum(grad_ln * normed, 0, keepdims=True)
        vec_own[3:4, :] += jnp.sum(grad_ln, 0, keepdims=True)
        vec_own[4 + pieces : 5 + pieces, :] += jnp.sum(gradf, 0, keepdims=True)
        grad_mid = gradf + normalize_back(grad_ln * gain_mid, normed, inverse)
        gmid[rows, :] = grad_mid
        branch = grad_mid.astype(BF)
        gwo[...] += dot(att_low, branch)
        grad_att = dot_nt(wo, branch).astype(BF)
        spare = jnp.zeros((128 - AUG, count), F32)
        yield
        for h in range(HEADS):
            part_of = slice(h * head, (h + 1) * head)
            grad_head = grad_att[part_of, :]
            dot_t[h, :, local_rows] = grad_head
            grad_head = grad_head.astype(F32)
            delta = jnp.sum(grad_head * attended[part_of, :], 0, keepdims=True)
            wide = jnp.concatenate([grad_head, split_rows(-delta, AUG - head), spare], 0)
            doa[h, local_rows, :] = wide.T.astype(BF)
            level = lse[h, 0:1, rows] * from_log2
            wide = jnp.concatenate([qt[h, :, rows].astype(F32), split_rows(-level, AUG - head), spare], 0)
            qa[h, local_rows, :] = wide.T.astype(BF)
            if h == 1:
                yield

    step_rows = min(512, length)

    @pl.loop(0, length // step_rows)
    def _(index):
        for _ in middle_rows(0, index * step_rows, step_rows, qa_near, doa_near, dot_near):
            pass

    out_keep.start()
    for load in middle_loads(1):
        load.wait()
    tk = min(256, length)
    inverse_root = 1.0 / math.sqrt(head)
    wq, wk, wv = (w_ref[index * width : (index + 1) * width, :] for index in range(3))
    gain = vec_ref[0:1, :]
    size = min(512, length)
    chunks = length // size

    def terms(half):
        def grads_of(core_rows):
            low = core_rows * own + half * length
            rows = slice(low, low + length)
            dk = (dk_sum[:, :, rows] * inverse_root).astype(BF).reshape(width, length)
            dv = dv_sum[:, :, rows].astype(BF).reshape(width, length)
            return rows, dk, dv

        rows, dk, dv = grads_of(1)
        part_out[half] = (dot(wk, dk) + dot(wv, dv)).astype(BF)
        part_send(half).start()
        yield
        gk[...] += dot(dk, ln[rows, :])
        gv[...] += dot(dv, ln[rows, :])
        yield
        rows, dk, dv = grads_of(0)
        dq = (dq_sum[:, :, rows] * inverse_root).astype(BF).reshape(width, length)
        gq[...] += dot(dq, ln[rows, :])
        gk[...] += dot(dk, ln[rows, :])
        gv[...] += dot(dv, ln[rows, :])
        yield
        if half == 0:
            into_slots(early, jnp.concatenate([gq[...].T, gk[...].T, gv[...].T], 0), per)
            for copy in early_first:
                copy.start()
        part[half] = dot(wq, dq) + dot(wk, dk) + dot(wv, dv)

    def rows_back(half):
        for c in range(chunks):
            rows = slice(half * length + c * size, half * length + (c + 1) * size)
            lanes = slice(c * size, (c + 1) * size)
            grad_ln = (part[half, :, lanes] + part_in[half, :, lanes].astype(F32)).T
            yield
            normed, inverse = normalize(x[rows, :].astype(F32))
            vec_own[0:1, :] += jnp.sum(grad_ln * normed, 0, keepdims=True)
            vec_own[1:2, :] += jnp.sum(grad_ln, 0, keepdims=True)
            made[rows, :] = (gmid[rows, :] + normalize_back(grad_ln * gain, normed, inverse)).astype(BF)
            (grad_send(half, c, size) if half else grad_keep(c, size)).start()
            yield

    def attention(h, half, base, qa, doa, dot_t, beside=None):
        beside = beside or iter(())
        queries, grads = qa[h, :, :AUG], doa[h, :, :AUG]
        where = slice(half * length, (half + 1) * length)
        queries_t, grads_t = qt[h, :, where], dot_t[h]
        parts = []
        for offset in (0, own):
            for low in range(0, length, tk):
                parts.append(pl.ds(pl.multiple_of(base + (offset + low), tk), tk))

        some = min(256, length)
        blocks = [slice(low, low + some) for low in range(0, length, some)]
        grad_query = [jnp.zeros((head, some), F32) for _ in blocks]
        probs_low, grad_scores, now = None, None, None
        for j in range(len(parts) + 1):
            part = parts[j] if j < len(parts) else None
            grad_value, grad_key = jnp.zeros((head, tk), F32), jnp.zeros((head, tk), F32)
            next_low, next_scores = [], []
            for c, rows in enumerate(blocks):
                if j < len(parts):
                    level = dot(queries[rows, :], kta[h, :, part])
                if now is not None:
                    grad_value = grad_value + dot(grads_t[:, rows], probs_low[c])
                    grad_key = grad_key + dot(queries_t[:, rows], grad_scores[c])
                if j < len(parts):
                    change = dot(grads[rows, :], vta[h, :, part])
                if now is not None:
                    grad_query[c] = grad_query[c] + dot(kta[h, :head, now], turned[1 - j % 2, :, rows])
                if j < len(parts):
                    probs = jnp.exp2(level * (LOG2E * inverse_root))
                    next_low.append(probs.astype(BF))
                    next_scores.append((probs * change).astype(BF))
                    turned[j % 2, :, rows] = next_scores[-1].T
            next(beside, None)
            if now is not None:
                dv_sum[h, :, now] += grad_value
                dk_sum[h, :, now] += grad_key
            probs_low, grad_scores, now = next_low, next_scores, part
        grad_query = jnp.concatenate(grad_query, 1)
        for _ in beside:
            pass
        dq_sum[h, :, where] += grad_query

    piece_rows = length // HEADS

    @pl.loop(0, HEADS)
    def _(h):
        for load in head_loads(h):
            load.wait()

        @pl.when(h < HEADS - 1)
        def _():
            for load in head_loads(h + 1):
                load.start()

        beside = middle_rows(length, h * piece_rows, piece_rows, qa_far, doa_far, dot_far)
        attention(h, 0, length, qa_near, doa_near, dot_near, beside)

    out_send.start()
    into_slots(late, jnp.concatenate([gwo[...], gup[...].T, gdown[...].T], 0), per)
    for copy in late_first:
        copy.start()

    @pl.loop(0, 2 * HEADS)
    def _(t):
        @pl.when(t == 1)
        def _():
            for y in range(2):
                late_first[y].wait_recv()
                late_pass[y] = (late[2 * y + core].astype(F32) + late_one[y].astype(F32)).astype(BF)
            late_second.start()

        @pl.when(t == 4)
        def _():
            late_second.wait_recv()
            late_sum[...] = (late_pass[mine].astype(F32) + late_two[...].astype(F32)).astype(BF)
            for step, other in enumerate(others):
                @pl.when(other >= owners)
                def _():
                    late_third(step).start()

        attention(lax.rem(t, HEADS), 1, jnp.where(t < HEADS, length, 0), qa_far, doa_far, dot_far)

    ln_load.wait()
    out_keep.wait()
    out_send.wait()

    attention(0, 0, 0, qa_near, doa_near, dot_near, terms(1))
    part_send(1).wait_recv()
    attention(1, 0, 0, qa_near, doa_near, dot_near, rows_back(1))

    @pl.loop(2, HEADS)
    def _(h):
        attention(h, 0, 0, qa_near, doa_near, dot_near)

    for _ in terms(0):
        pass
    part_send(0).wait_recv()
    for _ in rows_back(0):
        pass
    vec_first.start()
    for y in range(2):
        early_first[y].wait_recv()
        early_pass[y] = (early[2 * y + core].astype(F32) + early_one[y].astype(F32)).astype(BF)
    for copy in early_second:
        copy.start()
    vec_first.wait_recv()
    vec_pair[...] = vec_own[...] + vec_one[...]
    for copy in vec_second:
        copy.start()

    @pl.when(ctx >= owners)
    def _():
        total = late_sum[jnp.maximum(ctx - owners, 0)].astype(F32)
        for other in others:
            late_third_from(other).wait_recv()
            total = total + late_three[other].astype(F32)
        gw_ref[...] = total

    def from_plane(slot, holder, got):
        return remote(holder.at[slot], holder.at[slot], got.at[slot], got.at[slot], to_near)

    total = early_pass[mine, place].astype(F32)
    for slot in plane_slots:
        from_plane(slot, early_two, e2_got).wait_recv()
        total = total + early_two[slot].astype(F32)
    early_sum[...] = total.astype(BF)
    if groups > 1:
        @pl.when(group > 0)
        def _():
            early_third.start()

    vec_total = vec_pair[...]
    for slot in plane_slots:
        from_plane(slot, vec_two, v2_got).wait_recv()
        vec_total = vec_total + vec_two[slot]
    vec_sum[...] = vec_total
    for copy in vec_third:
        copy.start()

    @pl.when(group == 0)
    def _():
        whole_sum = total
        for slot in range(groups - 1):
            from_plane(slot, early_three, e3_got).wait_recv()
            whole_sum = whole_sum + early_three[slot].astype(F32)
        gw_ref[...] = whole_sum

    for copy in vec_third:
        copy.wait_send()
    for other in other_groups:
        from_plane(other, vec_three, v3_got).wait_recv()
        vec_total = vec_total + vec_three[other]
    vec_sum[...] = vec_total
    begin = (ctx * blk_size + blk) * entries
    row, shift = lax.div(begin, width), lax.rem(begin, width)
    after = jnp.minimum(row + 1, vec_sum.shape[0] - 1)
    pair_rows = jnp.concatenate([vec_sum[pl.ds(row, 1), :], vec_sum[pl.ds(after, 1), :]], 1)
    pair_rows = jnp.broadcast_to(pair_rows, (8, 2 * width))
    gvec_ref[...] = pltpu.roll(pair_rows, lax.rem(2 * width - shift, 2 * width), 1)[:, :128]

    for copy in late_first + [late_second, part_send(0), part_send(1), vec_first] + early_first + early_second + vec_second:
        copy.wait_send()
    for step, other in enumerate(others):
        @pl.when(other >= owners)
        def _():
            late_third(step).wait_send()

    if groups > 1:
        @pl.when(group > 0)
        def _():
            early_third.wait_send()

    for c in range(chunks):
        grad_keep(c, size).wait()
        grad_send(1, c, size).wait()


def back(ctx_size, blk_size, per, entries, owners, att, lse, qt, kta, vta, ln, rows, grad_near, grad_far, weights, vec):
    own, width = rows.shape
    head = width // HEADS
    total = 2 * own
    length = own // 2
    groups = ctx_size // owners
    hidden_width = (weights.shape[0] - 4 * width) // 2
    late_count = (weights.shape[0] - 3 * width) // (blk_size * per)
    padded = -(-per // 16) * 16
    dma = pltpu.SemaphoreType.DMA
    place = pl.BlockSpec(memory_space=pl.ANY)
    vmem = pl.BlockSpec(memory_space=pltpu.VMEM)
    chunks = length // min(512, length)
    low = lambda *shape: pltpu.VMEM(shape, BF)
    single = lambda *shape: pltpu.VMEM(shape, F32)
    plane = 2 * owners
    some = lambda count: dma((max(count, 1),))
    return pl.pallas_call(
        functools.partial(back_kernel, ctx_size, blk_size, per, entries),
        in_specs=[place] * 10 + [vmem],
        out_specs=[place, place, vmem, vmem],
        out_shape=[
            jax.ShapeDtypeStruct((2, length, width), BF),
            jax.ShapeDtypeStruct((2, length, width), BF),
            jax.ShapeDtypeStruct((padded, width), F32),
            jax.ShapeDtypeStruct((8, 128), F32),
        ],
        scratch_shapes=[
            low(*weights.shape), single(HEADS, head, own), single(HEADS, 8, own), low(own, width), single(width, width), single(width, hidden_width),
            single(width, hidden_width), low(blk_size, late_count, padded, width),
            low(HEADS, length, 128), low(HEADS, length, 128), low(HEADS, head, length),
            low(HEADS, length, 128), low(HEADS, length, 128), low(HEADS, head, length), low(HEADS, head, own),
            low(HEADS, AUG, total), low(HEADS, AUG, total), low(total, width),
            low(own, width), single(own, width), low(own, width), low(2, min(256, length), length),
            single(HEADS, head, own), single(HEADS, head, total), single(HEADS, head, total),
            single(width, width), single(width, width), single(width, width),
            single(2, width, length), low(2, width, length), low(2, width, length),
            low(2, late_count, padded, width), low(2, late_count, padded, width),
            low(late_count, padded, width), low(late_count, padded, width), low(ctx_size, padded, width),
            low(blk_size, owners, padded, width), low(2, owners, padded, width), low(2, owners, padded, width),
            low(plane, padded, width), low(padded, width), low(max(groups - 1, 1), padded, width),
            single(16, width), single(16, width), single(16, width), single(plane, 16, width), single(16, width),
            single(groups, 16, width),
            dma((2, HEADS)), dma((2, 6)), dma, dma, dma((1 + chunks,)), dma((chunks,)), dma((chunks,)), dma((2,)), dma((2,)),
            dma((2,)), dma((2,)), dma, dma, some(ctx_size - 1), dma((ctx_size,)),
            dma((2,)), dma((2,)), some(plane - 1), dma((plane,)), dma, some(groups - 1),
            dma, dma, some(plane - 1), dma((plane,)), some(groups - 1), dma((groups,)),
        ],
        compiler_params=params(collective_id=2, has_side_effects=True),
        name="back",
    )(att, lse, qt, kta, vta, ln, rows, grad_near, grad_far, weights, vec)


def publish_kernel(grad_ref, out_ref, mats_ref, vec_ref, grad_to, out_to, mats_to, vec_to, grad, out, mats, sems):
    ways = []
    for a, b, c in ((grad_ref, grad, grad_to), (out_ref, out, out_to)):
        pieces = 2
        size = a.shape[1] // pieces
        for half in range(2):
            for piece in range(pieces):
                part = pl.ds(piece * size, size)
                ways.append((a.at[half, part], b.at[half, part], c.at[half, part]))
    kept = pl.ds(0, mats_to.shape[0])
    ways.append((mats_ref.at[kept], mats.at[kept], mats_to))
    come = [pltpu.make_async_copy(a, b, sems.at[0, i]) for i, (a, b, _) in enumerate(ways)]
    go = [pltpu.make_async_copy(b, c, sems.at[1, i]) for i, (_, b, c) in enumerate(ways)]
    for copy in come:
        copy.start()
    vec_to[...] = vec_ref[0, : vec_to.shape[0]]
    for first, second in zip(come, go):
        first.wait()
        second.start()
    for copy in go:
        copy.wait()


def publish(grad, out, mats, vecs, per, entries):
    place = pl.BlockSpec(memory_space=pl.ANY)
    vmem = pl.BlockSpec(memory_space=pltpu.VMEM)
    shapes = [grad.shape, out.shape, (per, mats.shape[1]) if per % 8 == 0 else mats.shape, (entries,)]
    types = [BF, BF, F32, F32]
    return pl.pallas_call(
        publish_kernel,
        in_specs=[place] * 3 + [vmem],
        out_specs=[place] * 3 + [vmem],
        out_shape=[jax.ShapeDtypeStruct(shape, kind) for shape, kind in zip(shapes, types)],
        scratch_shapes=[
            pltpu.VMEM(grad.shape, BF), pltpu.VMEM(out.shape, BF), pltpu.VMEM(mats.shape, F32),
            pltpu.SemaphoreType.DMA((2, 10)),
        ],
        compiler_params=params(),
        name="publish",
    )(grad, out, mats, vecs)


def per_device(ctx_size, blk_size, layer_in, matrices, vectors, out_grad):
    seq_count, local_rows, width = layer_in.shape
    per, entries = matrices.shape[0], vectors.shape[0]
    far = [(b, (b + blk_size // 2) % blk_size) for b in range(blk_size)]
    owners = 3 * width // (per * blk_size)
    weights = lax.all_gather(matrices, ("ctx", "blk"), axis=0, tiled=True)
    rows, ln, qt, kn, kta, vta, vec = start(ctx_size, blk_size, layer_in, matrices, vectors, owners)

    out_grad, qt = lax.optimization_barrier((out_grad, qt))
    grad_far = lax.ppermute(out_grad, "blk", far)
    att, lse = attend(qt, kn, kta, vta)
    layer_grad, layer_out, matrices_grad, vecs = back(
        ctx_size, blk_size, per, entries, owners, att, lse, qt, kta, vta, ln, rows, out_grad, grad_far, weights, vec
    )
    layer_grad, layer_out, matrices_grad, vecs = publish(layer_grad, layer_out, matrices_grad, vecs, per, entries)
    return layer_out, layer_grad, matrices_grad[:per], vecs


def solution(mesh):
    rows = P("ctx", "blk", None)
    flat = P(("ctx", "blk"))
    return jax.shard_map(
        functools.partial(per_device, mesh.shape["ctx"], mesh.shape["blk"]),
        mesh=mesh,
        in_specs=(rows, flat, flat, rows),
        out_specs=(rows, rows, flat, flat),
        check_vma=False,
    )
```
